32 devices in a mesh: dom: 32 (over z, y, x, core).
Axes of the slice: x: 2, y: 2, z: 4, core: 2. Of those that a mesh axis runs over, the one named last changes fastest.
Arguments:
- velocity: float32 [3, 3, 512, 512], P(None, None, 'dom'), may hold values from -6 to 6
- conv_past: float32 [2, 3, 512, 512], P(None, None, 'dom'), may hold values from -0.6 to 0.6
- metric: float32 [3, 512, 512], P(None, 'dom'), may hold values from 0.5 to 2
- jacobian: float32 [512, 512], P('dom'), may hold values from 0.5 to 2
- element_slot: int32 [512], P('dom'), may hold values from 0 to 15, as said below
Outputs:
- pressure: float32 [256, 896], P('dom')
- residual: float32 [256, 896], P('dom')
The draws below stay inside these ranges and needn't reach their ends.
Inputs may be any that keep to these rules, and one draw needn't show every extreme that they name: `element_slot`: within each aligned block of 16 entries (one slab's elements) the entries are a permutation of 0 to 15.
All inputs are finite; a program needn't handle non-finite values.
Results may differ from the reference program's by a relative error of at most 0.0003.
Values sent between devices are 32-bit elements; how exact they have to be, the bound alone decides.
A program may use at most 64 MiB of HBM per device.

```python
import math
import jax
import jax.numpy as jnp
import numpy as np
from jax import lax

NP = 8
NF = 12
EA = 1
ES = 16
ER = 1
ITERS = 3
E_DEV = 16
ELEMS = 512
A0 = 8
A1 = 112
A2 = 8


def draw_element_slot(key, part):
    key = jax.random.fold_in(key, 11)
    keys = jax.random.split(key, ELEMS // E_DEV)
    orders = jax.vmap(lambda single: jax.random.permutation(single, E_DEV))(keys)
    return orders.reshape(-1).astype(jnp.int32)


def level_of(own_key, dims, shards, least, top_value):
    def one(dim, shards_of):
        steps = jax.random.uniform(jax.random.fold_in(jax.random.fold_in(own_key, 6), dim), (shards_of,), jnp.float32, least / len(shards), top_value / len(shards))
        return jnp.repeat(jnp.exp(steps), dims[dim] // shards_of).reshape((-1,) + (1,) * (len(dims) - dim - 1))

    factor_of = one(*shards[0])
    for cut in shards[1:]:
        factor_of = factor_of * one(*cut)
    return factor_of


def scatter_about(stream_key, shape, deviation, reach, shards=(), held_as=jnp.bfloat16):
    values = deviation * jax.random.normal(stream_key, shape, jnp.float32)
    if shards:
        values = values * level_of(stream_key, shape, shards, -0.22, 0.18)
    return jnp.clip(values, -reach, reach).astype(held_as)


def setup_inputs(seed: int = 0) -> dict:
    arg_keys = jax.random.split(jax.random.key(seed), 6)
    velocity = scatter_about(arg_keys[0], (3, 3, ELEMS, NP * NP * NP), 1.0, 6.0, ((2, 32),), jnp.float32)
    conv_past = scatter_about(arg_keys[1], (2, 3, ELEMS, NP * NP * NP), 0.1, 0.6, ((2, 32),), jnp.float32)
    metric = jnp.clip(jnp.exp(math.log(2.0) - 1.3862944 * jax.random.uniform(arg_keys[2], (3, ELEMS, NP * NP * NP), jnp.float32) ** level_of(arg_keys[2], (3, ELEMS, NP * NP * NP), ((1, 32),), -0.2, 0.2)), 0.5, 2.0)
    jacobian = jnp.clip(jnp.exp(math.log(2.0) - 1.3862944 * jax.random.uniform(arg_keys[3], (ELEMS, NP * NP * NP), jnp.float32) ** level_of(arg_keys[3], (ELEMS, NP * NP * NP), ((0, 32),), -0.2, 0.2)), 0.5, 2.0)
    element_slot = draw_element_slot(jax.random.fold_in(arg_keys[5], 71), 0)
    return dict(velocity=velocity, conv_past=conv_past, metric=metric, jacobian=jacobian, element_slot=element_slot)


HIGHEST = lax.Precision.HIGHEST
time_step = 0.25
viscosity = 0.05
mass_shift = 0.001

def legendre_pair(points, order):
    before = np.ones(points.shape)
    current = points * 1.0
    for level in range(2, order + 1):
        nextone = ((2 * level - 1) * points * current - (level - 1) * before) / level
        before = current
        current = nextone
    return (current, before)

def jacobi_eigen(matrix):
    size = matrix.shape[0]
    work = matrix * 1.0
    vectors = np.eye(size)
    for sweep in range(30):
        for first in range(size - 1):
            for second in range(first + 1, size):
                off = float(work[first, second])
                if abs(off) > 1e-300:
                    tau = (float(work[second, second]) - float(work[first, first])) / (2.0 * off)
                    if tau >= 0.0:
                        tangent = 1.0 / (tau + (1.0 + tau * tau) ** 0.5)
                    else:
                        tangent = -1.0 / (-tau + (1.0 + tau * tau) ** 0.5)
                    cosine = 1.0 / (1.0 + tangent * tangent) ** 0.5
                    sine = tangent * cosine
                    rotation = np.eye(size)
                    rotation[first, first] = cosine
                    rotation[second, second] = cosine
                    rotation[first, second] = sine
                    rotation[second, first] = -sine
                    work = rotation.T @ work @ rotation
                    vectors = vectors @ rotation
    diagonal_index = np.arange(size)
    return (work[diagonal_index, diagonal_index], vectors)

def build_tables(points_edge, points_fine):
    degree = points_edge - 1
    points = -np.cos(np.pi * np.arange(points_edge) / degree)
    for sweep in range(100):
        top, below = legendre_pair(points, degree)
        points = points - (points * top - below) / (points_edge * top)
    top, below = legendre_pair(points, degree)
    weight_gll = 2.0 / (degree * points_edge * top ** 2)
    spacing = points[:, None] - points[None, :] + np.eye(points_edge)
    barycentric = 1.0 / np.prod(spacing, axis=1)
    derivative = barycentric[None, :] / barycentric[:, None] / spacing
    derivative = derivative * (1.0 - np.eye(points_edge))
    derivative = derivative - np.eye(points_edge) * derivative.sum(axis=1)[:, None]
    fine_points = np.cos(np.pi * (np.arange(points_fine) + 0.75) / (points_fine + 0.5))
    for sweep in range(100):
        top, below = legendre_pair(fine_points, points_fine)
        slope = points_fine * (fine_points * top - below) / (fine_points * fine_points - 1.0)
        fine_points = fine_points - top / slope
    top, below = legendre_pair(fine_points, points_fine)
    slope = points_fine * (fine_points * top - below) / (fine_points * fine_points - 1.0)
    fine_weight = 2.0 / ((1.0 - fine_points * fine_points) * slope * slope)
    fine_points = fine_points[::-1]
    fine_weight = fine_weight[::-1]
    interpolate = np.ones((points_fine, points_edge))
    for column in range(points_edge):
        for other in range(points_edge):
            if other != column:
                interpolate[:, column] = interpolate[:, column] * (fine_points - points[other]) / (points[column] - points[other])
    stiffness = derivative.T @ (weight_gll[:, None] * derivative)
    extent = 3 * degree + 1
    joined_stiff = np.zeros((extent, extent))
    joined_mass = np.zeros(extent)
    for segment in range(3):
        offset = segment * degree
        joined_stiff[offset:offset + points_edge, offset:offset + points_edge] += stiffness
        joined_mass[offset:offset + points_edge] += weight_gll
    low = degree - 1
    high = 2 * degree + 2
    root_mass = np.sqrt(joined_mass[low:high])
    scaled = joined_stiff[low:high, low:high] / root_mass[:, None] / root_mass[None, :]
    scaled = 0.5 * (scaled + scaled.T)
    eigen_values, eigen_vectors = jacobi_eigen(scaled)
    solve_mat = eigen_vectors / root_mass[:, None]
    breadth = high - low
    identity = np.eye(points_edge)
    operator_tables = {'derivative': derivative, 'dpair': np.concatenate([np.kron(derivative, identity).T, np.kron(identity, derivative).T], axis=1), 'interpolate': interpolate, 'ipair': np.kron(interpolate, interpolate).T, 'mass_three': (weight_gll[:, None, None] * weight_gll[None, :, None] * weight_gll[None, None, :]).reshape(points_edge, points_edge * points_edge), 'fine_three': (fine_weight[:, None, None] * fine_weight[None, :, None] * fine_weight[None, None, :]).reshape(points_fine, points_fine * points_fine), 'solve_mat': solve_mat, 'solve_pair': np.kron(solve_mat, solve_mat), 'eigen_axial': eigen_values, 'eigen_around': np.repeat(eigen_values, breadth), 'eigen_radial': np.tile(eigen_values, breadth)}
    return {entry_name: jnp.asarray(entry_value, jnp.float32) for entry_name, entry_value in operator_tables.items()}

def matmul(left, right):
    return jnp.dot(left, right, precision=HIGHEST, preferred_element_type=jnp.float32)

def along_first(field, matrix, form):
    return jnp.einsum(form, field, matrix, precision=HIGHEST, preferred_element_type=jnp.float32)

def gradient(field, operator_tables):
    paired = matmul(field, operator_tables['dpair'])
    streamwise_piece = along_first(field, operator_tables['derivative'], 'ebx,ab->eax')
    return (streamwise_piece, paired[..., :NP * NP], paired[..., NP * NP:])

def gradient_t(streamwise_piece, azimuthal_piece, radial_piece, operator_tables):
    paired = matmul(jnp.concatenate([azimuthal_piece, radial_piece], axis=-1), operator_tables['dpair'].T)
    return paired + along_first(streamwise_piece, operator_tables['derivative'], 'eax,ab->ebx')

def coarse_to_dealiased(field, operator_tables):
    return along_first(matmul(field, operator_tables['ipair']), operator_tables['interpolate'], 'ebx,ab->eax')

def from_fine(field, operator_tables):
    return matmul(along_first(field, operator_tables['interpolate'], 'eax,ab->ebx'), operator_tables['ipair'].T)

def element_forcing(velocity, conv_past, metric, jacobian, operator_tables):
    mass_node = jacobian * operator_tables['mass_three']
    fine_jacobian = coarse_to_dealiased(jacobian, operator_tables) * operator_tables['fine_three']
    advecting_velocities = [coarse_to_dealiased(velocity[0, velocity_component] * metric[velocity_component], operator_tables) for velocity_component in range(3)]
    factors = [mass_node * metric[velocity_component] * metric[velocity_component] for velocity_component in range(3)]
    outputs = []
    for velocity_component in range(3):
        streamwise_piece, azimuthal_piece, radial_piece = gradient(velocity[0, velocity_component], operator_tables)
        pointwise_product = advecting_velocities[0] * coarse_to_dealiased(streamwise_piece, operator_tables) + advecting_velocities[1] * coarse_to_dealiased(azimuthal_piece, operator_tables) + advecting_velocities[2] * coarse_to_dealiased(radial_piece, operator_tables)
        convect = from_fine(fine_jacobian * pointwise_product, operator_tables)
        extrap_term = 3.0 * convect - 3.0 * conv_past[0, velocity_component] + conv_past[1, velocity_component]
        history = 3.0 * velocity[0, velocity_component] - 1.5 * velocity[1, velocity_component] + velocity[2, velocity_component] / 3.0
        guessed = 3.0 * velocity[0, velocity_component] - 3.0 * velocity[1, velocity_component] + velocity[2, velocity_component]
        streamwise_piece, azimuthal_piece, radial_piece = gradient(guessed, operator_tables)
        stiff_term = gradient_t(factors[0] * streamwise_piece, factors[1] * azimuthal_piece, factors[2] * radial_piece, operator_tables)
        helmholtz = viscosity * stiff_term + 11.0 / (6.0 * time_step) * mass_node * guessed
        outputs.append(mass_node * history / time_step - extrap_term - helmholtz)
    outputs.append(mass_node)
    return jnp.stack(outputs)

def element_divergence(accel, metric, jacobian, operator_tables):
    mass_node = jacobian * operator_tables['mass_three']
    return gradient_t(mass_node * metric[0] * accel[0], mass_node * metric[1] * accel[1], mass_node * metric[2] * accel[2], operator_tables)

def element_pressure(values, metric, jacobian, operator_tables):
    mass_node = jacobian * operator_tables['mass_three']
    streamwise_piece, azimuthal_piece, radial_piece = gradient(values, operator_tables)
    stiff_term = gradient_t(mass_node * metric[0] * metric[0] * streamwise_piece, mass_node * metric[1] * metric[1] * azimuthal_piece, mass_node * metric[2] * metric[2] * radial_piece, operator_tables)
    return stiff_term + mass_shift * mass_node * values

def local_solve(extended, metric, jacobian, operator_tables):
    mass_node = jacobian * operator_tables['mass_three']
    scales = [lax.optimization_barrier(jnp.sum(mass_node * metric[velocity_component] * metric[velocity_component], axis=(1, 2))) / 8.0 for velocity_component in range(3)]
    average = lax.optimization_barrier(jnp.sum(mass_node, axis=(1, 2))) / 8.0
    breadth = operator_tables['solve_mat'].shape[0]
    spectra = extended.reshape(-1, breadth, breadth * breadth)
    spectra = along_first(matmul(spectra, operator_tables['solve_pair']), operator_tables['solve_mat'], 'eax,ab->ebx')
    denom = scales[0][:, None, None] * operator_tables['eigen_axial'][None, :, None] + scales[1][:, None, None] * operator_tables['eigen_around'][None, None, :] + scales[2][:, None, None] * operator_tables['eigen_radial'][None, None, :] + mass_shift * average[:, None, None]
    spectra = spectra / denom
    restored = matmul(along_first(spectra, operator_tables['solve_mat'], 'ebx,ab->eax'), operator_tables['solve_pair'].T)
    return restored.reshape(extended.shape)

def element_index(slots, row_base, row_total, breadth, margin, radial_total):
    position = slots.astype(jnp.int32)
    along = (position // (ES * ER))[:, None, None, None]
    beside_all = (position // ER % ES)[:, None, None, None]
    radial = (position % ER)[:, None, None, None]
    offsets = jnp.arange(breadth, dtype=jnp.int32)
    row_index = (row_base + (NP - 1) * along + offsets[None, :, None, None] - margin) % row_total
    turn_index = ((NP - 1) * beside_all + offsets[None, None, :, None] - margin) % A1
    depth_index = (NP - 1) * radial + offsets[None, None, None, :] - margin + (radial_total - A2) // 2
    flat_index = (row_index * A1 + turn_index) * radial_total + depth_index
    return flat_index.reshape(position.shape[0], breadth, breadth * breadth).astype(jnp.int32)

def scatter_rows(values, index, grid_size):
    flat = values.reshape(values.shape[0], -1)
    return jnp.zeros((values.shape[0], grid_size), jnp.float32).at[:, index.reshape(-1)].add(flat)

def reference(velocity, conv_past, metric, jacobian, element_slot):
    operator_tables = build_tables(NP, NF)
    blocks_total = ELEMS // E_DEV
    grid_rows = (NP - 1) * EA * blocks_total
    grid_size = grid_rows * A1 * A2

    def by_block(array, lead):
        shaped = array.reshape(array.shape[:lead] + (blocks_total, E_DEV, NP, NP * NP))
        return jnp.moveaxis(shaped, lead, 0)
    velocity_blocks = by_block(velocity, 2)
    past_blocks = by_block(conv_past, 2)
    metric_blocks = by_block(metric, 1)
    jacobian_blocks = by_block(jacobian, 0)
    slot_blocks = element_slot.reshape(blocks_total, E_DEV)
    row_starts = jnp.arange(blocks_total, dtype=jnp.int32) * ((NP - 1) * EA)
    node_blocks = jax.vmap(lambda slots, row_start: element_index(slots, row_start, grid_rows, NP, 0, A2))(slot_blocks, row_starts)
    ext_blocks = jax.vmap(lambda slots, row_start: element_index(slots, row_start, grid_rows, NP + 2, 1, A2 + 2))(slot_blocks, row_starts)
    forcing = lax.map(lambda group: element_forcing(group[0], group[1], group[2], group[3], operator_tables), (velocity_blocks, past_blocks, metric_blocks, jacobian_blocks))
    summed = scatter_rows(jnp.moveaxis(forcing, 1, 0), node_blocks, grid_size)
    accel = summed[:3] / summed[3:]
    divergence = lax.map(lambda group: element_divergence(accel[:, group[2]], group[0], group[1], operator_tables), (metric_blocks, jacobian_blocks, node_blocks))
    source = scatter_rows(divergence[None], node_blocks, grid_size)[0]

    def operate(vector):
        values = lax.map(lambda group: element_pressure(vector[group[2]], group[0], group[1], operator_tables), (metric_blocks, jacobian_blocks, node_blocks))
        return scatter_rows(values[None], node_blocks, grid_size)[0]

    def schwarz(vector):
        padded = jnp.pad(vector.reshape(grid_rows, A1, A2), ((0, 0), (0, 0), (1, 1))).reshape(-1)
        solved = lax.map(lambda group: local_solve(padded[group[2]], group[0], group[1], operator_tables), (metric_blocks, jacobian_blocks, ext_blocks))
        spread = scatter_rows(solved[None], ext_blocks, grid_rows * A1 * (A2 + 2))[0]
        return spread.reshape(grid_rows, A1, A2 + 2)[:, :, 1:-1].reshape(-1)
    solution = jnp.zeros((grid_size,), jnp.float32)
    residual = source
    direction = source
    previous_sum = jnp.float32(1.0)
    for step in range(ITERS):
        smoothed = schwarz(residual)
        precond_sum = jnp.sum(residual * smoothed)
        direction = smoothed if step == 0 else smoothed + precond_sum / previous_sum * direction
        image = operate(direction)
        step_size = precond_sum / jnp.sum(direction * image)
        solution = solution + step_size * direction
        residual = residual - step_size * image
        previous_sum = precond_sum
    rows = (jnp.arange(blocks_total, dtype=jnp.int32)[:, None] * ((NP - 1) * EA) + jnp.arange(A0, dtype=jnp.int32)[None, :]) % grid_rows
    rows = rows.reshape(-1)
    pressure = solution.reshape(grid_rows, A1 * A2)[rows]
    residual_out = residual.reshape(grid_rows, A1 * A2)[rows]
    return (pressure, residual_out)
```

```python
import functools

import jax
import jax.numpy as jnp
import numpy as np
from jax import lax
from jax.experimental import pallas as pl
from jax.experimental.pallas import tpu as pltpu
from jax.sharding import PartitionSpec as P

NP = 8
NF = 12
ES = 16
ITERS = 3
A0 = 8
A1 = 112
A2 = 8
ROUNDS = 8
LANES = 128
MESH = pl.DeviceIdType.MESH

time_step = 0.25
viscosity = 0.05
mass_shift = 0.001


def legendre_pair(points, order):
    before = np.ones(points.shape)
    current = points * 1.0
    for level in range(2, order + 1):
        nextone = ((2 * level - 1) * points * current - (level - 1) * before) / level
        before = current
        current = nextone
    return (current, before)


def jacobi_eigen(matrix):
    size = matrix.shape[0]
    work = matrix * 1.0
    vectors = np.eye(size)
    for sweep in range(30):
        for first in range(size - 1):
            for second in range(first + 1, size):
                off = float(work[first, second])
                if abs(off) > 1e-300:
                    tau = (float(work[second, second]) - float(work[first, first])) / (2.0 * off)
                    if tau >= 0.0:
                        tangent = 1.0 / (tau + (1.0 + tau * tau) ** 0.5)
                    else:
                        tangent = -1.0 / (-tau + (1.0 + tau * tau) ** 0.5)
                    cosine = 1.0 / (1.0 + tangent * tangent) ** 0.5
                    sine = tangent * cosine
                    rotation = np.eye(size)
                    rotation[first, first] = cosine
                    rotation[second, second] = cosine
                    rotation[first, second] = sine
                    rotation[second, first] = -sine
                    work = rotation.T @ work @ rotation
                    vectors = vectors @ rotation
    diagonal_index = np.arange(size)
    return (work[diagonal_index, diagonal_index], vectors)


def build_tables(points_edge, points_fine):
    degree = points_edge - 1
    points = -np.cos(np.pi * np.arange(points_edge) / degree)
    for sweep in range(100):
        top, below = legendre_pair(points, degree)
        points = points - (points * top - below) / (points_edge * top)
    top, below = legendre_pair(points, degree)
    weight_gll = 2.0 / (degree * points_edge * top**2)
    spacing = points[:, None] - points[None, :] + np.eye(points_edge)
    barycentric = 1.0 / np.prod(spacing, axis=1)
    derivative = barycentric[None, :] / barycentric[:, None] / spacing
    derivative = derivative * (1.0 - np.eye(points_edge))
    derivative = derivative - np.eye(points_edge) * derivative.sum(axis=1)[:, None]
    fine_points = np.cos(np.pi * (np.arange(points_fine) + 0.75) / (points_fine + 0.5))
    for sweep in range(100):
        top, below = legendre_pair(fine_points, points_fine)
        slope = points_fine * (fine_points * top - below) / (fine_points * fine_points - 1.0)
        fine_points = fine_points - top / slope
    top, below = legendre_pair(fine_points, points_fine)
    slope = points_fine * (fine_points * top - below) / (fine_points * fine_points - 1.0)
    fine_weight = 2.0 / ((1.0 - fine_points * fine_points) * slope * slope)
    fine_points = fine_points[::-1]
    fine_weight = fine_weight[::-1]
    interpolate = np.ones((points_fine, points_edge))
    for column in range(points_edge):
        for other in range(points_edge):
            if other != column:
                interpolate[:, column] = (
                    interpolate[:, column]
                    * (fine_points - points[other])
                    / (points[column] - points[other])
                )
    stiffness = derivative.T @ (weight_gll[:, None] * derivative)
    extent = 3 * degree + 1
    joined_stiff = np.zeros((extent, extent))
    joined_mass = np.zeros(extent)
    for segment in range(3):
        offset = segment * degree
        joined_stiff[offset : offset + points_edge, offset : offset + points_edge] += stiffness
        joined_mass[offset : offset + points_edge] += weight_gll
    low = degree - 1
    high = 2 * degree + 2
    root_mass = np.sqrt(joined_mass[low:high])
    scaled = joined_stiff[low:high, low:high] / root_mass[:, None] / root_mass[None, :]
    scaled = 0.5 * (scaled + scaled.T)
    eigen_values, eigen_vectors = jacobi_eigen(scaled)
    solve_mat = eigen_vectors / root_mass[:, None]
    breadth = high - low
    identity = np.eye(points_edge)
    operator_tables = {
        "derivative": derivative,
        "dpair": np.concatenate(
            [np.kron(derivative, identity).T, np.kron(identity, derivative).T], axis=1
        ),
        "interpolate": interpolate,
        "ipair": np.kron(interpolate, interpolate).T,
        "mass_three": (
            weight_gll[:, None, None] * weight_gll[None, :, None] * weight_gll[None, None, :]
        ).reshape(points_edge, points_edge * points_edge),
        "fine_three": (
            fine_weight[:, None, None] * fine_weight[None, :, None] * fine_weight[None, None, :]
        ).reshape(points_fine, points_fine * points_fine),
        "solve_mat": solve_mat,
        "solve_pair": np.kron(solve_mat, solve_mat),
        "eigen_axial": eigen_values,
        "eigen_around": np.repeat(eigen_values, breadth),
        "eigen_radial": np.tile(eigen_values, breadth),
    }
    operator_tables["weight"] = weight_gll
    operator_tables["fine_weight"] = fine_weight
    return operator_tables


def split_rows(matrix):
    exact = np.asarray(matrix, np.float32)
    high = exact.astype(jnp.bfloat16)
    low = (exact - high.astype(np.float32)).astype(jnp.bfloat16)
    return np.concatenate([high, high, low], axis=0)


def halves(matrix):
    rows, columns = matrix.shape
    table = np.zeros((rows // 2, columns // 2, 2, LANES))
    for out in range(rows // 2):
        for into in range(columns // 2):
            table[out, into, 0, :64] = matrix[2 * out, 2 * into]
            table[out, into, 0, 64:] = matrix[2 * out + 1, 2 * into + 1]
            table[out, into, 1, :64] = matrix[2 * out, 2 * into + 1]
            table[out, into, 1, 64:] = matrix[2 * out + 1, 2 * into]
    return np.asarray(table.reshape(-1, LANES), np.float32)


def twice(block, stride):
    rows, columns = block.shape
    result = np.zeros((2 * rows, 2 * stride))
    result[:rows, :columns] = block
    result[rows:, stride : stride + columns] = block
    return result


def pad_columns(matrix, total):
    return np.pad(matrix, ((0, 0), (0, total - matrix.shape[1])))


def by_tile(table):
    return np.asarray(np.repeat(table.reshape(-1, LANES), ES, axis=0), np.float32)


@functools.cache
def constants():
    t = build_tables(NP, NF)
    d, itp, s = t["derivative"], t["interpolate"], t["solve_mat"]
    eye = np.eye(NP)
    pair = np.concatenate(
        [twice(np.kron(d, eye).T, 64), twice(np.kron(eye, d).T, 64)], axis=1
    )
    fine = pad_columns(twice(np.kron(itp, itp).T, 144), 384)
    slope = itp @ d
    fine_slope = np.concatenate(
        [
            pad_columns(twice(np.kron(slope, itp).T, 144), 384),
            pad_columns(twice(np.kron(itp, slope).T, 144), 384),
        ],
        axis=1,
    )
    inner = s[1:9]
    ahead = np.zeros((2 * LANES, 2 * LANES))
    back = np.zeros((2 * LANES, 2 * LANES))
    for h in range(2):
        out = slice(h * LANES, h * LANES + 100)

        def lanes(row):
            return slice(h * 64 + row * 8, h * 64 + row * 8 + 8)

        def beside(row):
            return slice(LANES + h * 64 + row * 8, LANES + h * 64 + row * 8 + 8)

        for row in range(NP):
            ahead[lanes(row), out] = np.kron(s[row + 1 : row + 2], inner)
            back[lanes(row), out] = np.kron(s[row + 1 : row + 2], inner)
        ahead[beside(6), out] = np.kron(s[0:1], inner)
        ahead[beside(1), out] = np.kron(s[9:10], inner)
        back[beside(0), out] = np.kron(s[8:9], inner)
        back[beside(1), out] = np.kron(s[9:10], inner)
        back[beside(7), out] = np.kron(s[1:2], inner)
        back[beside(6), out] = np.kron(s[0:1], inner)
    wf = t["fine_weight"]
    wf2 = (wf[:, None] * wf[None, :]).reshape(-1)
    fine_mass = np.zeros((6, 384))
    for j in range(6):
        fine_mass[j, :144] = wf[2 * j] * wf2
        fine_mass[j, 144:288] = wf[2 * j + 1] * wf2
    eigen = np.zeros((2, LANES))
    eigen[0, :100] = t["eigen_around"]
    eigen[1, :100] = t["eigen_radial"]
    share = np.ones((NP, NP, NP))
    share[0] *= 0.5
    share[-1] *= 0.5
    share[:, 0] *= 0.5
    share[:, -1] *= 0.5
    nodes = np.stack([by_tile(t["mass_three"]), by_tile(share)])
    arrays = [
        split_rows(pair),
        split_rows(pair.T),
        split_rows(fine),
        split_rows(fine_slope),
        split_rows(fine.T),
        split_rows(ahead),
        split_rows(back.T),
        np.concatenate([halves(d), halves(d.T), halves(itp), halves(slope), halves(itp.T)]),
        nodes,
        np.asarray(np.repeat(fine_mass, ES, axis=0), np.float32),
        np.asarray(eigen, np.float32),
    ]
    return arrays, np.asarray(s, np.float32), np.asarray(t["eigen_axial"], np.float32)


COEF_D, COEF_DT, COEF_I, COEF_S, COEF_IT = 0, 32, 64, 112, 160


def stages_of(count):
    stages = []
    stride = 1
    while stride < count:
        size = min(8, count // stride)
        while (count // stride) % size:
            size -= 1
        stages.append((stride, size))
        stride *= size
    return stages


def kernel(
    count,
    velocity,
    past,
    metric,
    jacobian,
    slots,
    w_pair,
    w_pair_t,
    w_fine,
    w_slope,
    w_fine_t,
    w_ahead,
    w_back,
    coef,
    nodes,
    fine_mass,
    eigen,
    pressure_ref,
    residual_ref,
    send_left,
    send_right,
    from_left,
    from_right,
    gathered,
    turned,
    send_left_sem,
    send_right_sem,
    from_left_sem,
    from_right_sem,
    gather_send_sem,
    gather_recv_sem,
):
    _, solve, eigen_axial = constants()
    me = lax.axis_index("dom")
    left = lax.rem(me + count - 1, count)
    right = lax.rem(me + 1, count)
    stages = stages_of(count)

    def peer(stage, offset):
        stride, size = stages[stage]
        digit = lax.rem(me // stride, size)
        other = lax.rem(digit + offset, size)
        return me + (other - digit) * stride

    barrier = pltpu.get_barrier_semaphore()
    greeted = [left, right] + [
        peer(stage, offset)
        for stage in range(len(stages))
        for offset in range(1, stages[stage][1])
    ]
    for other in greeted:
        pl.semaphore_signal(barrier, inc=1, device_id=(other,), device_id_type=MESH)

    lane = lax.broadcasted_iota(jnp.int32, (ES, LANES), 1)
    low = lane < 64
    node_s = lax.rem(lane, 64) // 8

    def tiles(field):
        return [field[i * ES : (i + 1) * ES] for i in range(field.shape[0] // ES)]

    def stack(parts):
        return jnp.concatenate(parts, axis=0)

    def mm(x, w):
        high = x.astype(jnp.bfloat16)
        rest = (x - high.astype(jnp.float32)).astype(jnp.bfloat16)
        return jnp.dot(
            jnp.concatenate([high, rest, high], axis=1), w[...], preferred_element_type=jnp.float32
        )

    def swap(tile):
        return pltpu.roll(tile, 64, 1)

    def along(field, base, total):
        parts = tiles(field)
        swapped = [swap(part) for part in parts]
        results = []
        for out in range(total):
            acc = None
            for into in range(len(parts)):
                at = base + 2 * (out * len(parts) + into)
                term = coef[at : at + 1] * parts[into] + coef[at + 1 : at + 2] * swapped[into]
                acc = term if acc is None else acc + term
            results.append(acc)
        return stack(results)

    def gradient(field):
        paired = mm(field, w_pair)
        return along(field, COEF_D, 4), paired[:, :LANES], paired[:, LANES:]

    def gradient_t(axial, around, radial):
        paired = mm(jnp.concatenate([around, radial], axis=1), w_pair_t)
        return paired + along(axial, COEF_DT, 4)

    def before(tile):
        return pltpu.roll(tile, 1, 0)

    def after(tile):
        return pltpu.roll(tile, ES - 1, 0)

    def around_sum(field):
        results = []
        for tile in tiles(field):
            first = before(pltpu.roll(tile, 72, 1))
            last = after(pltpu.roll(tile, 56, 1))
            results.append(
                tile + jnp.where(node_s == 0, first, jnp.where(node_s == 7, last, 0.0))
            )
        return stack(results)

    def copies(step):
        at, size = (0, 4 * ES) if step == 0 else ((3 + step) * ES, ES)
        rows = pl.ds(at, size)
        to_left = pltpu.make_async_remote_copy(
            src_ref=send_left.at[rows],
            dst_ref=from_right.at[rows],
            send_sem=send_left_sem.at[step],
            recv_sem=from_right_sem.at[step],
            device_id=(left,),
            device_id_type=MESH,
        )
        to_right = pltpu.make_async_remote_copy(
            src_ref=send_right.at[rows],
            dst_ref=from_left.at[rows],
            send_sem=send_right_sem.at[step],
            recv_sem=from_left_sem.at[step],
            device_id=(right,),
            device_id_type=MESH,
        )
        return rows, to_left, to_right

    def exchange(step, for_left, for_right):
        rows, to_left, to_right = copies(step)
        send_left[rows] = for_left
        to_left.start()
        send_right[rows] = for_right
        to_right.start()
        to_right.wait_recv()
        to_left.wait_recv()
        return from_left[rows], from_right[rows]

    def axial_sum(step, fields):
        parts = [tiles(field) for field in fields]
        lefts, rights = exchange(
            step, stack([p[0] for p in parts]), stack([p[3] for p in parts])
        )
        lefts, rights = tiles(lefts), tiles(rights)
        results = []
        for p, far_left, far_right in zip(parts, lefts, rights):
            results.append(
                stack(
                    [
                        p[0] + jnp.where(low, swap(far_left), 0.0),
                        p[1],
                        p[2],
                        p[3] + jnp.where(low, 0.0, swap(far_right)),
                    ]
                )
            )
        return results, jnp.where(low, lefts[0], rights[0])

    def element_field(ref, *index):
        return stack([ref[index + (slice(None), pl.ds(j * LANES, LANES))] for j in range(4)])

    weight3, share = nodes[0], nodes[1]
    jac = element_field(jacobian)
    mass = jac * weight3
    metrics = [element_field(metric, d) for d in range(3)]
    squares = [mass * m * m for m in metrics]
    newest = [element_field(velocity, 0, i) for i in range(3)]
    coarse = [along(jac, COEF_I, 6)]
    coarse += [along(newest[d] * metrics[d], COEF_I, 6) for d in range(3)]
    coarse += [along(newest[i], COEF_S, 6) for i in range(3)]
    fine = mm(stack(coarse), w_fine)
    fine = [fine[i * 96 : (i + 1) * 96] for i in range(7)]
    crossed = mm(stack([along(newest[i], COEF_I, 6) for i in range(3)]), w_slope)
    fine_jac = fine[0] * fine_mass[...]
    products = []
    for i in range(3):
        rows = slice(i * 96, (i + 1) * 96)
        products.append(
            fine_jac
            * (
                fine[1] * fine[4 + i]
                + fine[2] * crossed[rows, :384]
                + fine[3] * crossed[rows, 384:]
            )
        )
    advected = mm(stack(products), w_fine_t)
    guessed = [
        3.0 * newest[i] - 3.0 * element_field(velocity, 1, i) + element_field(velocity, 2, i)
        for i in range(3)
    ]
    paired = mm(stack(guessed), w_pair)
    slopes = jnp.concatenate(
        [
            stack([squares[1] * paired[i * 64 : (i + 1) * 64, :LANES] for i in range(3)]),
            stack([squares[2] * paired[i * 64 : (i + 1) * 64, LANES:] for i in range(3)]),
        ],
        axis=1,
    )
    paired_t = mm(slopes, w_pair_t)
    forcing = []
    for i in range(3):
        convect = along(advected[i * 96 : (i + 1) * 96], COEF_IT, 4)
        stiff = paired_t[i * 64 : (i + 1) * 64] + along(
            squares[0] * along(guessed[i], COEF_D, 4), COEF_DT, 4
        )
        history = (
            3.0 * newest[i]
            - 1.5 * element_field(velocity, 1, i)
            + element_field(velocity, 2, i) / 3.0
        )
        extrap = (
            3.0 * convect - 3.0 * element_field(past, 0, i) + element_field(past, 1, i)
        )
        helmholtz = viscosity * stiff + 11.0 / (6.0 * time_step) * mass * guessed[i]
        forcing.append(mass * history / time_step - extrap - helmholtz)

    fields = forcing + [mass] + metrics
    wide = jnp.concatenate([tile for field in fields for tile in tiles(field)], axis=1)
    first = wide.astype(jnp.bfloat16)
    rest = wide - first.astype(jnp.float32)
    second = rest.astype(jnp.bfloat16)
    third = (rest - second.astype(jnp.float32)).astype(jnp.bfloat16)
    position = lax.broadcasted_iota(jnp.int32, (ES, 3 * ES), 0)
    chosen = jnp.where(slots[...] == position, 1.0, 0.0).astype(jnp.bfloat16)
    placed = jnp.dot(chosen, stack([first, second, third]), preferred_element_type=jnp.float32)
    fields = [
        stack([placed[:, (4 * f + j) * LANES : (4 * f + j + 1) * LANES] for j in range(4)])
        for f in range(7)
    ]
    forcing, mass, metrics = fields[:3], fields[3], fields[4:]
    lumps = [mass * m for m in metrics]
    squares = [lumps[d] * metrics[d] for d in range(3)]

    def total(field):
        parts = tiles(field)
        return jnp.sum(parts[0] + parts[1] + parts[2] + parts[3], axis=1, keepdims=True) / 8.0

    scales = [total(square) for square in squares]
    flat = (
        scales[1] * eigen[0:1] + scales[2] * eigen[1:2] + mass_shift * total(mass)
    )
    inverse = [1.0 / (scales[0] * float(eigen_axial[k]) + flat) for k in range(10)]

    pl.semaphore_wait(barrier, len(greeted))
    summed, _ = axial_sum(0, [around_sum(f) for f in forcing + [mass]])
    accel = [lumps[d] * (summed[d] / summed[3]) for d in range(3)]
    divergence = around_sum(gradient_t(accel[0], accel[1], accel[2]))
    (source,), source_halo = axial_sum(1, [divergence])

    def smooth(step, field, halo):
        parts = tiles(field) + [halo]
        sides = [
            jnp.where(node_s == 6, before(p), jnp.where(node_s == 1, after(p), 0.0))
            for p in parts
        ]
        modes = mm(jnp.concatenate([stack(parts), stack(sides)], axis=1), w_ahead)
        rows = tiles(modes)
        order = [rows[4][:, :LANES]]
        for j in range(4):
            order += [rows[j][:, :LANES], rows[j][:, LANES:]]
        order.append(rows[4][:, LANES:])
        spectra = []
        for k in range(10):
            acc = order[0] * float(solve[0, k])
            for a in range(1, 10):
                acc = acc + order[a] * float(solve[a, k])
            spectra.append(acc * inverse[k])
        restored = []
        for a in range(10):
            acc = spectra[0] * float(solve[a, 0])
            for k in range(1, 10):
                acc = acc + spectra[k] * float(solve[a, k])
            restored.append(acc)
        lows = [restored[1], restored[3], restored[5], restored[7], restored[0]]
        highs = [restored[2], restored[4], restored[6], restored[8], restored[9]]
        given = mm(jnp.concatenate([stack(lows), stack(highs)], axis=1), w_back)
        own, other = tiles(given[:, :LANES]), tiles(given[:, LANES:])
        own = [
            o + jnp.where(node_s <= 1, before(n), jnp.where(node_s >= 6, after(n), 0.0))
            for o, n in zip(own, other)
        ]
        far_left, far_right = exchange(
            step,
            jnp.where(low, own[4], swap(own[0])),
            jnp.where(low, swap(own[3]), own[4]),
        )
        return stack([own[0] + far_left, own[1], own[2], own[3] + far_right])

    def apply(step, field):
        axial, around, radial = gradient(field)
        local = gradient_t(squares[0] * axial, squares[1] * around, squares[2] * radial)
        local = around_sum(local + mass_shift * mass * field)
        (image,), halo = axial_sum(step, [local])
        return image, halo

    def inner(one, two):
        return jnp.sum(one * two * share, axis=0, keepdims=True)

    spaces, images = [], []
    current, halo = source, source_halo
    for it in range(ITERS):
        spaces.append(smooth(2 + 2 * it, current, halo))
        current, halo = apply(3 + 2 * it, spaces[-1])
        images.append(current)

    pairs = [(source, spaces[0])] + [
        (images[i], spaces[j]) for i in range(3) for j in range(i, 3)
    ]
    value = jnp.concatenate([inner(x, y) for x, y in pairs] + [jnp.zeros((1, LANES))], axis=0)
    started = []
    for stage, (stride, size) in enumerate(stages):
        digit = lax.rem(me // stride, size)
        gathered[stage, digit] = value
        for offset in range(1, size):
            copy = pltpu.make_async_remote_copy(
                src_ref=gathered.at[stage, digit],
                dst_ref=gathered.at[stage, digit],
                send_sem=gather_send_sem.at[stage, offset],
                recv_sem=gather_recv_sem.at[stage, offset],
                device_id=(peer(stage, offset),),
                device_id_type=MESH,
            )
            copy.start()
            started.append(copy)
        for copy in started[1 - size :]:
            copy.wait_recv()
        value = gathered[stage, 0]
        for slot in range(1, size):
            value = value + gathered[stage, slot]
    sums = jnp.sum(value, axis=1, keepdims=True)
    sums = [sums[i : i + 1] for i in range(7)]
    gram = {}
    for at, (i, j) in enumerate([(i, j) for i in range(3) for j in range(i, 3)]):
        gram[i, j] = gram[j, i] = sums[1 + at]
    heads = [sums[0], gram[0, 0], gram[0, 1]]
    taken = [None] * 3
    direction = [None] * 3
    result = [None] * 3
    previous = None
    for it in range(ITERS):
        z = [None] * 3
        z[0] = jnp.ones((1, 1), jnp.float32)
        for k in range(1, it + 1):
            z[k] = taken[k - 1]
        rho = heads[0]
        for k in range(1, it + 1):
            rho = rho + z[k] * heads[k]
        for i in range(it):
            row = gram[i, 0]
            for k in range(1, it + 1):
                row = row + z[k] * gram[i, k]
            rho = rho + taken[i] * row
        if it == 0:
            direction = [z[0], None, None]
        else:
            beta = rho / previous
            direction = [
                None if k > it else z[k] if direction[k] is None else z[k] + beta * direction[k]
                for k in range(3)
            ]
        bottom = None
        for i in range(it + 1):
            row = None
            for k in range(it + 1):
                term = direction[k] * gram[i, k]
                row = term if row is None else row + term
            bottom = direction[i] * row if bottom is None else bottom + direction[i] * row
        alpha = rho / bottom
        for k in range(it + 1):
            step = alpha * direction[k]
            result[k] = step if result[k] is None else result[k] + step
            taken[k] = -step if taken[k] is None else taken[k] - step
        previous = rho
    final = [spaces[0] * result[0], source]
    for k in range(3):
        final[1] = final[1] + images[k] * taken[k]
        if k:
            final[0] = final[0] + spaces[k] * result[k]

    for which, ref in enumerate((pressure_ref, residual_ref)):
        for j, tile in enumerate(tiles(final[which])):
            turned[which, pl.ds(2 * j * ES, ES)] = tile
            turned[which, pl.ds((2 * j + 1) * ES, ES)] = swap(tile)
        for p in range(ES):
            block = turned[which, pl.ds(p, NP, stride=ES), :]
            ref[:, p * 56 : (p + 1) * 56] = block[:, :56]

    for step in range(ROUNDS):
        _, to_left, to_right = copies(step)
        to_left.wait_send()
        to_right.wait_send()
    for copy in started:
        copy.wait_send()


def shards(count, velocity, conv_past, metric, jacobian, element_slot):
    arrays, _, _ = constants()
    stages = stages_of(count)
    block = jax.ShapeDtypeStruct((A0, A1 * A2), jnp.float32)
    whole = pl.BlockSpec(memory_space=pltpu.VMEM)
    rows = (3 + ROUNDS) * ES
    slots = jnp.tile(element_slot, 3).reshape(1, 3 * ES)
    return pl.pallas_call(
        functools.partial(kernel, count),
        out_shape=(block, block),
        in_specs=[whole] * (5 + len(arrays)),
        out_specs=(whole, whole),
        scratch_shapes=[
            pltpu.VMEM((rows, LANES), jnp.float32),
            pltpu.VMEM((rows, LANES), jnp.float32),
            pltpu.VMEM((rows, LANES), jnp.float32),
            pltpu.VMEM((rows, LANES), jnp.float32),
            pltpu.VMEM((len(stages), 8, 8, LANES), jnp.float32),
            pltpu.VMEM((2, NP * ES, LANES), jnp.float32),
            pltpu.SemaphoreType.DMA((ROUNDS,)),
            pltpu.SemaphoreType.DMA((ROUNDS,)),
            pltpu.SemaphoreType.DMA((ROUNDS,)),
            pltpu.SemaphoreType.DMA((ROUNDS,)),
            pltpu.SemaphoreType.DMA((len(stages), 8)),
            pltpu.SemaphoreType.DMA((len(stages), 8)),
        ],
        compiler_params=pltpu.CompilerParams(
            collective_id=0, has_side_effects=True, vmem_limit_bytes=40 * 1024 * 1024
        ),
    )(velocity, conv_past, metric, jacobian, slots, *[jnp.asarray(a) for a in arrays])


def solution(mesh):
    return jax.shard_map(
        functools.partial(shards, mesh.shape["dom"]),
        mesh=mesh,
        in_specs=(
            P(None, None, "dom", None),
            P(None, None, "dom", None),
            P(None, "dom", None),
            P("dom", None),
            P("dom"),
        ),
        out_specs=(P("dom", None), P("dom", None)),
        check_vma=False,
    )
```

```python
import functools

import jax
import jax.numpy as jnp
import numpy as np
from jax import lax
from jax.experimental import pallas as pl
from jax.experimental.pallas import tpu as pltpu
from jax.sharding import PartitionSpec as P

NP = 8
NF = 12
ES = 16
ITERS = 3
A0 = 8
A1 = 112
A2 = 8
ROUNDS = 8
LANES = 128
MESH = pl.DeviceIdType.MESH

time_step = 0.25
viscosity = 0.05
mass_shift = 0.001


def legendre_pair(points, order):
    before = np.ones(points.shape)
    current = points * 1.0
    for level in range(2, order + 1):
        nextone = ((2 * level - 1) * points * current - (level - 1) * before) / level
        before = current
        current = nextone
    return (current, before)


def jacobi_eigen(matrix):
    size = matrix.shape[0]
    work = matrix * 1.0
    vectors = np.eye(size)
    for sweep in range(30):
        for first in range(size - 1):
            for second in range(first + 1, size):
                off = float(work[first, second])
                if abs(off) > 1e-300:
                    tau = (float(work[second, second]) - float(work[first, first])) / (2.0 * off)
                    if tau >= 0.0:
                        tangent = 1.0 / (tau + (1.0 + tau * tau) ** 0.5)
                    else:
                        tangent = -1.0 / (-tau + (1.0 + tau * tau) ** 0.5)
                    cosine = 1.0 / (1.0 + tangent * tangent) ** 0.5
                    sine = tangent * cosine
                    rotation = np.eye(size)
                    rotation[first, first] = cosine
                    rotation[second, second] = cosine
                    rotation[first, second] = sine
                    rotation[second, first] = -sine
                    work = rotation.T @ work @ rotation
                    vectors = vectors @ rotation
    diagonal_index = np.arange(size)
    return (work[diagonal_index, diagonal_index], vectors)


def build_tables(points_edge, points_fine):
    degree = points_edge - 1
    points = -np.cos(np.pi * np.arange(points_edge) / degree)
    for sweep in range(100):
        top, below = legendre_pair(points, degree)
        points = points - (points * top - below) / (points_edge * top)
    top, below = legendre_pair(points, degree)
    weight_gll = 2.0 / (degree * points_edge * top**2)
    spacing = points[:, None] - points[None, :] + np.eye(points_edge)
    barycentric = 1.0 / np.prod(spacing, axis=1)
    derivative = barycentric[None, :] / barycentric[:, None] / spacing
    derivative = derivative * (1.0 - np.eye(points_edge))
    derivative = derivative - np.eye(points_edge) * derivative.sum(axis=1)[:, None]
    fine_points = np.cos(np.pi * (np.arange(points_fine) + 0.75) / (points_fine + 0.5))
    for sweep in range(100):
        top, below = legendre_pair(fine_points, points_fine)
        slope = points_fine * (fine_points * top - below) / (fine_points * fine_points - 1.0)
        fine_points = fine_points - top / slope
    top, below = legendre_pair(fine_points, points_fine)
    slope = points_fine * (fine_points * top - below) / (fine_points * fine_points - 1.0)
    fine_weight = 2.0 / ((1.0 - fine_points * fine_points) * slope * slope)
    fine_points = fine_points[::-1]
    fine_weight = fine_weight[::-1]
    interpolate = np.ones((points_fine, points_edge))
    for column in range(points_edge):
        for other in range(points_edge):
            if other != column:
                interpolate[:, column] = (
                    interpolate[:, column]
                    * (fine_points - points[other])
                    / (points[column] - points[other])
                )
    stiffness = derivative.T @ (weight_gll[:, None] * derivative)
    extent = 3 * degree + 1
    joined_stiff = np.zeros((extent, extent))
    joined_mass = np.zeros(extent)
    for segment in range(3):
        offset = segment * degree
        joined_stiff[offset : offset + points_edge, offset : offset + points_edge] += stiffness
        joined_mass[offset : offset + points_edge] += weight_gll
    low = degree - 1
    high = 2 * degree + 2
    root_mass = np.sqrt(joined_mass[low:high])
    scaled = joined_stiff[low:high, low:high] / root_mass[:, None] / root_mass[None, :]
    scaled = 0.5 * (scaled + scaled.T)
    eigen_values, eigen_vectors = jacobi_eigen(scaled)
    solve_mat = eigen_vectors / root_mass[:, None]
    breadth = high - low
    identity = np.eye(points_edge)
    operator_tables = {
        "derivative": derivative,
        "dpair": np.concatenate(
            [np.kron(derivative, identity).T, np.kron(identity, derivative).T], axis=1
        ),
        "interpolate": interpolate,
        "ipair": np.kron(interpolate, interpolate).T,
        "mass_three": (
            weight_gll[:, None, None] * weight_gll[None, :, None] * weight_gll[None, None, :]
        ).reshape(points_edge, points_edge * points_edge),
        "fine_three": (
            fine_weight[:, None, None] * fine_weight[None, :, None] * fine_weight[None, None, :]
        ).reshape(points_fine, points_fine * points_fine),
        "solve_mat": solve_mat,
        "solve_pair": np.kron(solve_mat, solve_mat),
        "eigen_axial": eigen_values,
        "eigen_around": np.repeat(eigen_values, breadth),
        "eigen_radial": np.tile(eigen_values, breadth),
    }
    operator_tables["weight"] = weight_gll
    operator_tables["fine_weight"] = fine_weight
    return operator_tables


def split_rows(matrix):
    exact = np.asarray(matrix, np.float32)
    high = exact.astype(jnp.bfloat16)
    low = (exact - high.astype(np.float32)).astype(jnp.bfloat16)
    columns = range(0, exact.shape[1], LANES)
    return np.concatenate([part[:, c : c + LANES] for c in columns for part in (high, low)])


def halves(matrix):
    rows, columns = matrix.shape
    table = np.zeros((rows // 2, columns // 2, 2, LANES))
    for out in range(rows // 2):
        for into in range(columns // 2):
            table[out, into, 0, :64] = matrix[2 * out, 2 * into]
            table[out, into, 0, 64:] = matrix[2 * out + 1, 2 * into + 1]
            table[out, into, 1, :64] = matrix[2 * out, 2 * into + 1]
            table[out, into, 1, 64:] = matrix[2 * out + 1, 2 * into]
    return np.asarray(table.reshape(-1, LANES), np.float32)


def twice(block, stride):
    rows, columns = block.shape
    result = np.zeros((2 * rows, 2 * stride))
    result[:rows, :columns] = block
    result[rows:, stride : stride + columns] = block
    return result


def pad_columns(matrix, total):
    return np.pad(matrix, ((0, 0), (0, total - matrix.shape[1])))


def by_tile(table):
    return np.asarray(np.repeat(table.reshape(-1, LANES), ES, axis=0), np.float32)


@functools.cache
def constants():
    t = build_tables(NP, NF)
    d, itp, s = t["derivative"], t["interpolate"], t["solve_mat"]
    eye = np.eye(NP)
    pair = np.concatenate(
        [twice(np.kron(d, eye).T, 64), twice(np.kron(eye, d).T, 64)], axis=1
    )
    fine = pad_columns(twice(np.kron(itp, itp).T, 144), 384)
    slope = itp @ d
    fine_slope = np.concatenate(
        [
            pad_columns(twice(np.kron(slope, itp).T, 144), 384),
            pad_columns(twice(np.kron(itp, slope).T, 144), 384),
        ],
        axis=1,
    )
    inner = s[1:9]
    ahead = np.zeros((2 * LANES, 2 * LANES))
    back = np.zeros((2 * LANES, 2 * LANES))
    for h in range(2):
        out = slice(h * LANES, h * LANES + 100)

        def lanes(row):
            return slice(h * 64 + row * 8, h * 64 + row * 8 + 8)

        def beside(row):
            return slice(LANES + h * 64 + row * 8, LANES + h * 64 + row * 8 + 8)

        for row in range(NP):
            ahead[lanes(row), out] = np.kron(s[row + 1 : row + 2], inner)
            back[lanes(row), out] = np.kron(s[row + 1 : row + 2], inner)
        ahead[beside(6), out] = np.kron(s[0:1], inner)
        ahead[beside(1), out] = np.kron(s[9:10], inner)
        back[beside(0), out] = np.kron(s[8:9], inner)
        back[beside(1), out] = np.kron(s[9:10], inner)
        back[beside(7), out] = np.kron(s[1:2], inner)
        back[beside(6), out] = np.kron(s[0:1], inner)
    wf = t["fine_weight"]
    wf2 = (wf[:, None] * wf[None, :]).reshape(-1)
    fine_mass = np.zeros((6, 384))
    for j in range(6):
        fine_mass[j, :144] = wf[2 * j] * wf2
        fine_mass[j, 144:288] = wf[2 * j + 1] * wf2
    eigen = np.zeros((2, LANES))
    eigen[0, :100] = t["eigen_around"]
    eigen[1, :100] = t["eigen_radial"]
    nodes = by_tile(t["mass_three"])
    weights = np.concatenate(
        [split_rows(m) for m in (pair, pair.T, fine, fine_slope, fine.T, ahead, back.T)]
    )
    along = np.concatenate([halves(d), halves(d.T), halves(itp), halves(slope), halves(itp.T)])
    fine_mass = np.repeat(fine_mass, ES, axis=0)
    tables = np.concatenate(
        [along, nodes]
        + [fine_mass[:, c : c + LANES] for c in range(0, 384, LANES)]
        + [np.pad(eigen, ((0, 6), (0, 0)))]
    )
    return (
        weights,
        np.asarray(tables, np.float32),
        np.asarray(s, np.float32),
        np.asarray(t["eigen_axial"], np.float32),
    )


PAIR = (0, 128, 256)
PAIR_T = (512, 256, 128)
FINE = (1024, 128, 384)
SLOPE = (1792, 128, 768)
FINE_T = (3328, 384, 128)
AHEAD = (4096, 256, 256)
BACK = (5120, 256, 256)
TABLE_NODES, TABLE_FINE, TABLE_EIGEN = 208, 272, 560
COEF_D, COEF_DT, COEF_I, COEF_S, COEF_IT = 0, 32, 64, 112, 160


OPERANDS = 7


def stages_of(count):
    stages = []
    stride = 1
    while stride < count:
        size = min(8, count // stride)
        while (count // stride) % size:
            size -= 1
        stages.append((stride, size))
        stride *= size
    return stages


def kernel(
    count,
    *refs,
):
    operands, refs = refs[:OPERANDS], refs[OPERANDS:]
    pressure_ref, residual_ref = refs[:2]
    held, refs = refs[2 : 2 + OPERANDS], refs[2 + OPERANDS :]
    (
        load_sem,
    send_left,
    send_right,
    from_left,
    from_right,
    gathered,
    turned,
    send_left_sem,
    send_right_sem,
    from_left_sem,
    from_right_sem,
    gather_send_sem,
    gather_recv_sem,
    ) = refs
    split = [(0, None)] * 5 + [(0, AHEAD[0]), (AHEAD[0], None), (0, None)]
    loads = []
    for i, (at, end) in enumerate(split):
        which = min(i, 5) if i < 7 else 6
        rows = slice(None) if i < 5 else pl.ds(at, (end or operands[which].shape[0]) - at)
        loads.append(
            pltpu.make_async_copy(
                operands[which].at[rows], held[which].at[rows], load_sem.at[i]
            )
        )
    for i in (3, 2, 0, 7, 5, 1, 4, 6):
        loads[i].start()
    velocity, past, metric, jacobian, slots, weights, tables = held

    _, _, solve, eigen_axial = constants()
    me = lax.axis_index("dom")
    left = lax.rem(me + count - 1, count)
    right = lax.rem(me + 1, count)
    stages = stages_of(count)

    def peer(stage, offset):
        stride, size = stages[stage]
        digit = lax.rem(me // stride, size)
        other = lax.rem(digit + offset, size)
        return me + (other - digit) * stride

    barrier = pltpu.get_barrier_semaphore()
    greeted = [left, right] + [
        peer(stage, offset)
        for stage in range(len(stages))
        for offset in range(1, stages[stage][1])
    ]
    for other in greeted:
        pl.semaphore_signal(barrier, inc=1, device_id=(other,), device_id_type=MESH)

    lane = lax.broadcasted_iota(jnp.int32, (ES, LANES), 1)
    low = lane < 64
    node_s = lax.rem(lane, 64) // 8

    def tiles(field):
        return [field[i * ES : (i + 1) * ES] for i in range(field.shape[0] // ES)]

    def stack(parts):
        return jnp.concatenate(parts, axis=0)

    def mm(x, w):
        high = x.astype(jnp.bfloat16)
        rest = (x - high.astype(jnp.float32)).astype(jnp.bfloat16)
        at, depth, width = w
        columns = []
        for c in range(width // LANES):
            top = weights[at + 2 * c * depth : at + (2 * c + 1) * depth]
            bottom = weights[at + (2 * c + 1) * depth : at + (2 * c + 2) * depth]
            columns.append(jnp.concatenate([top, top, bottom], axis=0))
        return jnp.dot(
            jnp.concatenate([high, rest, high], axis=1),
            jnp.concatenate(columns, axis=1),
            preferred_element_type=jnp.float32,
        )

    def swap(tile):
        return pltpu.roll(tile, 64, 1)

    def along(field, base, total):
        parts = tiles(field)
        swapped = [swap(part) for part in parts]
        results = []
        for out in range(total):
            acc = None
            for into in range(len(parts)):
                at = base + 2 * (out * len(parts) + into)
                term = tables[at : at + 1] * parts[into] + tables[at + 1 : at + 2] * swapped[into]
                acc = term if acc is None else acc + term
            results.append(acc)
        return stack(results)

    def gradient(field):
        paired = mm(field, PAIR)
        return along(field, COEF_D, 4), paired[:, :LANES], paired[:, LANES:]

    def gradient_t(axial, around, radial):
        paired = mm(jnp.concatenate([around, radial], axis=1), PAIR_T)
        return paired + along(axial, COEF_DT, 4)

    def before(tile):
        return pltpu.roll(tile, 1, 0)

    def after(tile):
        return pltpu.roll(tile, ES - 1, 0)

    def around_sum(field):
        results = []
        for tile in tiles(field):
            first = before(pltpu.roll(tile, 72, 1))
            last = after(pltpu.roll(tile, 56, 1))
            results.append(
                tile + jnp.where(node_s == 0, first, jnp.where(node_s == 7, last, 0.0))
            )
        return stack(results)

    def copies(step):
        at, size = (0, 4 * ES) if step == 0 else ((3 + step) * ES, ES)
        rows = pl.ds(at, size)
        to_left = pltpu.make_async_remote_copy(
            src_ref=send_left.at[rows],
            dst_ref=from_right.at[rows],
            send_sem=send_left_sem.at[step],
            recv_sem=from_right_sem.at[step],
            device_id=(left,),
            device_id_type=MESH,
        )
        to_right = pltpu.make_async_remote_copy(
            src_ref=send_right.at[rows],
            dst_ref=from_left.at[rows],
            send_sem=send_right_sem.at[step],
            recv_sem=from_left_sem.at[step],
            device_id=(right,),
            device_id_type=MESH,
        )
        return rows, to_left, to_right

    def send(step, for_left, for_right):
        rows, to_left, to_right = copies(step)
        send_left[rows] = for_left
        to_left.start()
        send_right[rows] = for_right
        to_right.start()

    def receive(step):
        rows, to_left, to_right = copies(step)
        to_right.wait_recv()
        to_left.wait_recv()
        return from_left[rows], from_right[rows]

    def send_faces(step, fields):
        parts = [tiles(field) for field in fields]
        send(step, stack([p[0] for p in parts]), stack([p[3] for p in parts]))

    def axial_sum(step, fields):
        parts = [tiles(field) for field in fields]
        lefts, rights = receive(step)
        lefts, rights = tiles(lefts), tiles(rights)
        results = []
        for p, far_left, far_right in zip(parts, lefts, rights):
            results.append(
                stack(
                    [
                        p[0] + jnp.where(low, swap(far_left), 0.0),
                        p[1],
                        p[2],
                        p[3] + jnp.where(low, 0.0, swap(far_right)),
                    ]
                )
            )
        return results, jnp.where(low, lefts[0], rights[0])

    def element_field(ref, *index):
        return stack([ref[index + (slice(None), pl.ds(j * LANES, LANES))] for j in range(4)])

    for i in (3, 2, 0, 7, 5, 1, 4):
        loads[i].wait()
    weight3 = tables[TABLE_NODES:TABLE_FINE]
    fine_mass = jnp.concatenate(
        [tables[TABLE_FINE + 96 * c : TABLE_FINE + 96 * (c + 1)] for c in range(3)], axis=1
    )
    eigen = tables[TABLE_EIGEN:]
    jac = element_field(jacobian)
    mass = jac * weight3
    metrics = [element_field(metric, d) for d in range(3)]
    squares = [mass * m * m for m in metrics]
    newest = [element_field(velocity, 0, i) for i in range(3)]
    coarse = [along(jac, COEF_I, 6)]
    coarse += [along(newest[d] * metrics[d], COEF_I, 6) for d in range(3)]
    coarse += [along(newest[i], COEF_S, 6) for i in range(3)]
    fine = mm(stack(coarse), FINE)
    fine = [fine[i * 96 : (i + 1) * 96] for i in range(7)]
    crossed = mm(stack([along(newest[i], COEF_I, 6) for i in range(3)]), SLOPE)
    fine_jac = fine[0] * fine_mass
    products = []
    for i in range(3):
        rows = slice(i * 96, (i + 1) * 96)
        products.append(
            fine_jac
            * (
                fine[1] * fine[4 + i]
                + fine[2] * crossed[rows, :384]
                + fine[3] * crossed[rows, 384:]
            )
        )
    advected = mm(stack(products), FINE_T)
    guessed = [
        3.0 * newest[i] - 3.0 * element_field(velocity, 1, i) + element_field(velocity, 2, i)
        for i in range(3)
    ]
    paired = mm(stack(guessed), PAIR)
    slopes = jnp.concatenate(
        [
            stack([squares[1] * paired[i * 64 : (i + 1) * 64, :LANES] for i in range(3)]),
            stack([squares[2] * paired[i * 64 : (i + 1) * 64, LANES:] for i in range(3)]),
        ],
        axis=1,
    )
    paired_t = mm(slopes, PAIR_T)
    forcing = []
    for i in range(3):
        convect = along(advected[i * 96 : (i + 1) * 96], COEF_IT, 4)
        stiff = paired_t[i * 64 : (i + 1) * 64] + along(
            squares[0] * along(guessed[i], COEF_D, 4), COEF_DT, 4
        )
        history = (
            3.0 * newest[i]
            - 1.5 * element_field(velocity, 1, i)
            + element_field(velocity, 2, i) / 3.0
        )
        extrap = (
            3.0 * convect - 3.0 * element_field(past, 0, i) + element_field(past, 1, i)
        )
        helmholtz = viscosity * stiff + 11.0 / (6.0 * time_step) * mass * guessed[i]
        forcing.append(mass * history / time_step - extrap - helmholtz)

    fields = forcing + [mass] + metrics
    wide = jnp.concatenate([tile for field in fields for tile in tiles(field)], axis=1)
    first = wide.astype(jnp.bfloat16)
    rest = wide - first.astype(jnp.float32)
    second = rest.astype(jnp.bfloat16)
    third = (rest - second.astype(jnp.float32)).astype(jnp.bfloat16)
    position = lax.broadcasted_iota(jnp.int32, (ES, ES), 0)
    chosen = jnp.where(slots[...] == position, 1.0, 0.0)
    chosen = jnp.concatenate([chosen, chosen, chosen], axis=1).astype(jnp.bfloat16)
    placed = jnp.dot(chosen, stack([first, second, third]), preferred_element_type=jnp.float32)
    fields = [
        stack([placed[:, (4 * f + j) * LANES : (4 * f + j + 1) * LANES] for j in range(4)])
        for f in range(7)
    ]
    forcing, mass, metrics = fields[:3], fields[3], fields[4:]
    around = [around_sum(f) for f in forcing + [mass]]
    pl.semaphore_wait(barrier, len(greeted))
    send_faces(0, around)
    lumps = [mass * m for m in metrics]
    squares = [lumps[d] * metrics[d] for d in range(3)]

    def total(field):
        parts = tiles(field)
        return jnp.sum(parts[0] + parts[1] + parts[2] + parts[3], axis=1, keepdims=True) / 8.0

    scales = [total(square) for square in squares]
    flat = (
        scales[1] * eigen[0:1] + scales[2] * eigen[1:2] + mass_shift * total(mass)
    )
    inverse = [1.0 / (scales[0] * float(eigen_axial[k]) + flat) for k in range(10)]

    summed, _ = axial_sum(0, around)
    accel = [lumps[d] * (summed[d] / summed[3]) for d in range(3)]
    divergence = gradient_t(accel[0], accel[1], accel[2])
    source = around_sum(divergence)
    send_faces(1, [source])
    loads[6].wait()
    (source,), source_halo = axial_sum(1, [source])

    def smooth(step, field, halo):
        parts = tiles(field) + [halo]
        sides = [
            jnp.where(node_s == 6, before(p), jnp.where(node_s == 1, after(p), 0.0))
            for p in parts
        ]
        modes = mm(jnp.concatenate([stack(parts), stack(sides)], axis=1), AHEAD)
        rows = tiles(modes)
        order = [rows[4][:, :LANES]]
        for j in range(4):
            order += [rows[j][:, :LANES], rows[j][:, LANES:]]
        order.append(rows[4][:, LANES:])
        spectra = []
        for k in range(10):
            acc = order[0] * float(solve[0, k])
            for a in range(1, 10):
                acc = acc + order[a] * float(solve[a, k])
            spectra.append(acc * inverse[k])
        restored = []
        for a in range(10):
            acc = spectra[0] * float(solve[a, 0])
            for k in range(1, 10):
                acc = acc + spectra[k] * float(solve[a, k])
            restored.append(acc)
        lows = [restored[1], restored[3], restored[5], restored[7], restored[0]]
        highs = [restored[2], restored[4], restored[6], restored[8], restored[9]]
        given = mm(jnp.concatenate([stack(lows), stack(highs)], axis=1), BACK)
        own, other = tiles(given[:, :LANES]), tiles(given[:, LANES:])
        own = [
            o + jnp.where(node_s <= 1, before(n), jnp.where(node_s >= 6, after(n), 0.0))
            for o, n in zip(own, other)
        ]
        send(
            step,
            jnp.where(low, own[4], swap(own[0])),
            jnp.where(low, swap(own[3]), own[4]),
        )
        far_left, far_right = receive(step)
        return stack([own[0] + far_left, own[1], own[2], own[3] + far_right])

    def apply(field):
        axial, around, radial = gradient(field)
        local = gradient_t(squares[0] * axial, squares[1] * around, squares[2] * radial)
        return local + mass_shift * mass * field

    def inner(one, two):
        return jnp.sum(one * two, axis=0, keepdims=True)

    spaces, images, dots = [], [], {}
    current, halo = source, source_halo
    for it in range(ITERS):
        step = 3 + 2 * it
        spaces.append(smooth(step - 1, current, halo))
        local = apply(spaces[-1])
        image = around_sum(local)
        send_faces(step, [image])
        if it == 0:
            head = inner(divergence, spaces[0])
        for j in range(it + 1):
            dots[j, it] = inner(local, spaces[j])
        if it < ITERS - 1:
            (current,), halo = axial_sum(step, [image])
            images.append(current)

    value = jnp.concatenate(
        [head]
        + [dots[i, j] for i in range(3) for j in range(i, 3)]
        + [jnp.zeros((1, LANES), jnp.float32)],
        axis=0,
    )
    started = []
    for stage, (stride, size) in enumerate(stages):
        digit = lax.rem(me // stride, size)
        gathered[stage, digit] = value
        for offset in range(1, size):
            copy = pltpu.make_async_remote_copy(
                src_ref=gathered.at[stage, digit],
                dst_ref=gathered.at[stage, digit],
                send_sem=gather_send_sem.at[stage, offset],
                recv_sem=gather_recv_sem.at[stage, offset],
                device_id=(peer(stage, offset),),
                device_id_type=MESH,
            )
            copy.start()
            started.append(copy)
        for copy in started[1 - size :]:
            copy.wait_recv()
        value = gathered[stage, 0]
        for slot in range(1, size):
            value = value + gathered[stage, slot]
    sums = jnp.sum(value, axis=1, keepdims=True)
    sums = [sums[i : i + 1] for i in range(7)]
    gram = {}
    for at, (i, j) in enumerate([(i, j) for i in range(3) for j in range(i, 3)]):
        gram[i, j] = gram[j, i] = sums[1 + at]
    heads = [sums[0], gram[0, 0], gram[0, 1]]
    taken = [None] * 3
    direction = [None] * 3
    result = [None] * 3
    previous = None
    for it in range(ITERS):
        z = [None] * 3
        z[0] = jnp.ones((1, 1), jnp.float32)
        for k in range(1, it + 1):
            z[k] = taken[k - 1]
        rho = heads[0]
        for k in range(1, it + 1):
            rho = rho + z[k] * heads[k]
        for i in range(it):
            row = gram[i, 0]
            for k in range(1, it + 1):
                row = row + z[k] * gram[i, k]
            rho = rho + taken[i] * row
        if it == 0:
            direction = [z[0], None, None]
        else:
            beta = rho / previous
            direction = [
                None if k > it else z[k] if direction[k] is None else z[k] + beta * direction[k]
                for k in range(3)
            ]
        bottom = None
        for i in range(it + 1):
            row = None
            for k in range(it + 1):
                term = direction[k] * gram[i, k]
                row = term if row is None else row + term
            bottom = direction[i] * row if bottom is None else bottom + direction[i] * row
        alpha = rho / bottom
        for k in range(it + 1):
            step = alpha * direction[k]
            result[k] = step if result[k] is None else result[k] + step
            taken[k] = -step if taken[k] is None else taken[k] - step
        previous = rho
    (current,), _ = axial_sum(ROUNDS - 1, [image])
    images.append(current)
    final = [spaces[0] * result[0], source]
    for k in range(3):
        final[1] = final[1] + images[k] * taken[k]
        if k:
            final[0] = final[0] + spaces[k] * result[k]

    for which, ref in enumerate((pressure_ref, residual_ref)):
        for j, tile in enumerate(tiles(final[which])):
            turned[which, pl.ds(2 * j * ES, ES)] = tile
            turned[which, pl.ds((2 * j + 1) * ES, ES)] = swap(tile)
        for p in range(ES):
            block = turned[which, pl.ds(p, NP, stride=ES), :]
            ref[:, p * 56 : (p + 1) * 56] = block[:, :56]

    for step in range(ROUNDS):
        _, to_left, to_right = copies(step)
        to_left.wait_send()
        to_right.wait_send()
    for copy in started:
        copy.wait_send()


def shards(count, velocity, conv_past, metric, jacobian, element_slot):
    weights, tables, _, _ = constants()
    stages = stages_of(count)
    block = jax.ShapeDtypeStruct((A0, A1 * A2), jnp.float32)
    whole = pl.BlockSpec(memory_space=pltpu.VMEM)
    rows = (3 + ROUNDS) * ES
    slots = element_slot.reshape(1, ES)
    operands = [velocity, conv_past, metric, jacobian, slots]
    operands += [jnp.asarray(weights), jnp.asarray(tables)]
    return pl.pallas_call(
        functools.partial(kernel, count),
        out_shape=(block, block),
        in_specs=[pl.BlockSpec(memory_space=pltpu.HBM)] * len(operands),
        out_specs=(whole, whole),
        scratch_shapes=[pltpu.VMEM(x.shape, x.dtype) for x in operands]
        + [
            pltpu.SemaphoreType.DMA((len(operands) + 1,)),
            pltpu.VMEM((rows, LANES), jnp.float32),
            pltpu.VMEM((rows, LANES), jnp.float32),
            pltpu.VMEM((rows, LANES), jnp.float32),
            pltpu.VMEM((rows, LANES), jnp.float32),
            pltpu.VMEM((len(stages), 8, 8, LANES), jnp.float32),
            pltpu.VMEM((2, NP * ES, LANES), jnp.float32),
            pltpu.SemaphoreType.DMA((ROUNDS,)),
            pltpu.SemaphoreType.DMA((ROUNDS,)),
            pltpu.SemaphoreType.DMA((ROUNDS,)),
            pltpu.SemaphoreType.DMA((ROUNDS,)),
            pltpu.SemaphoreType.DMA((len(stages), 8)),
            pltpu.SemaphoreType.DMA((len(stages), 8)),
        ],
        compiler_params=pltpu.CompilerParams(
            collective_id=0, has_side_effects=True, vmem_limit_bytes=56 * 1024 * 1024
        ),
    )(*operands)


def solution(mesh):
    return jax.shard_map(
        functools.partial(shards, mesh.shape["dom"]),
        mesh=mesh,
        in_specs=(
            P(None, None, "dom", None),
            P(None, None, "dom", None),
            P(None, "dom", None),
            P("dom", None),
            P("dom"),
        ),
        out_specs=(P("dom", None), P("dom", None)),
        check_vma=False,
    )
```

```python
import functools

import jax
import jax.numpy as jnp
import numpy as np
from jax import lax
from jax.experimental import pallas as pl
from jax.experimental.pallas import tpu as pltpu
from jax.sharding import PartitionSpec as P

NP = 8
NF = 12
ES = 16
ITERS = 3
A0 = 8
A1 = 112
A2 = 8
ROUNDS = 5
WAYS = 4
LANES = 128
MESH = pl.DeviceIdType.MESH

time_step = 0.25
viscosity = 0.05
mass_shift = 0.001


def legendre_pair(points, order):
    before = np.ones(points.shape)
    current = points * 1.0
    for level in range(2, order + 1):
        nextone = ((2 * level - 1) * points * current - (level - 1) * before) / level
        before = current
        current = nextone
    return (current, before)


def jacobi_eigen(matrix):
    size = matrix.shape[0]
    work = matrix * 1.0
    vectors = np.eye(size)
    for sweep in range(30):
        for first in range(size - 1):
            for second in range(first + 1, size):
                off = float(work[first, second])
                if abs(off) > 1e-300:
                    tau = (float(work[second, second]) - float(work[first, first])) / (2.0 * off)
                    if tau >= 0.0:
                        tangent = 1.0 / (tau + (1.0 + tau * tau) ** 0.5)
                    else:
                        tangent = -1.0 / (-tau + (1.0 + tau * tau) ** 0.5)
                    cosine = 1.0 / (1.0 + tangent * tangent) ** 0.5
                    sine = tangent * cosine
                    rotation = np.eye(size)
                    rotation[first, first] = cosine
                    rotation[second, second] = cosine
                    rotation[first, second] = sine
                    rotation[second, first] = -sine
                    work = rotation.T @ work @ rotation
                    vectors = vectors @ rotation
    diagonal_index = np.arange(size)
    return (work[diagonal_index, diagonal_index], vectors)


def build_tables(points_edge, points_fine):
    degree = points_edge - 1
    points = -np.cos(np.pi * np.arange(points_edge) / degree)
    for sweep in range(100):
        top, below = legendre_pair(points, degree)
        points = points - (points * top - below) / (points_edge * top)
    top, below = legendre_pair(points, degree)
    weight_gll = 2.0 / (degree * points_edge * top**2)
    spacing = points[:, None] - points[None, :] + np.eye(points_edge)
    barycentric = 1.0 / np.prod(spacing, axis=1)
    derivative = barycentric[None, :] / barycentric[:, None] / spacing
    derivative = derivative * (1.0 - np.eye(points_edge))
    derivative = derivative - np.eye(points_edge) * derivative.sum(axis=1)[:, None]
    fine_points = np.cos(np.pi * (np.arange(points_fine) + 0.75) / (points_fine + 0.5))
    for sweep in range(100):
        top, below = legendre_pair(fine_points, points_fine)
        slope = points_fine * (fine_points * top - below) / (fine_points * fine_points - 1.0)
        fine_points = fine_points - top / slope
    top, below = legendre_pair(fine_points, points_fine)
    slope = points_fine * (fine_points * top - below) / (fine_points * fine_points - 1.0)
    fine_weight = 2.0 / ((1.0 - fine_points * fine_points) * slope * slope)
    fine_points = fine_points[::-1]
    fine_weight = fine_weight[::-1]
    interpolate = np.ones((points_fine, points_edge))
    for column in range(points_edge):
        for other in range(points_edge):
            if other != column:
                interpolate[:, column] = (
                    interpolate[:, column]
                    * (fine_points - points[other])
                    / (points[column] - points[other])
                )
    stiffness = derivative.T @ (weight_gll[:, None] * derivative)
    extent = 3 * degree + 1
    joined_stiff = np.zeros((extent, extent))
    joined_mass = np.zeros(extent)
    for segment in range(3):
        offset = segment * degree
        joined_stiff[offset : offset + points_edge, offset : offset + points_edge] += stiffness
        joined_mass[offset : offset + points_edge] += weight_gll
    low = degree - 1
    high = 2 * degree + 2
    root_mass = np.sqrt(joined_mass[low:high])
    scaled = joined_stiff[low:high, low:high] / root_mass[:, None] / root_mass[None, :]
    scaled = 0.5 * (scaled + scaled.T)
    eigen_values, eigen_vectors = jacobi_eigen(scaled)
    solve_mat = eigen_vectors / root_mass[:, None]
    breadth = high - low
    identity = np.eye(points_edge)
    operator_tables = {
        "derivative": derivative,
        "dpair": np.concatenate(
            [np.kron(derivative, identity).T, np.kron(identity, derivative).T], axis=1
        ),
        "interpolate": interpolate,
        "ipair": np.kron(interpolate, interpolate).T,
        "mass_three": (
            weight_gll[:, None, None] * weight_gll[None, :, None] * weight_gll[None, None, :]
        ).reshape(points_edge, points_edge * points_edge),
        "fine_three": (
            fine_weight[:, None, None] * fine_weight[None, :, None] * fine_weight[None, None, :]
        ).reshape(points_fine, points_fine * points_fine),
        "solve_mat": solve_mat,
        "solve_pair": np.kron(solve_mat, solve_mat),
        "eigen_axial": eigen_values,
        "eigen_around": np.repeat(eigen_values, breadth),
        "eigen_radial": np.tile(eigen_values, breadth),
    }
    operator_tables["weight"] = weight_gll
    operator_tables["fine_weight"] = fine_weight
    return operator_tables


def split_rows(matrix):
    exact = np.asarray(matrix, np.float32)
    high = exact.astype(jnp.bfloat16)
    low = (exact - high.astype(np.float32)).astype(jnp.bfloat16)
    columns = range(0, exact.shape[1], LANES)
    return np.concatenate([part[:, c : c + LANES] for c in columns for part in (high, low)])


def halves(matrix):
    rows, columns = matrix.shape
    table = np.zeros((rows // 2, columns // 2, 2, LANES))
    for out in range(rows // 2):
        for into in range(columns // 2):
            table[out, into, 0, :64] = matrix[2 * out, 2 * into]
            table[out, into, 0, 64:] = matrix[2 * out + 1, 2 * into + 1]
            table[out, into, 1, :64] = matrix[2 * out, 2 * into + 1]
            table[out, into, 1, 64:] = matrix[2 * out + 1, 2 * into]
    return np.asarray(table.reshape(-1, LANES), np.float32)


def twice(block, stride):
    rows, columns = block.shape
    result = np.zeros((2 * rows, 2 * stride))
    result[:rows, :columns] = block
    result[rows:, stride : stride + columns] = block
    return result


def pad_columns(matrix, total):
    return np.pad(matrix, ((0, 0), (0, total - matrix.shape[1])))


def by_tile(table):
    return np.asarray(np.repeat(table.reshape(-1, LANES), ES, axis=0), np.float32)


@functools.cache
def constants():
    t = build_tables(NP, NF)
    d, itp, s = t["derivative"], t["interpolate"], t["solve_mat"]
    eye = np.eye(NP)
    pair = np.concatenate(
        [twice(np.kron(d, eye).T, 64), twice(np.kron(eye, d).T, 64)], axis=1
    )
    fine = pad_columns(twice(np.kron(itp, itp).T, 144), 384)
    slope = itp @ d
    fine_slope = np.concatenate(
        [
            pad_columns(twice(np.kron(slope, itp).T, 144), 384),
            pad_columns(twice(np.kron(itp, slope).T, 144), 384),
        ],
        axis=1,
    )
    inner = s[1:9]
    ahead = np.zeros((2 * LANES, 2 * LANES))
    back = np.zeros((2 * LANES, 2 * LANES))
    for h in range(2):
        out = slice(h * LANES, h * LANES + 100)

        def lanes(row):
            return slice(h * 64 + row * 8, h * 64 + row * 8 + 8)

        def beside(row):
            return slice(LANES + h * 64 + row * 8, LANES + h * 64 + row * 8 + 8)

        for row in range(NP):
            ahead[lanes(row), out] = np.kron(s[row + 1 : row + 2], inner)
            back[lanes(row), out] = np.kron(s[row + 1 : row + 2], inner)
        ahead[beside(6), out] = np.kron(s[0:1], inner)
        ahead[beside(1), out] = np.kron(s[9:10], inner)
        back[beside(0), out] = np.kron(s[8:9], inner)
        back[beside(1), out] = np.kron(s[9:10], inner)
        back[beside(7), out] = np.kron(s[1:2], inner)
        back[beside(6), out] = np.kron(s[0:1], inner)
    wf = t["fine_weight"]
    wf2 = (wf[:, None] * wf[None, :]).reshape(-1)
    fine_mass = np.zeros((6, 384))
    for j in range(6):
        fine_mass[j, :144] = wf[2 * j] * wf2
        fine_mass[j, 144:288] = wf[2 * j + 1] * wf2
    eigen = np.zeros((2, LANES))
    eigen[0, :100] = t["eigen_around"]
    eigen[1, :100] = t["eigen_radial"]
    nodes = by_tile(t["mass_three"])
    weights = np.concatenate(
        [split_rows(m) for m in (pair, pair.T, fine, fine_slope, fine.T, ahead, back.T)]
    )
    along = np.concatenate([halves(d), halves(d.T), halves(itp), halves(slope), halves(itp.T)])
    fine_mass = np.repeat(fine_mass, ES, axis=0)
    tables = np.concatenate(
        [along, nodes]
        + [fine_mass[:, c : c + LANES] for c in range(0, 384, LANES)]
        + [np.pad(eigen, ((0, 6), (0, 0)))]
    )
    return (
        weights,
        np.asarray(tables, np.float32),
        np.asarray(s, np.float32),
        np.asarray(t["eigen_axial"], np.float32),
    )


PAIR = (0, 128, 256)
PAIR_T = (512, 256, 128)
FINE = (1024, 128, 384)
SLOPE = (1792, 128, 768)
FINE_T = (3328, 384, 128)
AHEAD = (4096, 256, 256)
BACK = (5120, 256, 256)
TABLE_NODES, TABLE_FINE, TABLE_EIGEN = 208, 272, 560
COEF_D, COEF_DT, COEF_I, COEF_S, COEF_IT = 0, 32, 64, 112, 160


OPERANDS = 7


def stages_of(count):
    stages = []
    stride = 1
    while stride < count:
        size = min(8, count // stride)
        while (count // stride) % size:
            size -= 1
        stages.append((stride, size))
        stride *= size
    return stages


def kernel(
    count,
    *refs,
):
    operands, refs = refs[:OPERANDS], refs[OPERANDS:]
    pressure_ref, residual_ref = refs[:2]
    held, refs = refs[2 : 2 + OPERANDS], refs[2 + OPERANDS :]
    (
        load_sem,
        first_out,
        first_in,
        outbox,
        inbox,
        inbox_far,
        gathered,
        turned,
        send_sem,
        recv_sem,
        gather_send_sem,
        gather_recv_sem,
    ) = refs
    split = [(0, None)] * 5 + [(0, AHEAD[0]), (AHEAD[0], None), (0, None)]
    loads = []
    for i, (at, end) in enumerate(split):
        which = min(i, 5) if i < 7 else 6
        rows = slice(None) if i < 5 else pl.ds(at, (end or operands[which].shape[0]) - at)
        loads.append(
            pltpu.make_async_copy(
                operands[which].at[rows], held[which].at[rows], load_sem.at[i]
            )
        )
    for i in (3, 2, 0, 7, 5, 1, 4, 6):
        loads[i].start()
    velocity, past, metric, jacobian, slots, weights, tables = held

    _, _, solve, eigen_axial = constants()
    me = lax.axis_index("dom")
    left = lax.rem(me + count - 1, count)
    right = lax.rem(me + 1, count)
    far_left = lax.rem(me + count - 2, count)
    far_right = lax.rem(me + 2, count)
    stages = stages_of(count)

    def peer(stage, offset):
        stride, size = stages[stage]
        digit = lax.rem(me // stride, size)
        other = lax.rem(digit + offset, size)
        return me + (other - digit) * stride

    barrier = pltpu.get_barrier_semaphore()
    greeted = [left, right, far_left, far_right] + [
        peer(stage, offset)
        for stage in range(len(stages))
        for offset in range(1, stages[stage][1])
    ]
    for other in greeted:
        pl.semaphore_signal(barrier, inc=1, device_id=(other,), device_id_type=MESH)

    lane = lax.broadcasted_iota(jnp.int32, (ES, LANES), 1)
    low = lane < 64
    node_s = lax.rem(lane, 64) // 8

    def tiles(field):
        return [field[i * ES : (i + 1) * ES] for i in range(field.shape[0] // ES)]

    def stack(parts):
        return jnp.concatenate(parts, axis=0)

    def mm(x, w):
        high = x.astype(jnp.bfloat16)
        rest = (x - high.astype(jnp.float32)).astype(jnp.bfloat16)
        at, depth, width = w
        columns = []
        for c in range(width // LANES):
            top = weights[at + 2 * c * depth : at + (2 * c + 1) * depth]
            bottom = weights[at + (2 * c + 1) * depth : at + (2 * c + 2) * depth]
            columns.append(jnp.concatenate([top, top, bottom], axis=0))
        return jnp.dot(
            jnp.concatenate([high, rest, high], axis=1),
            jnp.concatenate(columns, axis=1),
            preferred_element_type=jnp.float32,
        )

    def swap(tile):
        return pltpu.roll(tile, 64, 1)

    def along(field, base, total):
        parts = tiles(field)
        swapped = [swap(part) for part in parts]
        results = []
        for out in range(total):
            acc = None
            for into in range(len(parts)):
                at = base + 2 * (out * len(parts) + into)
                term = tables[at : at + 1] * parts[into] + tables[at + 1 : at + 2] * swapped[into]
                acc = term if acc is None else acc + term
            results.append(acc)
        return stack(results)

    def gradient(field):
        paired = mm(field, PAIR)
        return along(field, COEF_D, 4), paired[:, :LANES], paired[:, LANES:]

    def gradient_t(axial, around, radial):
        paired = mm(jnp.concatenate([around, radial], axis=1), PAIR_T)
        return paired + along(axial, COEF_DT, 4)

    def before(tile):
        return pltpu.roll(tile, 1, 0)

    def after(tile):
        return pltpu.roll(tile, ES - 1, 0)

    def around_sum(field):
        results = []
        for tile in tiles(field):
            first = before(pltpu.roll(tile, 72, 1))
            last = after(pltpu.roll(tile, 56, 1))
            results.append(
                tile + jnp.where(node_s == 0, first, jnp.where(node_s == 7, last, 0.0))
            )
        return stack(results)

    def copies(step):
        if step == 0:
            plan = [(first_out.at[0], first_in.at[1], left), (first_out.at[1], first_in.at[0], right)]
        elif step < ROUNDS - 1:
            plan = [
                (outbox.at[step, pl.ds(0, ES)], inbox_far.at[step, 1], far_left),
                (outbox.at[step, pl.ds(3 * ES, ES)], inbox_far.at[step, 0], far_right),
                (outbox.at[step], inbox.at[step, 1], left),
                (outbox.at[step], inbox.at[step, 0], right),
            ]
        else:
            plan = [
                (outbox.at[step, pl.ds(0, ES)], inbox_far.at[step, 1], left),
                (outbox.at[step, pl.ds(3 * ES, ES)], inbox_far.at[step, 0], right),
            ]
        return [
            pltpu.make_async_remote_copy(
                src_ref=source,
                dst_ref=target,
                send_sem=send_sem.at[step, way],
                recv_sem=recv_sem.at[step, way],
                device_id=(other,),
                device_id_type=MESH,
            )
            for way, (source, target, other) in enumerate(plan)
        ]

    def send(step, field):
        outbox[step] = field
        for copy in copies(step):
            copy.start()

    def receive(step):
        for copy in copies(step):
            copy.wait_recv()

    def axial_sum(field, before_it, after_it):
        parts = tiles(field)
        return stack(
            [
                parts[0] + jnp.where(low, swap(before_it), 0.0),
                parts[1],
                parts[2],
                parts[3] + jnp.where(low, 0.0, swap(after_it)),
            ]
        )

    def surrounded(step, field):
        receive(step)
        beside = [inbox[step, 0], inbox[step, 1]]
        ends = [inbox_far[step, 0], inbox_far[step, 1]]
        own = axial_sum(field, beside[0][3 * ES :], beside[1][:ES])
        return own, beside, ends

    def element_field(ref, *index):
        return stack([ref[index + (slice(None), pl.ds(j * LANES, LANES))] for j in range(4)])

    for i in (3, 2, 0, 7, 5, 1, 4):
        loads[i].wait()
    weight3 = tables[TABLE_NODES:TABLE_FINE]
    fine_mass = jnp.concatenate(
        [tables[TABLE_FINE + 96 * c : TABLE_FINE + 96 * (c + 1)] for c in range(3)], axis=1
    )
    eigen = tables[TABLE_EIGEN:]
    jac = element_field(jacobian)
    mass = jac * weight3
    metrics = [element_field(metric, d) for d in range(3)]
    squares = [mass * m * m for m in metrics]
    newest = [element_field(velocity, 0, i) for i in range(3)]
    coarse = [along(jac, COEF_I, 6)]
    coarse += [along(newest[d] * metrics[d], COEF_I, 6) for d in range(3)]
    coarse += [along(newest[i], COEF_S, 6) for i in range(3)]
    fine = mm(stack(coarse), FINE)
    fine = [fine[i * 96 : (i + 1) * 96] for i in range(7)]
    crossed = mm(stack([along(newest[i], COEF_I, 6) for i in range(3)]), SLOPE)
    fine_jac = fine[0] * fine_mass
    products = []
    for i in range(3):
        rows = slice(i * 96, (i + 1) * 96)
        products.append(
            fine_jac
            * (
                fine[1] * fine[4 + i]
                + fine[2] * crossed[rows, :384]
                + fine[3] * crossed[rows, 384:]
            )
        )
    advected = mm(stack(products), FINE_T)
    guessed = [
        3.0 * newest[i] - 3.0 * element_field(velocity, 1, i) + element_field(velocity, 2, i)
        for i in range(3)
    ]
    paired = mm(stack(guessed), PAIR)
    slopes = jnp.concatenate(
        [
            stack([squares[1] * paired[i * 64 : (i + 1) * 64, :LANES] for i in range(3)]),
            stack([squares[2] * paired[i * 64 : (i + 1) * 64, LANES:] for i in range(3)]),
        ],
        axis=1,
    )
    paired_t = mm(slopes, PAIR_T)
    forcing = []
    for i in range(3):
        convect = along(advected[i * 96 : (i + 1) * 96], COEF_IT, 4)
        stiff = paired_t[i * 64 : (i + 1) * 64] + along(
            squares[0] * along(guessed[i], COEF_D, 4), COEF_DT, 4
        )
        history = (
            3.0 * newest[i]
            - 1.5 * element_field(velocity, 1, i)
            + element_field(velocity, 2, i) / 3.0
        )
        extrap = (
            3.0 * convect - 3.0 * element_field(past, 0, i) + element_field(past, 1, i)
        )
        helmholtz = viscosity * stiff + 11.0 / (6.0 * time_step) * mass * guessed[i]
        forcing.append(mass * history / time_step - extrap - helmholtz)

    fields = forcing + [mass] + metrics
    wide = jnp.concatenate([tile for field in fields for tile in tiles(field)], axis=1)
    first = wide.astype(jnp.bfloat16)
    rest = wide - first.astype(jnp.float32)
    second = rest.astype(jnp.bfloat16)
    third = (rest - second.astype(jnp.float32)).astype(jnp.bfloat16)
    position = lax.broadcasted_iota(jnp.int32, (ES, ES), 0)
    chosen = jnp.where(slots[...] == position, 1.0, 0.0)
    chosen = jnp.concatenate([chosen, chosen, chosen], axis=1).astype(jnp.bfloat16)
    placed = jnp.dot(chosen, stack([first, second, third]), preferred_element_type=jnp.float32)
    fields = [
        stack([placed[:, (4 * f + j) * LANES : (4 * f + j + 1) * LANES] for j in range(4)])
        for f in range(7)
    ]
    forcing, mass, metrics = fields[:3], fields[3], fields[4:]
    lumps = [mass * m for m in metrics]
    squares = [lumps[d] * metrics[d] for d in range(3)]

    def total(field):
        parts = tiles(field)
        return jnp.sum(parts[0] + parts[1] + parts[2] + parts[3], axis=1, keepdims=True) / 8.0

    flat = (
        total(squares[1]) * eigen[0:1]
        + total(squares[2]) * eigen[1:2]
        + mass_shift * total(mass)
    )
    steep = jnp.broadcast_to(total(squares[0]), (ES, LANES))

    around = [around_sum(f) for f in forcing + [mass]]
    first_out[0] = stack([f[:ES] for f in around] + [flat, steep])
    first_out[1] = stack([f[3 * ES :] for f in around] + [flat, steep])
    pl.semaphore_wait(barrier, len(greeted))
    for copy in copies(0):
        copy.start()
    receive(0)
    lefts, rights = tiles(first_in[0]), tiles(first_in[1])
    summed = [axial_sum(around[f], lefts[f], rights[f]) for f in range(4)]
    accel = [lumps[d] * (summed[d] / summed[3]) for d in range(3)]
    divergence = gradient_t(accel[0], accel[1], accel[2])
    source = around_sum(divergence)
    send(1, source)
    loads[6].wait()
    flats = stack([lefts[4], flat, rights[4]])
    steeps = stack([lefts[5], steep, rights[5]])
    inverse = [1.0 / (steeps * float(eigen_axial[k]) + flats) for k in range(10)]
    source, beside, ends = surrounded(1, source)

    def combine(weight, parts):
        acc = parts[0] * float(weight[0])
        for one, part in zip(weight[1:], parts[1:]):
            acc = acc + part * float(one)
        return acc

    def smooth(own, beside, ends):
        lower, upper = tiles(beside[0]), tiles(beside[1])
        lower[0] = lower[0] + jnp.where(low, swap(ends[0]), 0.0)
        upper[3] = upper[3] + jnp.where(low, 0.0, swap(ends[1]))
        parts = [jnp.where(low, ends[0], ends[1])] + lower + upper + tiles(own)
        sides = [
            jnp.where(node_s == 6, before(p), jnp.where(node_s == 1, after(p), 0.0))
            for p in parts
        ]
        modes = tiles(mm(jnp.concatenate([stack(parts), stack(sides)], axis=1), AHEAD))
        firsts = [-7, -5, -3, -1, 7, 9, 11, 13, 0, 2, 4, 6]
        grid = {-8: modes[0][:, :LANES], 15: modes[0][:, LANES:]}
        for row, mode in zip(firsts, modes[1:]):
            grid[row], grid[row + 1] = mode[:, :LANES], mode[:, LANES:]
        order = [stack([grid[a - 7], grid[a], grid[a + 7]]) for a in range(-1, 9)]
        spectra = [combine(solve[:, k], order) * inverse[k] for k in range(10)]
        slabs = [[spectrum[b * ES : (b + 1) * ES] for spectrum in spectra] for b in range(3)]
        rows = [combine(solve[a + 1], slabs[1]) for a in range(NP)]
        rows[0] = rows[0] + combine(solve[8], slabs[0])
        rows[1] = rows[1] + combine(solve[9], slabs[0])
        rows[6] = rows[6] + combine(solve[0], slabs[2])
        rows[7] = rows[7] + combine(solve[1], slabs[2])
        given = mm(jnp.concatenate([stack(rows[0::2]), stack(rows[1::2])], axis=1), BACK)
        return stack(
            [
                o + jnp.where(node_s <= 1, before(n), jnp.where(node_s >= 6, after(n), 0.0))
                for o, n in zip(tiles(given[:, :LANES]), tiles(given[:, LANES:]))
            ]
        )

    def apply(field):
        axial, around, radial = gradient(field)
        local = gradient_t(squares[0] * axial, squares[1] * around, squares[2] * radial)
        return local + mass_shift * mass * field

    def inner(one, two):
        return jnp.sum(one * two, axis=0, keepdims=True)

    spaces, images, dots = [], [], {}
    current = source
    for it in range(ITERS):
        spaces.append(smooth(current, beside, ends))
        local = apply(spaces[-1])
        image = around_sum(local)
        send(2 + it, image)
        if it == 0:
            head = inner(divergence, spaces[0])
        for j in range(it + 1):
            dots[j, it] = inner(local, spaces[j])
        if it < ITERS - 1:
            current, beside, ends = surrounded(2 + it, image)
            images.append(current)

    value = jnp.concatenate(
        [head]
        + [dots[i, j] for i in range(3) for j in range(i, 3)]
        + [jnp.zeros((1, LANES), jnp.float32)],
        axis=0,
    )
    started = []
    for stage, (stride, size) in enumerate(stages):
        digit = lax.rem(me // stride, size)
        gathered[stage, digit] = value
        for offset in range(1, size):
            copy = pltpu.make_async_remote_copy(
                src_ref=gathered.at[stage, digit],
                dst_ref=gathered.at[stage, digit],
                send_sem=gather_send_sem.at[stage, offset],
                recv_sem=gather_recv_sem.at[stage, offset],
                device_id=(peer(stage, offset),),
                device_id_type=MESH,
            )
            copy.start()
            started.append(copy)
        for copy in started[1 - size :]:
            copy.wait_recv()
        value = gathered[stage, 0]
        for slot in range(1, size):
            value = value + gathered[stage, slot]
    sums = jnp.sum(value, axis=1, keepdims=True)
    sums = [sums[i : i + 1] for i in range(7)]
    gram = {}
    for at, (i, j) in enumerate([(i, j) for i in range(3) for j in range(i, 3)]):
        gram[i, j] = gram[j, i] = sums[1 + at]
    heads = [sums[0], gram[0, 0], gram[0, 1]]
    taken = [None] * 3
    direction = [None] * 3
    result = [None] * 3
    previous = None
    for it in range(ITERS):
        z = [None] * 3
        z[0] = jnp.ones((1, 1), jnp.float32)
        for k in range(1, it + 1):
            z[k] = taken[k - 1]
        rho = heads[0]
        for k in range(1, it + 1):
            rho = rho + z[k] * heads[k]
        for i in range(it):
            row = gram[i, 0]
            for k in range(1, it + 1):
                row = row + z[k] * gram[i, k]
            rho = rho + taken[i] * row
        if it == 0:
            direction = [z[0], None, None]
        else:
            beta = rho / previous
            direction = [
                None if k > it else z[k] if direction[k] is None else z[k] + beta * direction[k]
                for k in range(3)
            ]
        bottom = None
        for i in range(it + 1):
            row = None
            for k in range(it + 1):
                term = direction[k] * gram[i, k]
                row = term if row is None else row + term
            bottom = direction[i] * row if bottom is None else bottom + direction[i] * row
        alpha = rho / bottom
        for k in range(it + 1):
            step = alpha * direction[k]
            result[k] = step if result[k] is None else result[k] + step
            taken[k] = -step if taken[k] is None else taken[k] - step
        previous = rho
    receive(ROUNDS - 1)
    images.append(axial_sum(image, inbox_far[ROUNDS - 1, 0], inbox_far[ROUNDS - 1, 1]))
    final = [spaces[0] * result[0], source]
    for k in range(3):
        final[1] = final[1] + images[k] * taken[k]
        if k:
            final[0] = final[0] + spaces[k] * result[k]

    for which, ref in enumerate((pressure_ref, residual_ref)):
        for j, tile in enumerate(tiles(final[which])):
            turned[which, pl.ds(2 * j * ES, ES)] = tile
            turned[which, pl.ds((2 * j + 1) * ES, ES)] = swap(tile)
        for p in range(ES):
            block = turned[which, pl.ds(p, NP, stride=ES), :]
            ref[:, p * 56 : (p + 1) * 56] = block[:, :56]

    for step in range(ROUNDS):
        for copy in copies(step):
            copy.wait_send()
    for copy in started:
        copy.wait_send()


def shards(count, velocity, conv_past, metric, jacobian, element_slot):
    weights, tables, _, _ = constants()
    stages = stages_of(count)
    block = jax.ShapeDtypeStruct((A0, A1 * A2), jnp.float32)
    whole = pl.BlockSpec(memory_space=pltpu.VMEM)
    slots = element_slot.reshape(1, ES)
    operands = [velocity, conv_past, metric, jacobian, slots]
    operands += [jnp.asarray(weights), jnp.asarray(tables)]
    return pl.pallas_call(
        functools.partial(kernel, count),
        out_shape=(block, block),
        in_specs=[pl.BlockSpec(memory_space=pltpu.HBM)] * len(operands),
        out_specs=(whole, whole),
        scratch_shapes=[pltpu.VMEM(x.shape, x.dtype) for x in operands]
        + [
            pltpu.SemaphoreType.DMA((len(operands) + 1,)),
            pltpu.VMEM((2, 6 * ES, LANES), jnp.float32),
            pltpu.VMEM((2, 6 * ES, LANES), jnp.float32),
            pltpu.VMEM((ROUNDS, 4 * ES, LANES), jnp.float32),
            pltpu.VMEM((ROUNDS, 2, 4 * ES, LANES), jnp.float32),
            pltpu.VMEM((ROUNDS, 2, ES, LANES), jnp.float32),
            pltpu.VMEM((len(stages), 8, 8, LANES), jnp.float32),
            pltpu.VMEM((2, NP * ES, LANES), jnp.float32),
            pltpu.SemaphoreType.DMA((ROUNDS, WAYS)),
            pltpu.SemaphoreType.DMA((ROUNDS, WAYS)),
            pltpu.SemaphoreType.DMA((len(stages), 8)),
            pltpu.SemaphoreType.DMA((len(stages), 8)),
        ],
        compiler_params=pltpu.CompilerParams(
            collective_id=0, has_side_effects=True, vmem_limit_bytes=56 * 1024 * 1024
        ),
    )(*operands)


def solution(mesh):
    return jax.shard_map(
        functools.partial(shards, mesh.shape["dom"]),
        mesh=mesh,
        in_specs=(
            P(None, None, "dom", None),
            P(None, None, "dom", None),
            P(None, "dom", None),
            P("dom", None),
            P("dom"),
        ),
        out_specs=(P("dom", None), P("dom", None)),
        check_vma=False,
    )
```

```python
import functools

import jax
import jax.numpy as jnp
import numpy as np
from jax import lax
from jax.experimental import pallas as pl
from jax.experimental.pallas import tpu as pltpu
from jax.sharding import PartitionSpec as P

NP = 8
NF = 12
ES = 16
ITERS = 3
A0 = 8
A1 = 112
A2 = 8
ROUNDS = 5
WAYS = 4
PEERS = 32
LANES = 128
MESH = pl.DeviceIdType.MESH

time_step = 0.25
viscosity = 0.05
mass_shift = 0.001


def legendre_pair(points, order):
    before = np.ones(points.shape)
    current = points * 1.0
    for level in range(2, order + 1):
        nextone = ((2 * level - 1) * points * current - (level - 1) * before) / level
        before = current
        current = nextone
    return (current, before)


def jacobi_eigen(matrix):
    size = matrix.shape[0]
    work = matrix * 1.0
    vectors = np.eye(size)
    for sweep in range(30):
        for first in range(size - 1):
            for second in range(first + 1, size):
                off = float(work[first, second])
                if abs(off) > 1e-300:
                    tau = (float(work[second, second]) - float(work[first, first])) / (2.0 * off)
                    if tau >= 0.0:
                        tangent = 1.0 / (tau + (1.0 + tau * tau) ** 0.5)
                    else:
                        tangent = -1.0 / (-tau + (1.0 + tau * tau) ** 0.5)
                    cosine = 1.0 / (1.0 + tangent * tangent) ** 0.5
                    sine = tangent * cosine
                    rotation = np.eye(size)
                    rotation[first, first] = cosine
                    rotation[second, second] = cosine
                    rotation[first, second] = sine
                    rotation[second, first] = -sine
                    work = rotation.T @ work @ rotation
                    vectors = vectors @ rotation
    diagonal_index = np.arange(size)
    return (work[diagonal_index, diagonal_index], vectors)


def build_tables(points_edge, points_fine):
    degree = points_edge - 1
    points = -np.cos(np.pi * np.arange(points_edge) / degree)
    for sweep in range(100):
        top, below = legendre_pair(points, degree)
        points = points - (points * top - below) / (points_edge * top)
    top, below = legendre_pair(points, degree)
    weight_gll = 2.0 / (degree * points_edge * top**2)
    spacing = points[:, None] - points[None, :] + np.eye(points_edge)
    barycentric = 1.0 / np.prod(spacing, axis=1)
    derivative = barycentric[None, :] / barycentric[:, None] / spacing
    derivative = derivative * (1.0 - np.eye(points_edge))
    derivative = derivative - np.eye(points_edge) * derivative.sum(axis=1)[:, None]
    fine_points = np.cos(np.pi * (np.arange(points_fine) + 0.75) / (points_fine + 0.5))
    for sweep in range(100):
        top, below = legendre_pair(fine_points, points_fine)
        slope = points_fine * (fine_points * top - below) / (fine_points * fine_points - 1.0)
        fine_points = fine_points - top / slope
    top, below = legendre_pair(fine_points, points_fine)
    slope = points_fine * (fine_points * top - below) / (fine_points * fine_points - 1.0)
    fine_weight = 2.0 / ((1.0 - fine_points * fine_points) * slope * slope)
    fine_points = fine_points[::-1]
    fine_weight = fine_weight[::-1]
    interpolate = np.ones((points_fine, points_edge))
    for column in range(points_edge):
        for other in range(points_edge):
            if other != column:
                interpolate[:, column] = (
                    interpolate[:, column]
                    * (fine_points - points[other])
                    / (points[column] - points[other])
                )
    stiffness = derivative.T @ (weight_gll[:, None] * derivative)
    extent = 3 * degree + 1
    joined_stiff = np.zeros((extent, extent))
    joined_mass = np.zeros(extent)
    for segment in range(3):
        offset = segment * degree
        joined_stiff[offset : offset + points_edge, offset : offset + points_edge] += stiffness
        joined_mass[offset : offset + points_edge] += weight_gll
    low = degree - 1
    high = 2 * degree + 2
    root_mass = np.sqrt(joined_mass[low:high])
    scaled = joined_stiff[low:high, low:high] / root_mass[:, None] / root_mass[None, :]
    scaled = 0.5 * (scaled + scaled.T)
    eigen_values, eigen_vectors = jacobi_eigen(scaled)
    solve_mat = eigen_vectors / root_mass[:, None]
    breadth = high - low
    identity = np.eye(points_edge)
    operator_tables = {
        "derivative": derivative,
        "dpair": np.concatenate(
            [np.kron(derivative, identity).T, np.kron(identity, derivative).T], axis=1
        ),
        "interpolate": interpolate,
        "ipair": np.kron(interpolate, interpolate).T,
        "mass_three": (
            weight_gll[:, None, None] * weight_gll[None, :, None] * weight_gll[None, None, :]
        ).reshape(points_edge, points_edge * points_edge),
        "fine_three": (
            fine_weight[:, None, None] * fine_weight[None, :, None] * fine_weight[None, None, :]
        ).reshape(points_fine, points_fine * points_fine),
        "solve_mat": solve_mat,
        "solve_pair": np.kron(solve_mat, solve_mat),
        "eigen_axial": eigen_values,
        "eigen_around": np.repeat(eigen_values, breadth),
        "eigen_radial": np.tile(eigen_values, breadth),
    }
    operator_tables["weight"] = weight_gll
    operator_tables["fine_weight"] = fine_weight
    return operator_tables


def split_rows(matrix):
    exact = np.asarray(matrix, np.float32)
    high = exact.astype(jnp.bfloat16)
    low = (exact - high.astype(np.float32)).astype(jnp.bfloat16)
    columns = range(0, exact.shape[1], LANES)
    return np.concatenate([part[:, c : c + LANES] for c in columns for part in (high, low)])


def halves(matrix):
    rows, columns = matrix.shape
    table = np.zeros((rows // 2, columns // 2, 2, LANES))
    for out in range(rows // 2):
        for into in range(columns // 2):
            table[out, into, 0, :64] = matrix[2 * out, 2 * into]
            table[out, into, 0, 64:] = matrix[2 * out + 1, 2 * into + 1]
            table[out, into, 1, :64] = matrix[2 * out, 2 * into + 1]
            table[out, into, 1, 64:] = matrix[2 * out + 1, 2 * into]
    return np.asarray(table.reshape(-1, LANES), np.float32)


def twice(block, stride):
    rows, columns = block.shape
    result = np.zeros((2 * rows, 2 * stride))
    result[:rows, :columns] = block
    result[rows:, stride : stride + columns] = block
    return result


def pad_columns(matrix, total):
    return np.pad(matrix, ((0, 0), (0, total - matrix.shape[1])))


def by_tile(table):
    return np.asarray(np.repeat(table.reshape(-1, LANES), ES, axis=0), np.float32)


@functools.cache
def constants():
    t = build_tables(NP, NF)
    d, itp, s = t["derivative"], t["interpolate"], t["solve_mat"]
    eye = np.eye(NP)
    pair = np.concatenate(
        [twice(np.kron(d, eye).T, 64), twice(np.kron(eye, d).T, 64)], axis=1
    )
    fine = pad_columns(twice(np.kron(itp, itp).T, 144), 384)
    slope = itp @ d
    fine_slope = np.concatenate(
        [
            pad_columns(twice(np.kron(slope, itp).T, 144), 384),
            pad_columns(twice(np.kron(itp, slope).T, 144), 384),
        ],
        axis=1,
    )
    inner = s[1:9]
    ahead = np.zeros((2 * LANES, 2 * LANES))
    back = np.zeros((2 * LANES, 2 * LANES))
    for h in range(2):
        out = slice(h * LANES, h * LANES + 100)

        def lanes(row):
            return slice(h * 64 + row * 8, h * 64 + row * 8 + 8)

        def beside(row):
            return slice(LANES + h * 64 + row * 8, LANES + h * 64 + row * 8 + 8)

        for row in range(NP):
            ahead[lanes(row), out] = np.kron(s[row + 1 : row + 2], inner)
            back[lanes(row), out] = np.kron(s[row + 1 : row + 2], inner)
        ahead[beside(6), out] = np.kron(s[0:1], inner)
        ahead[beside(1), out] = np.kron(s[9:10], inner)
        back[beside(0), out] = np.kron(s[8:9], inner)
        back[beside(1), out] = np.kron(s[9:10], inner)
        back[beside(7), out] = np.kron(s[1:2], inner)
        back[beside(6), out] = np.kron(s[0:1], inner)
    wf = t["fine_weight"]
    wf2 = (wf[:, None] * wf[None, :]).reshape(-1)
    fine_mass = np.zeros((6, 384))
    for j in range(6):
        fine_mass[j, :144] = wf[2 * j] * wf2
        fine_mass[j, 144:288] = wf[2 * j + 1] * wf2
    eigen = np.zeros((2, LANES))
    eigen[0, :100] = t["eigen_around"]
    eigen[1, :100] = t["eigen_radial"]
    nodes = by_tile(t["mass_three"])
    weights = np.concatenate(
        [split_rows(m) for m in (pair, pair.T, fine, fine_slope, fine.T, ahead, back.T)]
    )
    along = np.concatenate([halves(d), halves(d.T), halves(itp), halves(slope), halves(itp.T)])
    fine_mass = np.repeat(fine_mass, ES, axis=0)
    tables = np.concatenate(
        [along, nodes]
        + [fine_mass[:, c : c + LANES] for c in range(0, 384, LANES)]
        + [np.pad(eigen, ((0, 6), (0, 0)))]
    )
    return (
        weights,
        np.asarray(tables, np.float32),
        np.asarray(s, np.float32),
        np.asarray(t["eigen_axial"], np.float32),
    )


PAIR = (0, 128, 256)
PAIR_T = (512, 256, 128)
FINE = (1024, 128, 384)
SLOPE = (1792, 128, 768)
FINE_T = (3328, 384, 128)
AHEAD = (4096, 256, 256)
BACK = (5120, 256, 256)
TABLE_NODES, TABLE_FINE, TABLE_EIGEN = 208, 272, 560
COEF_D, COEF_DT, COEF_I, COEF_S, COEF_IT = 0, 32, 64, 112, 160


OPERANDS = 7


def stages_of(count):
    stages = []
    stride = 1
    while stride < count:
        size = min(PEERS, count // stride)
        while (count // stride) % size:
            size -= 1
        stages.append((stride, size))
        stride *= size
    return stages


def kernel(
    count,
    *refs,
):
    operands, refs = refs[:OPERANDS], refs[OPERANDS:]
    pressure_ref, residual_ref = refs[:2]
    held, refs = refs[2 : 2 + OPERANDS], refs[2 + OPERANDS :]
    (
        load_sem,
        first_out,
        first_in,
        outbox,
        inbox,
        inbox_far,
        gathered,
        turned,
        basis,
        send_sem,
        recv_sem,
        gather_send_sem,
        gather_recv_sem,
    ) = refs
    split = [(0, None)] * 5 + [(0, AHEAD[0]), (AHEAD[0], None), (0, None)]
    loads = []
    for i, (at, end) in enumerate(split):
        which = min(i, 5) if i < 7 else 6
        rows = slice(None) if i < 5 else pl.ds(at, (end or operands[which].shape[0]) - at)
        loads.append(
            pltpu.make_async_copy(
                operands[which].at[rows], held[which].at[rows], load_sem.at[i]
            )
        )
    for i in (3, 2, 0, 7, 5, 1, 4, 6):
        loads[i].start()
    velocity, past, metric, jacobian, slots, weights, tables = held

    _, _, solve, eigen_axial = constants()
    me = lax.axis_index("dom")
    left = lax.rem(me + count - 1, count)
    right = lax.rem(me + 1, count)
    far_left = lax.rem(me + count - 2, count)
    far_right = lax.rem(me + 2, count)
    stages = stages_of(count)

    def peer(stage, offset):
        stride, size = stages[stage]
        digit = lax.rem(me // stride, size)
        other = lax.rem(digit + offset, size)
        return me + (other - digit) * stride

    barrier = pltpu.get_barrier_semaphore()
    greeted = [left, right, far_left, far_right] + [
        peer(stage, offset)
        for stage in range(len(stages))
        for offset in range(1, stages[stage][1])
    ]
    for other in greeted:
        pl.semaphore_signal(barrier, inc=1, device_id=(other,), device_id_type=MESH)

    lane = lax.broadcasted_iota(jnp.int32, (ES, LANES), 1)
    low = lane < 64
    node_s = lax.rem(lane, 64) // 8

    def tiles(field):
        return [field[i * ES : (i + 1) * ES] for i in range(field.shape[0] // ES)]

    def stack(parts):
        return jnp.concatenate(parts, axis=0)

    def mm(x, w):
        high = x.astype(jnp.bfloat16)
        rest = (x - high.astype(jnp.float32)).astype(jnp.bfloat16)
        at, depth, width = w
        columns = []
        for c in range(width // LANES):
            top = weights[at + 2 * c * depth : at + (2 * c + 1) * depth]
            bottom = weights[at + (2 * c + 1) * depth : at + (2 * c + 2) * depth]
            columns.append(jnp.concatenate([top, top, bottom], axis=0))
        return jnp.dot(
            jnp.concatenate([high, rest, high], axis=1),
            jnp.concatenate(columns, axis=1),
            preferred_element_type=jnp.float32,
        )

    def swap(tile):
        return pltpu.roll(tile, 64, 1)

    def along(field, base, total):
        parts = tiles(field)
        swapped = [swap(part) for part in parts]
        results = []
        for out in range(total):
            acc = None
            for into in range(len(parts)):
                at = base + 2 * (out * len(parts) + into)
                term = tables[at : at + 1] * parts[into] + tables[at + 1 : at + 2] * swapped[into]
                acc = term if acc is None else acc + term
            results.append(acc)
        return stack(results)

    def gradient(field):
        paired = mm(field, PAIR)
        return along(field, COEF_D, 4), paired[:, :LANES], paired[:, LANES:]

    def gradient_t(axial, around, radial):
        paired = mm(jnp.concatenate([around, radial], axis=1), PAIR_T)
        return paired + along(axial, COEF_DT, 4)

    def before(tile):
        return pltpu.roll(tile, 1, 0)

    def after(tile):
        return pltpu.roll(tile, ES - 1, 0)

    def around_sum(field):
        results = []
        for tile in tiles(field):
            first = before(pltpu.roll(tile, 72, 1))
            last = after(pltpu.roll(tile, 56, 1))
            results.append(
                tile + jnp.where(node_s == 0, first, jnp.where(node_s == 7, last, 0.0))
            )
        return stack(results)

    def copies(step):
        if step == 0:
            plan = [(first_out.at[0], first_in.at[1], left), (first_out.at[1], first_in.at[0], right)]
        elif step < ROUNDS - 1:
            plan = [
                (outbox.at[step, pl.ds(0, ES)], inbox_far.at[step, 1], far_left),
                (outbox.at[step, pl.ds(3 * ES, ES)], inbox_far.at[step, 0], far_right),
                (outbox.at[step], inbox.at[step, 1], left),
                (outbox.at[step], inbox.at[step, 0], right),
            ]
        else:
            plan = [
                (outbox.at[step, pl.ds(0, ES)], inbox_far.at[step, 1], left),
                (outbox.at[step, pl.ds(3 * ES, ES)], inbox_far.at[step, 0], right),
            ]
        return [
            pltpu.make_async_remote_copy(
                src_ref=source,
                dst_ref=target,
                send_sem=send_sem.at[step, way],
                recv_sem=recv_sem.at[step, way],
                device_id=(other,),
                device_id_type=MESH,
            )
            for way, (source, target, other) in enumerate(plan)
        ]

    def send(step, field):
        outbox[step] = field
        for copy in copies(step):
            copy.start()

    def receive(step):
        for copy in copies(step):
            copy.wait_recv()

    def axial_sum(field, before_it, after_it):
        parts = tiles(field)
        return stack(
            [
                parts[0] + jnp.where(low, swap(before_it), 0.0),
                parts[1],
                parts[2],
                parts[3] + jnp.where(low, 0.0, swap(after_it)),
            ]
        )

    def surrounded(step, field):
        receive(step)
        beside = [inbox[step, 0], inbox[step, 1]]
        ends = [inbox_far[step, 0], inbox_far[step, 1]]
        own = axial_sum(field, beside[0][3 * ES :], beside[1][:ES])
        return own, beside, ends

    def element_field(ref, *index):
        return stack([ref[index + (slice(None), pl.ds(j * LANES, LANES))] for j in range(4)])

    loads[7].wait()
    loads[3].wait()
    weight3 = tables[TABLE_NODES:TABLE_FINE]
    fine_mass = jnp.concatenate(
        [tables[TABLE_FINE + 96 * c : TABLE_FINE + 96 * (c + 1)] for c in range(3)], axis=1
    )
    eigen = tables[TABLE_EIGEN:]
    jac = element_field(jacobian)
    mass = jac * weight3
    coarse = [along(jac, COEF_I, 6)]
    loads[2].wait()
    metrics = [element_field(metric, d) for d in range(3)]
    squares = [mass * m * m for m in metrics]
    loads[0].wait()
    newest = [element_field(velocity, 0, i) for i in range(3)]
    coarse += [along(newest[d] * metrics[d], COEF_I, 6) for d in range(3)]
    coarse += [along(newest[i], COEF_S, 6) for i in range(3)]
    loads[5].wait()
    fine = mm(stack(coarse), FINE)
    fine = [fine[i * 96 : (i + 1) * 96] for i in range(7)]
    crossed = mm(stack([along(newest[i], COEF_I, 6) for i in range(3)]), SLOPE)
    fine_jac = fine[0] * fine_mass
    products = []
    for i in range(3):
        rows = slice(i * 96, (i + 1) * 96)
        products.append(
            fine_jac
            * (
                fine[1] * fine[4 + i]
                + fine[2] * crossed[rows, :384]
                + fine[3] * crossed[rows, 384:]
            )
        )
    advected = mm(stack(products), FINE_T)
    guessed = [
        3.0 * newest[i] - 3.0 * element_field(velocity, 1, i) + element_field(velocity, 2, i)
        for i in range(3)
    ]
    paired = mm(stack(guessed), PAIR)
    slopes = jnp.concatenate(
        [
            stack([squares[1] * paired[i * 64 : (i + 1) * 64, :LANES] for i in range(3)]),
            stack([squares[2] * paired[i * 64 : (i + 1) * 64, LANES:] for i in range(3)]),
        ],
        axis=1,
    )
    paired_t = mm(slopes, PAIR_T)
    forcing = []
    loads[1].wait()
    loads[4].wait()
    for i in range(3):
        convect = along(advected[i * 96 : (i + 1) * 96], COEF_IT, 4)
        stiff = paired_t[i * 64 : (i + 1) * 64] + along(
            squares[0] * along(guessed[i], COEF_D, 4), COEF_DT, 4
        )
        history = (
            3.0 * newest[i]
            - 1.5 * element_field(velocity, 1, i)
            + element_field(velocity, 2, i) / 3.0
        )
        extrap = (
            3.0 * convect - 3.0 * element_field(past, 0, i) + element_field(past, 1, i)
        )
        helmholtz = viscosity * stiff + 11.0 / (6.0 * time_step) * mass * guessed[i]
        forcing.append(mass * history / time_step - extrap - helmholtz)

    fields = forcing + [mass] + metrics
    wide = jnp.concatenate([tile for field in fields for tile in tiles(field)], axis=1)
    first = wide.astype(jnp.bfloat16)
    rest = wide - first.astype(jnp.float32)
    second = rest.astype(jnp.bfloat16)
    third = (rest - second.astype(jnp.float32)).astype(jnp.bfloat16)
    position = lax.broadcasted_iota(jnp.int32, (ES, ES), 0)
    chosen = jnp.where(slots[...] == position, 1.0, 0.0)
    chosen = jnp.concatenate([chosen, chosen, chosen], axis=1).astype(jnp.bfloat16)
    placed = jnp.dot(chosen, stack([first, second, third]), preferred_element_type=jnp.float32)
    fields = [
        stack([placed[:, (4 * f + j) * LANES : (4 * f + j + 1) * LANES] for j in range(4)])
        for f in range(7)
    ]
    forcing, mass, metrics = fields[:3], fields[3], fields[4:]
    lumps = [mass * m for m in metrics]
    squares = [lumps[d] * metrics[d] for d in range(3)]

    def total(field):
        parts = tiles(field)
        return jnp.sum(parts[0] + parts[1] + parts[2] + parts[3], axis=1, keepdims=True) / 8.0

    flat = (
        total(squares[1]) * eigen[0:1]
        + total(squares[2]) * eigen[1:2]
        + mass_shift * total(mass)
    )
    steep = jnp.broadcast_to(total(squares[0]), (ES, LANES))

    around = [around_sum(f) for f in forcing + [mass]]
    first_out[0] = stack([f[:ES] for f in around] + [flat, steep])
    first_out[1] = stack([f[3 * ES :] for f in around] + [flat, steep])
    pl.semaphore_wait(barrier, len(greeted))
    for copy in copies(0):
        copy.start()
    receive(0)
    lefts, rights = tiles(first_in[0]), tiles(first_in[1])
    summed = [axial_sum(around[f], lefts[f], rights[f]) for f in range(4)]
    accel = [lumps[d] * (summed[d] / summed[3]) for d in range(3)]
    divergence = gradient_t(accel[0], accel[1], accel[2])
    source = around_sum(divergence)
    send(1, source)
    loads[6].wait()
    flats = stack([lefts[4], flat, rights[4]])
    steeps = stack([lefts[5], steep, rights[5]])
    inverse = [1.0 / (steeps * float(eigen_axial[k]) + flats) for k in range(10)]
    source, beside, ends = surrounded(1, source)

    def combine(weight, parts):
        acc = parts[0] * float(weight[0])
        for one, part in zip(weight[1:], parts[1:]):
            acc = acc + part * float(one)
        return acc

    def smooth(own, beside, ends):
        lower, upper = tiles(beside[0]), tiles(beside[1])
        lower[0] = lower[0] + jnp.where(low, swap(ends[0]), 0.0)
        upper[3] = upper[3] + jnp.where(low, 0.0, swap(ends[1]))
        parts = [jnp.where(low, ends[0], ends[1])] + lower + upper + tiles(own)
        sides = [
            jnp.where(node_s == 6, before(p), jnp.where(node_s == 1, after(p), 0.0))
            for p in parts
        ]
        modes = tiles(mm(jnp.concatenate([stack(parts), stack(sides)], axis=1), AHEAD))
        firsts = [-7, -5, -3, -1, 7, 9, 11, 13, 0, 2, 4, 6]
        grid = {-8: modes[0][:, :LANES], 15: modes[0][:, LANES:]}
        for row, mode in zip(firsts, modes[1:]):
            grid[row], grid[row + 1] = mode[:, :LANES], mode[:, LANES:]
        order = [stack([grid[a - 7], grid[a], grid[a + 7]]) for a in range(-1, 9)]
        spectra = [combine(solve[:, k], order) * inverse[k] for k in range(10)]
        slabs = [[spectrum[b * ES : (b + 1) * ES] for spectrum in spectra] for b in range(3)]
        rows = [combine(solve[a + 1], slabs[1]) for a in range(NP)]
        rows[0] = rows[0] + combine(solve[8], slabs[0])
        rows[1] = rows[1] + combine(solve[9], slabs[0])
        rows[6] = rows[6] + combine(solve[0], slabs[2])
        rows[7] = rows[7] + combine(solve[1], slabs[2])
        given = mm(jnp.concatenate([stack(rows[0::2]), stack(rows[1::2])], axis=1), BACK)
        return stack(
            [
                o + jnp.where(node_s <= 1, before(n), jnp.where(node_s >= 6, after(n), 0.0))
                for o, n in zip(tiles(given[:, :LANES]), tiles(given[:, LANES:]))
            ]
        )

    def apply(field):
        axial, around, radial = gradient(field)
        local = gradient_t(squares[0] * axial, squares[1] * around, squares[2] * radial)
        return local + mass_shift * mass * field

    def inner(one, two):
        return jnp.sum(one * two, axis=0, keepdims=True)

    def turn(which, field):
        for j, tile in enumerate(tiles(field)):
            turned[which, pl.ds(2 * j * ES, ES)] = tile
            turned[which, pl.ds((2 * j + 1) * ES, ES)] = swap(tile)
        for p in range(ES):
            block = turned[which, pl.ds(p, NP, stride=ES), :]
            basis[which, :, p * 56 : (p + 1) * 56] = block[:, :56]

    spaces, images, dots = [], [], {}
    current = source
    for it in range(ITERS):
        spaces.append(smooth(current, beside, ends))
        local = apply(spaces[-1])
        image = around_sum(local)
        send(2 + it, image)
        if it == 0:
            head = inner(divergence, spaces[0])
        for j in range(it + 1):
            dots[j, it] = inner(local, spaces[j])
        if it < ITERS - 1:
            turn(2 * it, spaces[it])
            if it == 0:
                turn(6, current)
            else:
                turn(2 * it - 1, current)
            current, beside, ends = surrounded(2 + it, image)
            images.append(current)

    value = jnp.concatenate(
        [head]
        + [dots[i, j] for i in range(3) for j in range(i, 3)]
        + [jnp.zeros((1, LANES), jnp.float32)],
        axis=0,
    )
    started = []
    for stage, (stride, size) in enumerate(stages):
        digit = lax.rem(me // stride, size)
        gathered[stage, digit] = value
        for offset in range(1, size):
            copy = pltpu.make_async_remote_copy(
                src_ref=gathered.at[stage, digit],
                dst_ref=gathered.at[stage, digit],
                send_sem=gather_send_sem.at[stage, offset],
                recv_sem=gather_recv_sem.at[stage, offset],
                device_id=(peer(stage, offset),),
                device_id_type=MESH,
            )
            copy.start()
            started.append(copy)
        if stage == 0:
            turn(4, spaces[2])
            turn(3, images[1])
            receive(ROUNDS - 1)
            ends = [inbox_far[ROUNDS - 1, 0], inbox_far[ROUNDS - 1, 1]]
            turn(5, axial_sum(image, ends[0], ends[1]))
        for copy in started[1 - size :]:
            copy.wait_recv()
        value = gathered[stage, 0]
        for slot in range(1, size):
            value = value + gathered[stage, slot]
    sums = jnp.sum(value, axis=1, keepdims=True)
    sums = [sums[i : i + 1] for i in range(7)]
    gram = {}
    for at, (i, j) in enumerate([(i, j) for i in range(3) for j in range(i, 3)]):
        gram[i, j] = gram[j, i] = sums[1 + at]
    heads = [sums[0], gram[0, 0], gram[0, 1]]
    taken = [None] * 3
    direction = [None] * 3
    result = [None] * 3
    previous = None
    for it in range(ITERS):
        z = [None] * 3
        z[0] = jnp.ones((1, 1), jnp.float32)
        for k in range(1, it + 1):
            z[k] = taken[k - 1]
        rho = heads[0]
        for k in range(1, it + 1):
            rho = rho + z[k] * heads[k]
        for i in range(it):
            row = gram[i, 0]
            for k in range(1, it + 1):
                row = row + z[k] * gram[i, k]
            rho = rho + taken[i] * row
        if it == 0:
            direction = [z[0], None, None]
        else:
            beta = rho / previous
            direction = [
                None if k > it else z[k] if direction[k] is None else z[k] + beta * direction[k]
                for k in range(3)
            ]
        bottom = None
        for i in range(it + 1):
            row = None
            for k in range(it + 1):
                term = direction[k] * gram[i, k]
                row = term if row is None else row + term
            bottom = direction[i] * row if bottom is None else bottom + direction[i] * row
        alpha = rho / bottom
        for k in range(it + 1):
            step = alpha * direction[k]
            result[k] = step if result[k] is None else result[k] + step
            taken[k] = -step if taken[k] is None else taken[k] - step
        previous = rho
    pressure_ref[...] = sum(basis[2 * k] * result[k] for k in range(3))
    residual_ref[...] = basis[6] + sum(basis[2 * k + 1] * taken[k] for k in range(3))

    for step in range(ROUNDS):
        for copy in copies(step):
            copy.wait_send()
    for copy in started:
        copy.wait_send()


def shards(count, velocity, conv_past, metric, jacobian, element_slot):
    weights, tables, _, _ = constants()
    stages = stages_of(count)
    block = jax.ShapeDtypeStruct((A0, A1 * A2), jnp.float32)
    whole = pl.BlockSpec(memory_space=pltpu.VMEM)
    slots = element_slot.reshape(1, ES)
    operands = [velocity, conv_past, metric, jacobian, slots]
    operands += [jnp.asarray(weights), jnp.asarray(tables)]
    return pl.pallas_call(
        functools.partial(kernel, count),
        out_shape=(block, block),
        in_specs=[pl.BlockSpec(memory_space=pltpu.HBM)] * len(operands),
        out_specs=(whole, whole),
        scratch_shapes=[pltpu.VMEM(x.shape, x.dtype) for x in operands]
        + [
            pltpu.SemaphoreType.DMA((len(operands) + 1,)),
            pltpu.VMEM((2, 6 * ES, LANES), jnp.float32),
            pltpu.VMEM((2, 6 * ES, LANES), jnp.float32),
            pltpu.VMEM((ROUNDS, 4 * ES, LANES), jnp.float32),
            pltpu.VMEM((ROUNDS, 2, 4 * ES, LANES), jnp.float32),
            pltpu.VMEM((ROUNDS, 2, ES, LANES), jnp.float32),
            pltpu.VMEM((len(stages), PEERS, 8, LANES), jnp.float32),
            pltpu.VMEM((7, NP * ES, LANES), jnp.float32),
            pltpu.VMEM((7, A0, A1 * A2), jnp.float32),
            pltpu.SemaphoreType.DMA((ROUNDS, WAYS)),
            pltpu.SemaphoreType.DMA((ROUNDS, WAYS)),
            pltpu.SemaphoreType.DMA((len(stages), PEERS)),
            pltpu.SemaphoreType.DMA((len(stages), PEERS)),
        ],
        compiler_params=pltpu.CompilerParams(
            collective_id=0, has_side_effects=True, vmem_limit_bytes=55168 * 1024
        ),
    )(*operands)


def solution(mesh):
    return jax.shard_map(
        functools.partial(shards, mesh.shape["dom"]),
        mesh=mesh,
        in_specs=(
            P(None, None, "dom", None),
            P(None, None, "dom", None),
            P(None, "dom", None),
            P("dom", None),
            P("dom"),
        ),
        out_specs=(P("dom", None), P("dom", None)),
        check_vma=False,
    )
```

```python
import functools

import jax
import jax.numpy as jnp
import numpy as np
from jax import lax
from jax.experimental import pallas as pl
from jax.experimental.pallas import tpu as pltpu
from jax.sharding import PartitionSpec as P

NP = 8
NF = 12
ES = 16
ITERS = 3
A0 = 8
A1 = 112
A2 = 8
ROUNDS = 5
WAYS = 4
PEERS = 32
LANES = 128
MESH = pl.DeviceIdType.MESH

time_step = 0.25
viscosity = 0.05
mass_shift = 0.001


def legendre_pair(points, order):
    before = np.ones(points.shape)
    current = points * 1.0
    for level in range(2, order + 1):
        nextone = ((2 * level - 1) * points * current - (level - 1) * before) / level
        before = current
        current = nextone
    return (current, before)


def jacobi_eigen(matrix):
    size = matrix.shape[0]
    work = matrix * 1.0
    vectors = np.eye(size)
    for sweep in range(30):
        for first in range(size - 1):
            for second in range(first + 1, size):
                off = float(work[first, second])
                if abs(off) > 1e-300:
                    tau = (float(work[second, second]) - float(work[first, first])) / (2.0 * off)
                    if tau >= 0.0:
                        tangent = 1.0 / (tau + (1.0 + tau * tau) ** 0.5)
                    else:
                        tangent = -1.0 / (-tau + (1.0 + tau * tau) ** 0.5)
                    cosine = 1.0 / (1.0 + tangent * tangent) ** 0.5
                    sine = tangent * cosine
                    rotation = np.eye(size)
                    rotation[first, first] = cosine
                    rotation[second, second] = cosine
                    rotation[first, second] = sine
                    rotation[second, first] = -sine
                    work = rotation.T @ work @ rotation
                    vectors = vectors @ rotation
    diagonal_index = np.arange(size)
    return (work[diagonal_index, diagonal_index], vectors)


def build_tables(points_edge, points_fine):
    degree = points_edge - 1
    points = -np.cos(np.pi * np.arange(points_edge) / degree)
    for sweep in range(100):
        top, below = legendre_pair(points, degree)
        points = points - (points * top - below) / (points_edge * top)
    top, below = legendre_pair(points, degree)
    weight_gll = 2.0 / (degree * points_edge * top**2)
    spacing = points[:, None] - points[None, :] + np.eye(points_edge)
    barycentric = 1.0 / np.prod(spacing, axis=1)
    derivative = barycentric[None, :] / barycentric[:, None] / spacing
    derivative = derivative * (1.0 - np.eye(points_edge))
    derivative = derivative - np.eye(points_edge) * derivative.sum(axis=1)[:, None]
    fine_points = np.cos(np.pi * (np.arange(points_fine) + 0.75) / (points_fine + 0.5))
    for sweep in range(100):
        top, below = legendre_pair(fine_points, points_fine)
        slope = points_fine * (fine_points * top - below) / (fine_points * fine_points - 1.0)
        fine_points = fine_points - top / slope
    top, below = legendre_pair(fine_points, points_fine)
    slope = points_fine * (fine_points * top - below) / (fine_points * fine_points - 1.0)
    fine_weight = 2.0 / ((1.0 - fine_points * fine_points) * slope * slope)
    fine_points = fine_points[::-1]
    fine_weight = fine_weight[::-1]
    interpolate = np.ones((points_fine, points_edge))
    for column in range(points_edge):
        for other in range(points_edge):
            if other != column:
                interpolate[:, column] = (
                    interpolate[:, column]
                    * (fine_points - points[other])
                    / (points[column] - points[other])
                )
    stiffness = derivative.T @ (weight_gll[:, None] * derivative)
    extent = 3 * degree + 1
    joined_stiff = np.zeros((extent, extent))
    joined_mass = np.zeros(extent)
    for segment in range(3):
        offset = segment * degree
        joined_stiff[offset : offset + points_edge, offset : offset + points_edge] += stiffness
        joined_mass[offset : offset + points_edge] += weight_gll
    low = degree - 1
    high = 2 * degree + 2
    root_mass = np.sqrt(joined_mass[low:high])
    scaled = joined_stiff[low:high, low:high] / root_mass[:, None] / root_mass[None, :]
    scaled = 0.5 * (scaled + scaled.T)
    eigen_values, eigen_vectors = jacobi_eigen(scaled)
    solve_mat = eigen_vectors / root_mass[:, None]
    breadth = high - low
    identity = np.eye(points_edge)
    operator_tables = {
        "derivative": derivative,
        "dpair": np.concatenate(
            [np.kron(derivative, identity).T, np.kron(identity, derivative).T], axis=1
        ),
        "interpolate": interpolate,
        "ipair": np.kron(interpolate, interpolate).T,
        "mass_three": (
            weight_gll[:, None, None] * weight_gll[None, :, None] * weight_gll[None, None, :]
        ).reshape(points_edge, points_edge * points_edge),
        "fine_three": (
            fine_weight[:, None, None] * fine_weight[None, :, None] * fine_weight[None, None, :]
        ).reshape(points_fine, points_fine * points_fine),
        "solve_mat": solve_mat,
        "solve_pair": np.kron(solve_mat, solve_mat),
        "eigen_axial": eigen_values,
        "eigen_around": np.repeat(eigen_values, breadth),
        "eigen_radial": np.tile(eigen_values, breadth),
    }
    operator_tables["weight"] = weight_gll
    operator_tables["fine_weight"] = fine_weight
    return operator_tables


def split_rows(matrix):
    exact = np.asarray(matrix, np.float32)
    high = exact.astype(jnp.bfloat16)
    low = (exact - high.astype(np.float32)).astype(jnp.bfloat16)
    columns = range(0, exact.shape[1], LANES)
    return np.concatenate([part[:, c : c + LANES] for c in columns for part in (high, low)])


def halves(matrix):
    rows, columns = matrix.shape
    table = np.zeros((rows // 2, columns // 2, 2, LANES))
    for out in range(rows // 2):
        for into in range(columns // 2):
            table[out, into, 0, :64] = matrix[2 * out, 2 * into]
            table[out, into, 0, 64:] = matrix[2 * out + 1, 2 * into + 1]
            table[out, into, 1, :64] = matrix[2 * out, 2 * into + 1]
            table[out, into, 1, 64:] = matrix[2 * out + 1, 2 * into]
    return np.asarray(table.reshape(-1, LANES), np.float32)


def twice(block, stride):
    rows, columns = block.shape
    result = np.zeros((2 * rows, 2 * stride))
    result[:rows, :columns] = block
    result[rows:, stride : stride + columns] = block
    return result


def pad_columns(matrix, total):
    return np.pad(matrix, ((0, 0), (0, total - matrix.shape[1])))


def by_tile(table):
    return np.asarray(np.repeat(table.reshape(-1, LANES), ES, axis=0), np.float32)


@functools.cache
def constants():
    t = build_tables(NP, NF)
    d, itp, s = t["derivative"], t["interpolate"], t["solve_mat"]
    eye = np.eye(NP)
    pair = np.concatenate(
        [twice(np.kron(d, eye).T, 64), twice(np.kron(eye, d).T, 64)], axis=1
    )
    fine = pad_columns(twice(np.kron(itp, itp).T, 144), 384)
    slope = itp @ d
    fine_slope = np.concatenate(
        [
            pad_columns(twice(np.kron(slope, itp).T, 144), 384),
            pad_columns(twice(np.kron(itp, slope).T, 144), 384),
        ],
        axis=1,
    )
    inner = s[1:9]
    ahead = np.zeros((2 * LANES, 2 * LANES))
    back = np.zeros((2 * LANES, 2 * LANES))
    for h in range(2):
        out = slice(h * LANES, h * LANES + 100)

        def lanes(row):
            return slice(h * 64 + row * 8, h * 64 + row * 8 + 8)

        def beside(row):
            return slice(LANES + h * 64 + row * 8, LANES + h * 64 + row * 8 + 8)

        for row in range(NP):
            ahead[lanes(row), out] = np.kron(s[row + 1 : row + 2], inner)
            back[lanes(row), out] = np.kron(s[row + 1 : row + 2], inner)
        ahead[beside(6), out] = np.kron(s[0:1], inner)
        ahead[beside(1), out] = np.kron(s[9:10], inner)
        back[beside(0), out] = np.kron(s[8:9], inner)
        back[beside(1), out] = np.kron(s[9:10], inner)
        back[beside(7), out] = np.kron(s[1:2], inner)
        back[beside(6), out] = np.kron(s[0:1], inner)
    wf = t["fine_weight"]
    wf2 = (wf[:, None] * wf[None, :]).reshape(-1)
    fine_mass = np.zeros((6, 384))
    for j in range(6):
        fine_mass[j, :144] = wf[2 * j] * wf2
        fine_mass[j, 144:288] = wf[2 * j + 1] * wf2
    eigen = np.zeros((2, LANES))
    eigen[0, :100] = t["eigen_around"]
    eigen[1, :100] = t["eigen_radial"]
    nodes = by_tile(t["mass_three"])
    weights = np.concatenate(
        [split_rows(m) for m in (pair, pair.T, fine, fine_slope, fine.T, ahead, back.T)]
    )
    along = np.concatenate([halves(d), halves(d.T), halves(itp), halves(slope), halves(itp.T)])
    fine_mass = np.repeat(fine_mass, ES, axis=0)
    tables = np.concatenate(
        [along, nodes]
        + [fine_mass[:, c : c + LANES] for c in range(0, 384, LANES)]
        + [np.pad(eigen, ((0, 6), (0, 0)))]
    )
    return (
        weights,
        np.asarray(tables, np.float32),
        np.asarray(s, np.float32),
        np.asarray(t["eigen_axial"], np.float32),
    )


PAIR = (0, 128, 256)
PAIR_T = (512, 256, 128)
FINE = (1024, 128, 384)
SLOPE = (1792, 128, 768)
FINE_T = (3328, 384, 128)
AHEAD = (4096, 256, 256)
BACK = (5120, 256, 256)
TABLE_NODES, TABLE_FINE, TABLE_EIGEN = 208, 272, 560
COEF_D, COEF_DT, COEF_I, COEF_S, COEF_IT = 0, 32, 64, 112, 160


OPERANDS = 7


def stages_of(count):
    stages = []
    stride = 1
    while stride < count:
        size = min(PEERS, count // stride)
        while (count // stride) % size:
            size -= 1
        stages.append((stride, size))
        stride *= size
    return stages


def kernel(
    count,
    *refs,
):
    operands, refs = refs[:OPERANDS], refs[OPERANDS:]
    pressure_ref, residual_ref = refs[:2]
    held, refs = refs[2 : 2 + OPERANDS], refs[2 + OPERANDS :]
    (
        load_sem,
        first_out,
        first_in,
        outbox,
        inbox,
        inbox_far,
        gathered,
        turned,
        basis,
        inverses,
        shares,
        spaces,
        dots,
        send_sem,
        recv_sem,
        gather_send_sem,
        gather_recv_sem,
    ) = refs
    split = [(0, None)] * 5 + [(0, AHEAD[0]), (AHEAD[0], None), (0, None)]
    loads = []
    for i, (at, end) in enumerate(split):
        which = min(i, 5) if i < 7 else 6
        rows = slice(None) if i < 5 else pl.ds(at, (end or operands[which].shape[0]) - at)
        loads.append(
            pltpu.make_async_copy(
                operands[which].at[rows], held[which].at[rows], load_sem.at[i]
            )
        )
    for i in (3, 2, 0, 7, 5, 1, 4, 6):
        loads[i].start()
    velocity, past, metric, jacobian, slots, weights, tables = held

    _, _, solve, eigen_axial = constants()
    me = lax.axis_index("dom")
    left = lax.rem(me + count - 1, count)
    right = lax.rem(me + 1, count)
    far_left = lax.rem(me + count - 2, count)
    far_right = lax.rem(me + 2, count)
    stages = stages_of(count)

    def peer(stage, offset):
        stride, size = stages[stage]
        digit = lax.rem(me // stride, size)
        other = lax.rem(digit + offset, size)
        return me + (other - digit) * stride

    barrier = pltpu.get_barrier_semaphore()
    greeted = [left, right, far_left, far_right] + [
        peer(stage, offset)
        for stage in range(len(stages))
        for offset in range(1, stages[stage][1])
    ]
    for other in greeted:
        pl.semaphore_signal(barrier, inc=1, device_id=(other,), device_id_type=MESH)

    lane = lax.broadcasted_iota(jnp.int32, (ES, LANES), 1)
    low = lane < 64
    node_s = lax.rem(lane, 64) // 8

    def tiles(field):
        return [field[i * ES : (i + 1) * ES] for i in range(field.shape[0] // ES)]

    def stack(parts):
        return jnp.concatenate(parts, axis=0)

    def mm(x, w):
        high = x.astype(jnp.bfloat16)
        rest = (x - high.astype(jnp.float32)).astype(jnp.bfloat16)
        at, depth, width = w
        columns = []
        for c in range(width // LANES):
            top = weights[at + 2 * c * depth : at + (2 * c + 1) * depth]
            bottom = weights[at + (2 * c + 1) * depth : at + (2 * c + 2) * depth]
            columns.append(jnp.concatenate([top, top, bottom], axis=0))
        return jnp.dot(
            jnp.concatenate([high, rest, high], axis=1),
            jnp.concatenate(columns, axis=1),
            preferred_element_type=jnp.float32,
        )

    def swap(tile):
        return pltpu.roll(tile, 64, 1)

    def along(field, base, total):
        parts = tiles(field)
        swapped = [swap(part) for part in parts]
        results = []
        for out in range(total):
            acc = None
            for into in range(len(parts)):
                at = base + 2 * (out * len(parts) + into)
                term = tables[at : at + 1] * parts[into] + tables[at + 1 : at + 2] * swapped[into]
                acc = term if acc is None else acc + term
            results.append(acc)
        return stack(results)

    def gradient(field):
        paired = mm(field, PAIR)
        return along(field, COEF_D, 4), paired[:, :LANES], paired[:, LANES:]

    def gradient_t(axial, around, radial):
        paired = mm(jnp.concatenate([around, radial], axis=1), PAIR_T)
        return paired + along(axial, COEF_DT, 4)

    def before(tile):
        return pltpu.roll(tile, 1, 0)

    def after(tile):
        return pltpu.roll(tile, ES - 1, 0)

    def around_sum(field):
        results = []
        for tile in tiles(field):
            first = before(pltpu.roll(tile, 72, 1))
            last = after(pltpu.roll(tile, 56, 1))
            results.append(
                tile + jnp.where(node_s == 0, first, jnp.where(node_s == 7, last, 0.0))
            )
        return stack(results)

    def copies(step, first=False):
        if first:
            plan = [(first_out.at[0], first_in.at[1], left), (first_out.at[1], first_in.at[0], right)]
        else:
            plan = [
                (outbox.at[step, pl.ds(0, ES)], inbox_far.at[step, 1], far_left),
                (outbox.at[step, pl.ds(3 * ES, ES)], inbox_far.at[step, 0], far_right),
                (outbox.at[step], inbox.at[step, 1], left),
                (outbox.at[step], inbox.at[step, 0], right),
            ]
        return [
            pltpu.make_async_remote_copy(
                src_ref=source,
                dst_ref=target,
                send_sem=send_sem.at[step, way],
                recv_sem=recv_sem.at[step, way],
                device_id=(other,),
                device_id_type=MESH,
            )
            for way, (source, target, other) in enumerate(plan)
        ]

    def send(step, field):
        outbox[step] = field
        for copy in copies(step):
            copy.start()

    def receive(step):
        for copy in copies(step):
            copy.wait_recv()

    def axial_sum(field, before_it, after_it):
        parts = tiles(field)
        return stack(
            [
                parts[0] + jnp.where(low, swap(before_it), 0.0),
                parts[1],
                parts[2],
                parts[3] + jnp.where(low, 0.0, swap(after_it)),
            ]
        )

    def element_field(ref, *index):
        return stack([ref[index + (slice(None), pl.ds(j * LANES, LANES))] for j in range(4)])

    loads[7].wait()
    loads[3].wait()
    weight3 = tables[TABLE_NODES:TABLE_FINE]
    fine_mass = jnp.concatenate(
        [tables[TABLE_FINE + 96 * c : TABLE_FINE + 96 * (c + 1)] for c in range(3)], axis=1
    )
    eigen = tables[TABLE_EIGEN:]
    jac = element_field(jacobian)
    mass = jac * weight3
    coarse = [along(jac, COEF_I, 6)]
    loads[2].wait()
    metrics = [element_field(metric, d) for d in range(3)]
    squares = [mass * m * m for m in metrics]
    loads[0].wait()
    newest = [element_field(velocity, 0, i) for i in range(3)]
    coarse += [along(newest[d] * metrics[d], COEF_I, 6) for d in range(3)]
    coarse += [along(newest[i], COEF_S, 6) for i in range(3)]
    loads[5].wait()
    fine = mm(stack(coarse), FINE)
    fine = [fine[i * 96 : (i + 1) * 96] for i in range(7)]
    crossed = mm(stack([along(newest[i], COEF_I, 6) for i in range(3)]), SLOPE)
    fine_jac = fine[0] * fine_mass
    products = []
    for i in range(3):
        rows = slice(i * 96, (i + 1) * 96)
        products.append(
            fine_jac
            * (
                fine[1] * fine[4 + i]
                + fine[2] * crossed[rows, :384]
                + fine[3] * crossed[rows, 384:]
            )
        )
    advected = mm(stack(products), FINE_T)
    guessed = [
        3.0 * newest[i] - 3.0 * element_field(velocity, 1, i) + element_field(velocity, 2, i)
        for i in range(3)
    ]
    paired = mm(stack(guessed), PAIR)
    slopes = jnp.concatenate(
        [
            stack([squares[1] * paired[i * 64 : (i + 1) * 64, :LANES] for i in range(3)]),
            stack([squares[2] * paired[i * 64 : (i + 1) * 64, LANES:] for i in range(3)]),
        ],
        axis=1,
    )
    paired_t = mm(slopes, PAIR_T)
    forcing = []
    loads[1].wait()
    loads[4].wait()
    for i in range(3):
        convect = along(advected[i * 96 : (i + 1) * 96], COEF_IT, 4)
        stiff = paired_t[i * 64 : (i + 1) * 64] + along(
            squares[0] * along(guessed[i], COEF_D, 4), COEF_DT, 4
        )
        history = (
            3.0 * newest[i]
            - 1.5 * element_field(velocity, 1, i)
            + element_field(velocity, 2, i) / 3.0
        )
        extrap = (
            3.0 * convect - 3.0 * element_field(past, 0, i) + element_field(past, 1, i)
        )
        helmholtz = viscosity * stiff + 11.0 / (6.0 * time_step) * mass * guessed[i]
        forcing.append(mass * history / time_step - extrap - helmholtz)

    fields = forcing + [mass] + metrics
    wide = jnp.concatenate([tile for field in fields for tile in tiles(field)], axis=1)
    first = wide.astype(jnp.bfloat16)
    rest = wide - first.astype(jnp.float32)
    second = rest.astype(jnp.bfloat16)
    third = (rest - second.astype(jnp.float32)).astype(jnp.bfloat16)
    position = lax.broadcasted_iota(jnp.int32, (ES, ES), 0)
    chosen = jnp.where(slots[...] == position, 1.0, 0.0)
    chosen = jnp.concatenate([chosen, chosen, chosen], axis=1).astype(jnp.bfloat16)
    placed = jnp.dot(chosen, stack([first, second, third]), preferred_element_type=jnp.float32)
    fields = [
        stack([placed[:, (4 * f + j) * LANES : (4 * f + j + 1) * LANES] for j in range(4)])
        for f in range(7)
    ]
    forcing, mass, metrics = fields[:3], fields[3], fields[4:]
    lumps = [mass * m for m in metrics]
    squares = [lumps[d] * metrics[d] for d in range(3)]

    def total(field):
        parts = tiles(field)
        return jnp.sum(parts[0] + parts[1] + parts[2] + parts[3], axis=1, keepdims=True) / 8.0

    flat = (
        total(squares[1]) * eigen[0:1]
        + total(squares[2]) * eigen[1:2]
        + mass_shift * total(mass)
    )
    steep = jnp.broadcast_to(total(squares[0]), (ES, LANES))

    around = [around_sum(f) for f in forcing + [mass]]
    first_out[0] = stack([f[:ES] for f in around] + [flat, steep])
    first_out[1] = stack([f[3 * ES :] for f in around] + [flat, steep])
    pl.semaphore_wait(barrier, len(greeted))
    for copy in copies(0, True):
        copy.start()
    for copy in copies(0, True):
        copy.wait_recv()
    lefts, rights = tiles(first_in[0]), tiles(first_in[1])
    summed = [axial_sum(around[f], lefts[f], rights[f]) for f in range(4)]
    accel = [lumps[d] * (summed[d] / summed[3]) for d in range(3)]
    divergence = gradient_t(accel[0], accel[1], accel[2])
    send(1, around_sum(divergence))
    loads[6].wait()
    flats = stack([lefts[4], flat, rights[4]])
    steeps = stack([lefts[5], steep, rights[5]])
    inverse = [1.0 / (steeps * float(eigen_axial[k]) + flats) for k in range(10)]
    for k in range(10):
        inverses[k] = inverse[k]
    shares[...] = divergence
    spaces[...] = jnp.zeros_like(spaces)

    def combine(weight, parts):
        acc = parts[0] * float(weight[0])
        for one, part in zip(weight[1:], parts[1:]):
            acc = acc + part * float(one)
        return acc

    def smooth(own, beside, ends):
        lower, upper = tiles(beside[0]), tiles(beside[1])
        lower[0] = lower[0] + jnp.where(low, swap(ends[0]), 0.0)
        upper[3] = upper[3] + jnp.where(low, 0.0, swap(ends[1]))
        parts = [jnp.where(low, ends[0], ends[1])] + lower + upper + tiles(own)
        sides = [
            jnp.where(node_s == 6, before(p), jnp.where(node_s == 1, after(p), 0.0))
            for p in parts
        ]
        modes = tiles(mm(jnp.concatenate([stack(parts), stack(sides)], axis=1), AHEAD))
        firsts = [-7, -5, -3, -1, 7, 9, 11, 13, 0, 2, 4, 6]
        grid = {-8: modes[0][:, :LANES], 15: modes[0][:, LANES:]}
        for row, mode in zip(firsts, modes[1:]):
            grid[row], grid[row + 1] = mode[:, :LANES], mode[:, LANES:]
        order = [stack([grid[a - 7], grid[a], grid[a + 7]]) for a in range(-1, 9)]
        spectra = [combine(solve[:, k], order) * inverses[k] for k in range(10)]
        slabs = [[spectrum[b * ES : (b + 1) * ES] for spectrum in spectra] for b in range(3)]
        rows = [combine(solve[a + 1], slabs[1]) for a in range(NP)]
        rows[0] = rows[0] + combine(solve[8], slabs[0])
        rows[1] = rows[1] + combine(solve[9], slabs[0])
        rows[6] = rows[6] + combine(solve[0], slabs[2])
        rows[7] = rows[7] + combine(solve[1], slabs[2])
        given = mm(jnp.concatenate([stack(rows[0::2]), stack(rows[1::2])], axis=1), BACK)
        return stack(
            [
                o + jnp.where(node_s <= 1, before(n), jnp.where(node_s >= 6, after(n), 0.0))
                for o, n in zip(tiles(given[:, :LANES]), tiles(given[:, LANES:]))
            ]
        )

    def apply(field):
        axial, around, radial = gradient(field)
        local = gradient_t(squares[0] * axial, squares[1] * around, squares[2] * radial)
        return local + mass_shift * mass * field

    def inner(one, two):
        return jnp.sum(one * two, axis=0, keepdims=True)

    def turn(which, field):
        for j, tile in enumerate(tiles(field)):
            turned[pl.ds(2 * j * ES, ES)] = tile
            turned[pl.ds((2 * j + 1) * ES, ES)] = swap(tile)
        for p in range(ES):
            block = turned[pl.ds(p, NP, stride=ES), :]
            basis[which, :, p * 56 : (p + 1) * 56] = block[:, :56]

    def iteration(it, carry):
        step = it + 1
        receive(step)
        beside = [inbox[step, 0], inbox[step, 1]]
        ends = [inbox_far[step, 0], inbox_far[step, 1]]
        current = axial_sum(outbox[step], beside[0][3 * ES :], beside[1][:ES])
        space = smooth(current, beside, ends)
        local = apply(space)
        spaces[it] = space
        send(step + 1, around_sum(local))
        dots[it] = jnp.concatenate([inner(local, spaces[j]) for j in range(ITERS)], axis=0)
        turn(2 * it, current)
        turn(2 * it + 1, space)
        return carry

    lax.fori_loop(0, ITERS, iteration, 0)
    head = inner(shares[...], spaces[0])
    value = jnp.concatenate(
        [head]
        + [dots[j, i : i + 1] for i in range(3) for j in range(i, 3)]
        + [jnp.zeros((1, LANES), jnp.float32)],
        axis=0,
    )
    started = []
    for stage, (stride, size) in enumerate(stages):
        digit = lax.rem(me // stride, size)
        gathered[stage, digit] = value
        for offset in range(1, size):
            copy = pltpu.make_async_remote_copy(
                src_ref=gathered.at[stage, digit],
                dst_ref=gathered.at[stage, digit],
                send_sem=gather_send_sem.at[stage, offset],
                recv_sem=gather_recv_sem.at[stage, offset],
                device_id=(peer(stage, offset),),
                device_id_type=MESH,
            )
            copy.start()
            started.append(copy)
        if stage == 0:
            last = ROUNDS - 1
            receive(last)
            turn(
                6, axial_sum(outbox[last], inbox[last, 0, 3 * ES :], inbox[last, 1, :ES])
            )
        for copy in started[1 - size :]:
            copy.wait_recv()
        value = gathered[stage, 0]
        for slot in range(1, size):
            value = value + gathered[stage, slot]
    sums = jnp.sum(value, axis=1, keepdims=True)
    sums = [sums[i : i + 1] for i in range(7)]
    gram = {}
    for at, (i, j) in enumerate([(i, j) for i in range(3) for j in range(i, 3)]):
        gram[i, j] = gram[j, i] = sums[1 + at]
    heads = [sums[0], gram[0, 0], gram[0, 1]]
    taken = [None] * 3
    direction = [None] * 3
    result = [None] * 3
    previous = None
    for it in range(ITERS):
        z = [None] * 3
        z[0] = jnp.ones((1, 1), jnp.float32)
        for k in range(1, it + 1):
            z[k] = taken[k - 1]
        rho = heads[0]
        for k in range(1, it + 1):
            rho = rho + z[k] * heads[k]
        for i in range(it):
            row = gram[i, 0]
            for k in range(1, it + 1):
                row = row + z[k] * gram[i, k]
            rho = rho + taken[i] * row
        if it == 0:
            direction = [z[0], None, None]
        else:
            beta = rho / previous
            direction = [
                None if k > it else z[k] if direction[k] is None else z[k] + beta * direction[k]
                for k in range(3)
            ]
        bottom = None
        for i in range(it + 1):
            row = None
            for k in range(it + 1):
                term = direction[k] * gram[i, k]
                row = term if row is None else row + term
            bottom = direction[i] * row if bottom is None else bottom + direction[i] * row
        alpha = rho / bottom
        for k in range(it + 1):
            step = alpha * direction[k]
            result[k] = step if result[k] is None else result[k] + step
            taken[k] = -step if taken[k] is None else taken[k] - step
        previous = rho
    pressure_ref[...] = sum(basis[2 * k + 1] * result[k] for k in range(3))
    residual_ref[...] = basis[0] + sum(basis[2 * k + 2] * taken[k] for k in range(3))

    for step in range(ROUNDS):
        for copy in copies(step, step == 0):
            copy.wait_send()
    for copy in started:
        copy.wait_send()


def shards(count, velocity, conv_past, metric, jacobian, element_slot):
    weights, tables, _, _ = constants()
    stages = stages_of(count)
    block = jax.ShapeDtypeStruct((A0, A1 * A2), jnp.float32)
    whole = pl.BlockSpec(memory_space=pltpu.VMEM)
    slots = element_slot.reshape(1, ES)
    operands = [velocity, conv_past, metric, jacobian, slots]
    operands += [jnp.asarray(weights), jnp.asarray(tables)]
    return pl.pallas_call(
        functools.partial(kernel, count),
        out_shape=(block, block),
        in_specs=[pl.BlockSpec(memory_space=pltpu.HBM)] * len(operands),
        out_specs=(whole, whole),
        scratch_shapes=[pltpu.VMEM(x.shape, x.dtype) for x in operands]
        + [
            pltpu.SemaphoreType.DMA((len(operands) + 1,)),
            pltpu.VMEM((2, 6 * ES, LANES), jnp.float32),
            pltpu.VMEM((2, 6 * ES, LANES), jnp.float32),
            pltpu.VMEM((ROUNDS, 4 * ES, LANES), jnp.float32),
            pltpu.VMEM((ROUNDS, 2, 4 * ES, LANES), jnp.float32),
            pltpu.VMEM((ROUNDS, 2, ES, LANES), jnp.float32),
            pltpu.VMEM((len(stages), PEERS, 8, LANES), jnp.float32),
            pltpu.VMEM((NP * ES, LANES), jnp.float32),
            pltpu.VMEM((7, A0, A1 * A2), jnp.float32),
            pltpu.VMEM((10, 3 * ES, LANES), jnp.float32),
            pltpu.VMEM((4 * ES, LANES), jnp.float32),
            pltpu.VMEM((ITERS, 4 * ES, LANES), jnp.float32),
            pltpu.VMEM((ITERS, ITERS, LANES), jnp.float32),
            pltpu.SemaphoreType.DMA((ROUNDS, WAYS)),
            pltpu.SemaphoreType.DMA((ROUNDS, WAYS)),
            pltpu.SemaphoreType.DMA((len(stages), PEERS)),
            pltpu.SemaphoreType.DMA((len(stages), PEERS)),
        ],
        compiler_params=pltpu.CompilerParams(
            collective_id=0, has_side_effects=True, vmem_limit_bytes=55168 * 1024
        ),
    )(*operands)


def solution(mesh):
    return jax.shard_map(
        functools.partial(shards, mesh.shape["dom"]),
        mesh=mesh,
        in_specs=(
            P(None, None, "dom", None),
            P(None, None, "dom", None),
            P(None, "dom", None),
            P("dom", None),
            P("dom"),
        ),
        out_specs=(P("dom", None), P("dom", None)),
        check_vma=False,
    )
```

```python
import functools

import jax
import jax.numpy as jnp
import numpy as np
from jax import lax
from jax.experimental import pallas as pl
from jax.experimental.pallas import tpu as pltpu
from jax.sharding import PartitionSpec as P

NP = 8
NF = 12
ES = 16
ITERS = 3
A0 = 8
A1 = 112
A2 = 8
ROUNDS = 5
WAYS = 4
PEERS = 8
LANES = 128
MESH = pl.DeviceIdType.MESH

time_step = 0.25
viscosity = 0.05
mass_shift = 0.001


def legendre_pair(points, order):
    before = np.ones(points.shape)
    current = points * 1.0
    for level in range(2, order + 1):
        nextone = ((2 * level - 1) * points * current - (level - 1) * before) / level
        before = current
        current = nextone
    return (current, before)


def jacobi_eigen(matrix):
    size = matrix.shape[0]
    work = matrix * 1.0
    vectors = np.eye(size)
    for sweep in range(30):
        for first in range(size - 1):
            for second in range(first + 1, size):
                off = float(work[first, second])
                if abs(off) > 1e-300:
                    tau = (float(work[second, second]) - float(work[first, first])) / (2.0 * off)
                    if tau >= 0.0:
                        tangent = 1.0 / (tau + (1.0 + tau * tau) ** 0.5)
                    else:
                        tangent = -1.0 / (-tau + (1.0 + tau * tau) ** 0.5)
                    cosine = 1.0 / (1.0 + tangent * tangent) ** 0.5
                    sine = tangent * cosine
                    rotation = np.eye(size)
                    rotation[first, first] = cosine
                    rotation[second, second] = cosine
                    rotation[first, second] = sine
                    rotation[second, first] = -sine
                    work = rotation.T @ work @ rotation
                    vectors = vectors @ rotation
    diagonal_index = np.arange(size)
    return (work[diagonal_index, diagonal_index], vectors)


def build_tables(points_edge, points_fine):
    degree = points_edge - 1
    points = -np.cos(np.pi * np.arange(points_edge) / degree)
    for sweep in range(100):
        top, below = legendre_pair(points, degree)
        points = points - (points * top - below) / (points_edge * top)
    top, below = legendre_pair(points, degree)
    weight_gll = 2.0 / (degree * points_edge * top**2)
    spacing = points[:, None] - points[None, :] + np.eye(points_edge)
    barycentric = 1.0 / np.prod(spacing, axis=1)
    derivative = barycentric[None, :] / barycentric[:, None] / spacing
    derivative = derivative * (1.0 - np.eye(points_edge))
    derivative = derivative - np.eye(points_edge) * derivative.sum(axis=1)[:, None]
    fine_points = np.cos(np.pi * (np.arange(points_fine) + 0.75) / (points_fine + 0.5))
    for sweep in range(100):
        top, below = legendre_pair(fine_points, points_fine)
        slope = points_fine * (fine_points * top - below) / (fine_points * fine_points - 1.0)
        fine_points = fine_points - top / slope
    top, below = legendre_pair(fine_points, points_fine)
    slope = points_fine * (fine_points * top - below) / (fine_points * fine_points - 1.0)
    fine_weight = 2.0 / ((1.0 - fine_points * fine_points) * slope * slope)
    fine_points = fine_points[::-1]
    fine_weight = fine_weight[::-1]
    interpolate = np.ones((points_fine, points_edge))
    for column in range(points_edge):
        for other in range(points_edge):
            if other != column:
                interpolate[:, column] = (
                    interpolate[:, column]
                    * (fine_points - points[other])
                    / (points[column] - points[other])
                )
    stiffness = derivative.T @ (weight_gll[:, None] * derivative)
    extent = 3 * degree + 1
    joined_stiff = np.zeros((extent, extent))
    joined_mass = np.zeros(extent)
    for segment in range(3):
        offset = segment * degree
        joined_stiff[offset : offset + points_edge, offset : offset + points_edge] += stiffness
        joined_mass[offset : offset + points_edge] += weight_gll
    low = degree - 1
    high = 2 * degree + 2
    root_mass = np.sqrt(joined_mass[low:high])
    scaled = joined_stiff[low:high, low:high] / root_mass[:, None] / root_mass[None, :]
    scaled = 0.5 * (scaled + scaled.T)
    eigen_values, eigen_vectors = jacobi_eigen(scaled)
    solve_mat = eigen_vectors / root_mass[:, None]
    breadth = high - low
    identity = np.eye(points_edge)
    operator_tables = {
        "derivative": derivative,
        "dpair": np.concatenate(
            [np.kron(derivative, identity).T, np.kron(identity, derivative).T], axis=1
        ),
        "interpolate": interpolate,
        "ipair": np.kron(interpolate, interpolate).T,
        "mass_three": (
            weight_gll[:, None, None] * weight_gll[None, :, None] * weight_gll[None, None, :]
        ).reshape(points_edge, points_edge * points_edge),
        "fine_three": (
            fine_weight[:, None, None] * fine_weight[None, :, None] * fine_weight[None, None, :]
        ).reshape(points_fine, points_fine * points_fine),
        "solve_mat": solve_mat,
        "solve_pair": np.kron(solve_mat, solve_mat),
        "eigen_axial": eigen_values,
        "eigen_around": np.repeat(eigen_values, breadth),
        "eigen_radial": np.tile(eigen_values, breadth),
    }
    operator_tables["weight"] = weight_gll
    operator_tables["fine_weight"] = fine_weight
    return operator_tables


def split_rows(matrix):
    exact = np.asarray(matrix, np.float32)
    high = exact.astype(jnp.bfloat16)
    low = (exact - high.astype(np.float32)).astype(jnp.bfloat16)
    columns = range(0, exact.shape[1], LANES)
    return np.concatenate([part[:, c : c + LANES] for c in columns for part in (high, low)])


def halves(matrix):
    rows, columns = matrix.shape
    table = np.zeros((rows // 2, columns // 2, 2, LANES))
    for out in range(rows // 2):
        for into in range(columns // 2):
            table[out, into, 0, :64] = matrix[2 * out, 2 * into]
            table[out, into, 0, 64:] = matrix[2 * out + 1, 2 * into + 1]
            table[out, into, 1, :64] = matrix[2 * out, 2 * into + 1]
            table[out, into, 1, 64:] = matrix[2 * out + 1, 2 * into]
    return np.asarray(table.reshape(-1, LANES), np.float32)


def twice(block, stride):
    rows, columns = block.shape
    result = np.zeros((2 * rows, 2 * stride))
    result[:rows, :columns] = block
    result[rows:, stride : stride + columns] = block
    return result


def pad_columns(matrix, total):
    return np.pad(matrix, ((0, 0), (0, total - matrix.shape[1])))


def by_tile(table):
    return np.asarray(np.repeat(table.reshape(-1, LANES), ES, axis=0), np.float32)


@functools.cache
def constants():
    t = build_tables(NP, NF)
    d, itp, s = t["derivative"], t["interpolate"], t["solve_mat"]
    eye = np.eye(NP)
    pair = np.concatenate(
        [twice(np.kron(d, eye).T, 64), twice(np.kron(eye, d).T, 64)], axis=1
    )
    fine = pad_columns(twice(np.kron(itp, itp).T, 144), 384)
    slope = itp @ d
    fine_slope = np.concatenate(
        [
            pad_columns(twice(np.kron(slope, itp).T, 144), 384),
            pad_columns(twice(np.kron(itp, slope).T, 144), 384),
        ],
        axis=1,
    )
    inner = s[1:9]
    ahead = np.zeros((2 * LANES, 2 * LANES))
    back = np.zeros((2 * LANES, 2 * LANES))
    for h in range(2):
        out = slice(h * LANES, h * LANES + 100)

        def lanes(row):
            return slice(h * 64 + row * 8, h * 64 + row * 8 + 8)

        def beside(row):
            return slice(LANES + h * 64 + row * 8, LANES + h * 64 + row * 8 + 8)

        for row in range(NP):
            ahead[lanes(row), out] = np.kron(s[row + 1 : row + 2], inner)
            back[lanes(row), out] = np.kron(s[row + 1 : row + 2], inner)
        ahead[beside(6), out] = np.kron(s[0:1], inner)
        ahead[beside(1), out] = np.kron(s[9:10], inner)
        back[beside(0), out] = np.kron(s[8:9], inner)
        back[beside(1), out] = np.kron(s[9:10], inner)
        back[beside(7), out] = np.kron(s[1:2], inner)
        back[beside(6), out] = np.kron(s[0:1], inner)
    wf = t["fine_weight"]
    wf2 = (wf[:, None] * wf[None, :]).reshape(-1)
    fine_mass = np.zeros((6, 384))
    for j in range(6):
        fine_mass[j, :144] = wf[2 * j] * wf2
        fine_mass[j, 144:288] = wf[2 * j + 1] * wf2
    eigen = np.zeros((2, LANES))
    eigen[0, :100] = t["eigen_around"]
    eigen[1, :100] = t["eigen_radial"]
    nodes = by_tile(t["mass_three"])
    weights = np.concatenate(
        [split_rows(m) for m in (pair, pair.T, fine, fine_slope, fine.T, ahead, back.T)]
    )
    along = np.concatenate([halves(d), halves(d.T), halves(itp), halves(slope), halves(itp.T)])
    fine_mass = np.repeat(fine_mass, ES, axis=0)
    tables = np.concatenate(
        [along, nodes]
        + [fine_mass[:, c : c + LANES] for c in range(0, 384, LANES)]
        + [np.pad(eigen, ((0, 6), (0, 0)))]
    )
    return (
        weights,
        np.asarray(tables, np.float32),
        np.asarray(s, np.float32),
        np.asarray(t["eigen_axial"], np.float32),
    )


PAIR = (0, 128, 256)
PAIR_T = (512, 256, 128)
FINE = (1024, 128, 384)
SLOPE = (1792, 128, 768)
FINE_T = (3328, 384, 128)
AHEAD = (4096, 256, 256)
BACK = (5120, 256, 256)
TABLE_NODES, TABLE_FINE, TABLE_EIGEN = 208, 272, 560
COEF_D, COEF_DT, COEF_I, COEF_S, COEF_IT = 0, 32, 64, 112, 160


OPERANDS = 7


def stages_of(count):
    stages = []
    stride = 1
    while stride < count:
        size = min(PEERS, count // stride)
        while (count // stride) % size:
            size -= 1
        stages.append((stride, size))
        stride *= size
    return stages


def kernel(
    count,
    *refs,
):
    operands, refs = refs[:OPERANDS], refs[OPERANDS:]
    pressure_ref, residual_ref = refs[:2]
    held, refs = refs[2 : 2 + OPERANDS], refs[2 + OPERANDS :]
    (
        load_sem,
        first_out,
        first_in,
        outbox,
        inbox,
        inbox_far,
        gathered,
        turned,
        basis,
        send_sem,
        recv_sem,
        gather_send_sem,
        gather_recv_sem,
    ) = refs
    split = [(0, None)] * 5 + [(0, AHEAD[0]), (AHEAD[0], None), (0, None)]
    loads = []
    for i, (at, end) in enumerate(split):
        which = min(i, 5) if i < 7 else 6
        rows = slice(None) if i < 5 else pl.ds(at, (end or operands[which].shape[0]) - at)
        loads.append(
            pltpu.make_async_copy(
                operands[which].at[rows], held[which].at[rows], load_sem.at[i]
            )
        )
    for i in (3, 2, 0, 7, 5, 1, 4, 6):
        loads[i].start()
    velocity, past, metric, jacobian, slots, weights, tables = held

    _, _, solve, eigen_axial = constants()
    me = lax.axis_index("dom")
    left = lax.rem(me + count - 1, count)
    right = lax.rem(me + 1, count)
    far_left = lax.rem(me + count - 2, count)
    far_right = lax.rem(me + 2, count)
    stages = stages_of(count)

    def peer(stage, offset):
        stride, size = stages[stage]
        digit = lax.rem(me // stride, size)
        other = lax.rem(digit + offset, size)
        return me + (other - digit) * stride

    barrier = pltpu.get_barrier_semaphore()
    greeted = [left, right, far_left, far_right] + [
        peer(stage, offset)
        for stage in range(len(stages))
        for offset in range(1, stages[stage][1])
    ]
    for other in greeted:
        pl.semaphore_signal(barrier, inc=1, device_id=(other,), device_id_type=MESH)

    lane = lax.broadcasted_iota(jnp.int32, (ES, LANES), 1)
    low = lane < 64
    node_s = lax.rem(lane, 64) // 8

    def tiles(field):
        return [field[i * ES : (i + 1) * ES] for i in range(field.shape[0] // ES)]

    def stack(parts):
        return jnp.concatenate(parts, axis=0)

    def mm(x, w):
        high = x.astype(jnp.bfloat16)
        rest = (x - high.astype(jnp.float32)).astype(jnp.bfloat16)
        at, depth, width = w
        columns = []
        for c in range(width // LANES):
            top = weights[at + 2 * c * depth : at + (2 * c + 1) * depth]
            bottom = weights[at + (2 * c + 1) * depth : at + (2 * c + 2) * depth]
            columns.append(jnp.concatenate([top, top, bottom], axis=0))
        return jnp.dot(
            jnp.concatenate([high, rest, high], axis=1),
            jnp.concatenate(columns, axis=1),
            preferred_element_type=jnp.float32,
        )

    def swap(tile):
        return pltpu.roll(tile, 64, 1)

    def along(field, base, total):
        parts = tiles(field)
        swapped = [swap(part) for part in parts]
        results = []
        for out in range(total):
            acc = None
            for into in range(len(parts)):
                at = base + 2 * (out * len(parts) + into)
                term = tables[at : at + 1] * parts[into] + tables[at + 1 : at + 2] * swapped[into]
                acc = term if acc is None else acc + term
            results.append(acc)
        return stack(results)

    def gradient(field):
        paired = mm(field, PAIR)
        return along(field, COEF_D, 4), paired[:, :LANES], paired[:, LANES:]

    def gradient_t(axial, around, radial):
        paired = mm(jnp.concatenate([around, radial], axis=1), PAIR_T)
        return paired + along(axial, COEF_DT, 4)

    def before(tile):
        return pltpu.roll(tile, 1, 0)

    def after(tile):
        return pltpu.roll(tile, ES - 1, 0)

    def around_sum(field):
        results = []
        for tile in tiles(field):
            first = before(pltpu.roll(tile, 72, 1))
            last = after(pltpu.roll(tile, 56, 1))
            results.append(
                tile + jnp.where(node_s == 0, first, jnp.where(node_s == 7, last, 0.0))
            )
        return stack(results)

    def copies(step):
        if step == 0:
            plan = [(first_out.at[0], first_in.at[1], left), (first_out.at[1], first_in.at[0], right)]
        elif step < ROUNDS - 1:
            plan = [
                (outbox.at[step, pl.ds(0, ES)], inbox_far.at[step, 1], far_left),
                (outbox.at[step, pl.ds(3 * ES, ES)], inbox_far.at[step, 0], far_right),
                (outbox.at[step], inbox.at[step, 1], left),
                (outbox.at[step], inbox.at[step, 0], right),
            ]
        else:
            plan = [
                (outbox.at[step, pl.ds(0, ES)], inbox_far.at[step, 1], left),
                (outbox.at[step, pl.ds(3 * ES, ES)], inbox_far.at[step, 0], right),
            ]
        return [
            pltpu.make_async_remote_copy(
                src_ref=source,
                dst_ref=target,
                send_sem=send_sem.at[step, way],
                recv_sem=recv_sem.at[step, way],
                device_id=(other,),
                device_id_type=MESH,
            )
            for way, (source, target, other) in enumerate(plan)
        ]

    def send(step, field):
        outbox[step] = field
        for copy in copies(step):
            copy.start()

    def receive(step):
        for copy in copies(step):
            copy.wait_recv()

    def axial_sum(field, before_it, after_it):
        parts = tiles(field)
        return stack(
            [
                parts[0] + jnp.where(low, swap(before_it), 0.0),
                parts[1],
                parts[2],
                parts[3] + jnp.where(low, 0.0, swap(after_it)),
            ]
        )

    def surrounded(step, field):
        receive(step)
        beside = [inbox[step, 0], inbox[step, 1]]
        ends = [inbox_far[step, 0], inbox_far[step, 1]]
        own = axial_sum(field, beside[0][3 * ES :], beside[1][:ES])
        return own, beside, ends

    def element_field(ref, *index):
        return stack([ref[index + (slice(None), pl.ds(j * LANES, LANES))] for j in range(4)])

    loads[7].wait()
    loads[3].wait()
    weight3 = tables[TABLE_NODES:TABLE_FINE]
    fine_mass = jnp.concatenate(
        [tables[TABLE_FINE + 96 * c : TABLE_FINE + 96 * (c + 1)] for c in range(3)], axis=1
    )
    eigen = tables[TABLE_EIGEN:]
    jac = element_field(jacobian)
    mass = jac * weight3
    coarse = [along(jac, COEF_I, 6)]
    loads[2].wait()
    metrics = [element_field(metric, d) for d in range(3)]
    squares = [mass * m * m for m in metrics]
    loads[0].wait()
    newest = [element_field(velocity, 0, i) for i in range(3)]
    coarse += [along(newest[d] * metrics[d], COEF_I, 6) for d in range(3)]
    coarse += [along(newest[i], COEF_S, 6) for i in range(3)]
    loads[5].wait()
    fine = mm(stack(coarse), FINE)
    fine = [fine[i * 96 : (i + 1) * 96] for i in range(7)]
    crossed = mm(stack([along(newest[i], COEF_I, 6) for i in range(3)]), SLOPE)
    fine_jac = fine[0] * fine_mass
    products = []
    for i in range(3):
        rows = slice(i * 96, (i + 1) * 96)
        products.append(
            fine_jac
            * (
                fine[1] * fine[4 + i]
                + fine[2] * crossed[rows, :384]
                + fine[3] * crossed[rows, 384:]
            )
        )
    advected = mm(stack(products), FINE_T)
    guessed = [
        3.0 * newest[i] - 3.0 * element_field(velocity, 1, i) + element_field(velocity, 2, i)
        for i in range(3)
    ]
    paired = mm(stack(guessed), PAIR)
    slopes = jnp.concatenate(
        [
            stack([squares[1] * paired[i * 64 : (i + 1) * 64, :LANES] for i in range(3)]),
            stack([squares[2] * paired[i * 64 : (i + 1) * 64, LANES:] for i in range(3)]),
        ],
        axis=1,
    )
    paired_t = mm(slopes, PAIR_T)
    forcing = []
    loads[1].wait()
    loads[4].wait()
    for i in range(3):
        convect = along(advected[i * 96 : (i + 1) * 96], COEF_IT, 4)
        stiff = paired_t[i * 64 : (i + 1) * 64] + along(
            squares[0] * along(guessed[i], COEF_D, 4), COEF_DT, 4
        )
        history = (
            3.0 * newest[i]
            - 1.5 * element_field(velocity, 1, i)
            + element_field(velocity, 2, i) / 3.0
        )
        extrap = (
            3.0 * convect - 3.0 * element_field(past, 0, i) + element_field(past, 1, i)
        )
        helmholtz = viscosity * stiff + 11.0 / (6.0 * time_step) * mass * guessed[i]
        forcing.append(mass * history / time_step - extrap - helmholtz)

    fields = forcing + [mass] + metrics
    wide = jnp.concatenate([tile for field in fields for tile in tiles(field)], axis=1)
    first = wide.astype(jnp.bfloat16)
    rest = wide - first.astype(jnp.float32)
    second = rest.astype(jnp.bfloat16)
    third = (rest - second.astype(jnp.float32)).astype(jnp.bfloat16)
    position = lax.broadcasted_iota(jnp.int32, (ES, ES), 0)
    chosen = jnp.where(slots[...] == position, 1.0, 0.0)
    chosen = jnp.concatenate([chosen, chosen, chosen], axis=1).astype(jnp.bfloat16)
    placed = jnp.dot(chosen, stack([first, second, third]), preferred_element_type=jnp.float32)
    fields = [
        stack([placed[:, (4 * f + j) * LANES : (4 * f + j + 1) * LANES] for j in range(4)])
        for f in range(7)
    ]
    forcing, mass, metrics = fields[:3], fields[3], fields[4:]
    lumps = [mass * m for m in metrics]
    squares = [lumps[d] * metrics[d] for d in range(3)]

    def total(field):
        parts = tiles(field)
        return jnp.sum(parts[0] + parts[1] + parts[2] + parts[3], axis=1, keepdims=True) / 8.0

    flat = (
        total(squares[1]) * eigen[0:1]
        + total(squares[2]) * eigen[1:2]
        + mass_shift * total(mass)
    )
    steep = jnp.broadcast_to(total(squares[0]), (ES, LANES))

    around = [around_sum(f) for f in forcing + [mass]]
    first_out[0] = stack([f[:ES] for f in around] + [flat, steep])
    first_out[1] = stack([f[3 * ES :] for f in around] + [flat, steep])
    pl.semaphore_wait(barrier, len(greeted))
    for copy in copies(0):
        copy.start()
    receive(0)
    lefts, rights = tiles(first_in[0]), tiles(first_in[1])
    summed = [axial_sum(around[f], lefts[f], rights[f]) for f in range(4)]
    accel = [lumps[d] * (summed[d] / summed[3]) for d in range(3)]
    divergence = gradient_t(accel[0], accel[1], accel[2])
    source = around_sum(divergence)
    send(1, source)
    loads[6].wait()
    flats = stack([lefts[4], flat, rights[4]])
    steeps = stack([lefts[5], steep, rights[5]])
    inverse = [1.0 / (steeps * float(eigen_axial[k]) + flats) for k in range(10)]
    source, beside, ends = surrounded(1, source)

    def combine(weight, parts):
        acc = parts[0] * float(weight[0])
        for one, part in zip(weight[1:], parts[1:]):
            acc = acc + part * float(one)
        return acc

    def smooth(own, beside, ends):
        lower, upper = tiles(beside[0]), tiles(beside[1])
        lower[0] = lower[0] + jnp.where(low, swap(ends[0]), 0.0)
        upper[3] = upper[3] + jnp.where(low, 0.0, swap(ends[1]))
        parts = [jnp.where(low, ends[0], ends[1])] + lower + upper + tiles(own)
        sides = [
            jnp.where(node_s == 6, before(p), jnp.where(node_s == 1, after(p), 0.0))
            for p in parts
        ]
        modes = tiles(mm(jnp.concatenate([stack(parts), stack(sides)], axis=1), AHEAD))
        firsts = [-7, -5, -3, -1, 7, 9, 11, 13, 0, 2, 4, 6]
        grid = {-8: modes[0][:, :LANES], 15: modes[0][:, LANES:]}
        for row, mode in zip(firsts, modes[1:]):
            grid[row], grid[row + 1] = mode[:, :LANES], mode[:, LANES:]
        order = [stack([grid[a - 7], grid[a], grid[a + 7]]) for a in range(-1, 9)]
        spectra = [combine(solve[:, k], order) * inverse[k] for k in range(10)]
        slabs = [[spectrum[b * ES : (b + 1) * ES] for spectrum in spectra] for b in range(3)]
        rows = [combine(solve[a + 1], slabs[1]) for a in range(NP)]
        rows[0] = rows[0] + combine(solve[8], slabs[0])
        rows[1] = rows[1] + combine(solve[9], slabs[0])
        rows[6] = rows[6] + combine(solve[0], slabs[2])
        rows[7] = rows[7] + combine(solve[1], slabs[2])
        given = mm(jnp.concatenate([stack(rows[0::2]), stack(rows[1::2])], axis=1), BACK)
        return stack(
            [
                o + jnp.where(node_s <= 1, before(n), jnp.where(node_s >= 6, after(n), 0.0))
                for o, n in zip(tiles(given[:, :LANES]), tiles(given[:, LANES:]))
            ]
        )

    def apply(field):
        axial, around, radial = gradient(field)
        local = gradient_t(squares[0] * axial, squares[1] * around, squares[2] * radial)
        return local + mass_shift * mass * field

    def inner(one, two):
        return jnp.sum(one * two, axis=0, keepdims=True)

    def turn(which, field):
        for j, tile in enumerate(tiles(field)):
            turned[which, pl.ds(2 * j * ES, ES)] = tile
            turned[which, pl.ds((2 * j + 1) * ES, ES)] = swap(tile)
        for p in range(ES):
            block = turned[which, pl.ds(p, NP, stride=ES), :]
            basis[which, :, p * 56 : (p + 1) * 56] = block[:, :56]

    spaces, images, dots = [], [], {}
    current = source
    for it in range(ITERS):
        spaces.append(smooth(current, beside, ends))
        local = apply(spaces[-1])
        image = around_sum(local)
        send(2 + it, image)
        if it == 0:
            head = inner(divergence, spaces[0])
        for j in range(it + 1):
            dots[j, it] = inner(local, spaces[j])
        if it < ITERS - 1:
            turn(2 * it, spaces[it])
            if it == 0:
                turn(6, current)
            else:
                turn(2 * it - 1, current)
            current, beside, ends = surrounded(2 + it, image)
            images.append(current)

    value = jnp.concatenate(
        [head]
        + [dots[i, j] for i in range(3) for j in range(i, 3)]
        + [jnp.zeros((1, LANES), jnp.float32)],
        axis=0,
    )
    started = []
    for stage, (stride, size) in enumerate(stages):
        digit = lax.rem(me // stride, size)
        gathered[stage, digit] = value
        for offset in range(1, size):
            copy = pltpu.make_async_remote_copy(
                src_ref=gathered.at[stage, digit],
                dst_ref=gathered.at[stage, digit],
                send_sem=gather_send_sem.at[stage, offset],
                recv_sem=gather_recv_sem.at[stage, offset],
                device_id=(peer(stage, offset),),
                device_id_type=MESH,
            )
            copy.start()
            started.append(copy)
        if stage == 0:
            turn(4, spaces[2])
            turn(3, images[1])
            receive(ROUNDS - 1)
            ends = [inbox_far[ROUNDS - 1, 0], inbox_far[ROUNDS - 1, 1]]
            turn(5, axial_sum(image, ends[0], ends[1]))
        for copy in started[1 - size :]:
            copy.wait_recv()
        value = gathered[stage, 0]
        for slot in range(1, size):
            value = value + gathered[stage, slot]
    sums = jnp.sum(value, axis=1, keepdims=True)
    sums = [sums[i : i + 1] for i in range(7)]
    gram = {}
    for at, (i, j) in enumerate([(i, j) for i in range(3) for j in range(i, 3)]):
        gram[i, j] = gram[j, i] = sums[1 + at]
    heads = [sums[0], gram[0, 0], gram[0, 1]]
    taken = [None] * 3
    direction = [None] * 3
    result = [None] * 3
    previous = None
    for it in range(ITERS):
        z = [None] * 3
        z[0] = jnp.ones((1, 1), jnp.float32)
        for k in range(1, it + 1):
            z[k] = taken[k - 1]
        rho = heads[0]
        for k in range(1, it + 1):
            rho = rho + z[k] * heads[k]
        for i in range(it):
            row = gram[i, 0]
            for k in range(1, it + 1):
                row = row + z[k] * gram[i, k]
            rho = rho + taken[i] * row
        if it == 0:
            direction = [z[0], None, None]
        else:
            beta = rho / previous
            direction = [
                None if k > it else z[k] if direction[k] is None else z[k] + beta * direction[k]
                for k in range(3)
            ]
        bottom = None
        for i in range(it + 1):
            row = None
            for k in range(it + 1):
                term = direction[k] * gram[i, k]
                row = term if row is None else row + term
            bottom = direction[i] * row if bottom is None else bottom + direction[i] * row
        alpha = rho / bottom
        for k in range(it + 1):
            step = alpha * direction[k]
            result[k] = step if result[k] is None else result[k] + step
            taken[k] = -step if taken[k] is None else taken[k] - step
        previous = rho
    pressure_ref[...] = sum(basis[2 * k] * result[k] for k in range(3))
    residual_ref[...] = basis[6] + sum(basis[2 * k + 1] * taken[k] for k in range(3))

    for step in range(ROUNDS):
        for copy in copies(step):
            copy.wait_send()
    for copy in started:
        copy.wait_send()


def shards(count, velocity, conv_past, metric, jacobian, element_slot):
    weights, tables, _, _ = constants()
    stages = stages_of(count)
    block = jax.ShapeDtypeStruct((A0, A1 * A2), jnp.float32)
    whole = pl.BlockSpec(memory_space=pltpu.VMEM)
    slots = element_slot.reshape(1, ES)
    operands = [velocity, conv_past, metric, jacobian, slots]
    operands += [jnp.asarray(weights), jnp.asarray(tables)]
    return pl.pallas_call(
        functools.partial(kernel, count),
        out_shape=(block, block),
        in_specs=[pl.BlockSpec(memory_space=pltpu.HBM)] * len(operands),
        out_specs=(whole, whole),
        scratch_shapes=[pltpu.VMEM(x.shape, x.dtype) for x in operands]
        + [
            pltpu.SemaphoreType.DMA((len(operands) + 1,)),
            pltpu.VMEM((2, 6 * ES, LANES), jnp.float32),
            pltpu.VMEM((2, 6 * ES, LANES), jnp.float32),
            pltpu.VMEM((ROUNDS, 4 * ES, LANES), jnp.float32),
            pltpu.VMEM((ROUNDS, 2, 4 * ES, LANES), jnp.float32),
            pltpu.VMEM((ROUNDS, 2, ES, LANES), jnp.float32),
            pltpu.VMEM((len(stages), PEERS, 8, LANES), jnp.float32),
            pltpu.VMEM((7, NP * ES, LANES), jnp.float32),
            pltpu.VMEM((7, A0, A1 * A2), jnp.float32),
            pltpu.SemaphoreType.DMA((ROUNDS, WAYS)),
            pltpu.SemaphoreType.DMA((ROUNDS, WAYS)),
            pltpu.SemaphoreType.DMA((len(stages), PEERS)),
            pltpu.SemaphoreType.DMA((len(stages), PEERS)),
        ],
        compiler_params=pltpu.CompilerParams(
            collective_id=0, has_side_effects=True, vmem_limit_bytes=55168 * 1024
        ),
    )(*operands)


def solution(mesh):
    return jax.shard_map(
        functools.partial(shards, mesh.shape["dom"]),
        mesh=mesh,
        in_specs=(
            P(None, None, "dom", None),
            P(None, None, "dom", None),
            P(None, "dom", None),
            P("dom", None),
            P("dom"),
        ),
        out_specs=(P("dom", None), P("dom", None)),
        check_vma=False,
    )
```

```python
import functools

import jax
import jax.numpy as jnp
import numpy as np
from jax import lax
from jax.experimental import pallas as pl
from jax.experimental.pallas import tpu as pltpu
from jax.sharding import PartitionSpec as P

NP = 8
NF = 12
ES = 16
ITERS = 3
A0 = 8
A1 = 112
A2 = 8
ROUNDS = 5
WAYS = 6
PEERS = 32
LANES = 128
MESH = pl.DeviceIdType.MESH

time_step = 0.25
viscosity = 0.05
mass_shift = 0.001


def legendre_pair(points, order):
    before = np.ones(points.shape)
    current = points * 1.0
    for level in range(2, order + 1):
        nextone = ((2 * level - 1) * points * current - (level - 1) * before) / level
        before = current
        current = nextone
    return (current, before)


def jacobi_eigen(matrix):
    size = matrix.shape[0]
    work = matrix * 1.0
    vectors = np.eye(size)
    for sweep in range(30):
        for first in range(size - 1):
            for second in range(first + 1, size):
                off = float(work[first, second])
                if abs(off) > 1e-300:
                    tau = (float(work[second, second]) - float(work[first, first])) / (2.0 * off)
                    if tau >= 0.0:
                        tangent = 1.0 / (tau + (1.0 + tau * tau) ** 0.5)
                    else:
                        tangent = -1.0 / (-tau + (1.0 + tau * tau) ** 0.5)
                    cosine = 1.0 / (1.0 + tangent * tangent) ** 0.5
                    sine = tangent * cosine
                    rotation = np.eye(size)
                    rotation[first, first] = cosine
                    rotation[second, second] = cosine
                    rotation[first, second] = sine
                    rotation[second, first] = -sine
                    work = rotation.T @ work @ rotation
                    vectors = vectors @ rotation
    diagonal_index = np.arange(size)
    return (work[diagonal_index, diagonal_index], vectors)


def build_tables(points_edge, points_fine):
    degree = points_edge - 1
    points = -np.cos(np.pi * np.arange(points_edge) / degree)
    for sweep in range(100):
        top, below = legendre_pair(points, degree)
        points = points - (points * top - below) / (points_edge * top)
    top, below = legendre_pair(points, degree)
    weight_gll = 2.0 / (degree * points_edge * top**2)
    spacing = points[:, None] - points[None, :] + np.eye(points_edge)
    barycentric = 1.0 / np.prod(spacing, axis=1)
    derivative = barycentric[None, :] / barycentric[:, None] / spacing
    derivative = derivative * (1.0 - np.eye(points_edge))
    derivative = derivative - np.eye(points_edge) * derivative.sum(axis=1)[:, None]
    fine_points = np.cos(np.pi * (np.arange(points_fine) + 0.75) / (points_fine + 0.5))
    for sweep in range(100):
        top, below = legendre_pair(fine_points, points_fine)
        slope = points_fine * (fine_points * top - below) / (fine_points * fine_points - 1.0)
        fine_points = fine_points - top / slope
    top, below = legendre_pair(fine_points, points_fine)
    slope = points_fine * (fine_points * top - below) / (fine_points * fine_points - 1.0)
    fine_weight = 2.0 / ((1.0 - fine_points * fine_points) * slope * slope)
    fine_points = fine_points[::-1]
    fine_weight = fine_weight[::-1]
    interpolate = np.ones((points_fine, points_edge))
    for column in range(points_edge):
        for other in range(points_edge):
            if other != column:
                interpolate[:, column] = (
                    interpolate[:, column]
                    * (fine_points - points[other])
                    / (points[column] - points[other])
                )
    stiffness = derivative.T @ (weight_gll[:, None] * derivative)
    extent = 3 * degree + 1
    joined_stiff = np.zeros((extent, extent))
    joined_mass = np.zeros(extent)
    for segment in range(3):
        offset = segment * degree
        joined_stiff[offset : offset + points_edge, offset : offset + points_edge] += stiffness
        joined_mass[offset : offset + points_edge] += weight_gll
    low = degree - 1
    high = 2 * degree + 2
    root_mass = np.sqrt(joined_mass[low:high])
    scaled = joined_stiff[low:high, low:high] / root_mass[:, None] / root_mass[None, :]
    scaled = 0.5 * (scaled + scaled.T)
    eigen_values, eigen_vectors = jacobi_eigen(scaled)
    solve_mat = eigen_vectors / root_mass[:, None]
    breadth = high - low
    identity = np.eye(points_edge)
    operator_tables = {
        "derivative": derivative,
        "dpair": np.concatenate(
            [np.kron(derivative, identity).T, np.kron(identity, derivative).T], axis=1
        ),
        "interpolate": interpolate,
        "ipair": np.kron(interpolate, interpolate).T,
        "mass_three": (
            weight_gll[:, None, None] * weight_gll[None, :, None] * weight_gll[None, None, :]
        ).reshape(points_edge, points_edge * points_edge),
        "fine_three": (
            fine_weight[:, None, None] * fine_weight[None, :, None] * fine_weight[None, None, :]
        ).reshape(points_fine, points_fine * points_fine),
        "solve_mat": solve_mat,
        "solve_pair": np.kron(solve_mat, solve_mat),
        "eigen_axial": eigen_values,
        "eigen_around": np.repeat(eigen_values, breadth),
        "eigen_radial": np.tile(eigen_values, breadth),
    }
    operator_tables["weight"] = weight_gll
    operator_tables["fine_weight"] = fine_weight
    return operator_tables


def split_rows(matrix):
    exact = np.asarray(matrix, np.float32)
    high = exact.astype(jnp.bfloat16)
    low = (exact - high.astype(np.float32)).astype(jnp.bfloat16)
    columns = range(0, exact.shape[1], LANES)
    return np.concatenate([part[:, c : c + LANES] for c in columns for part in (high, low)])


def halves(matrix):
    rows, columns = matrix.shape
    table = np.zeros((rows // 2, columns // 2, 2, LANES))
    for out in range(rows // 2):
        for into in range(columns // 2):
            table[out, into, 0, :64] = matrix[2 * out, 2 * into]
            table[out, into, 0, 64:] = matrix[2 * out + 1, 2 * into + 1]
            table[out, into, 1, :64] = matrix[2 * out, 2 * into + 1]
            table[out, into, 1, 64:] = matrix[2 * out + 1, 2 * into]
    return np.asarray(table.reshape(-1, LANES), np.float32)


def twice(block, stride):
    rows, columns = block.shape
    result = np.zeros((2 * rows, 2 * stride))
    result[:rows, :columns] = block
    result[rows:, stride : stride + columns] = block
    return result


def pad_columns(matrix, total):
    return np.pad(matrix, ((0, 0), (0, total - matrix.shape[1])))


def by_tile(table):
    return np.asarray(np.repeat(table.reshape(-1, LANES), ES, axis=0), np.float32)


@functools.cache
def constants():
    t = build_tables(NP, NF)
    d, itp, s = t["derivative"], t["interpolate"], t["solve_mat"]
    eye = np.eye(NP)
    pair = np.concatenate(
        [twice(np.kron(d, eye).T, 64), twice(np.kron(eye, d).T, 64)], axis=1
    )
    fine = pad_columns(twice(np.kron(itp, itp).T, 144), 384)
    slope = itp @ d
    fine_slope = np.concatenate(
        [
            pad_columns(twice(np.kron(slope, itp).T, 144), 384),
            pad_columns(twice(np.kron(itp, slope).T, 144), 384),
        ],
        axis=1,
    )
    inner = s[1:9]
    ahead = np.zeros((2 * LANES, 2 * LANES))
    back = np.zeros((2 * LANES, 2 * LANES))
    for h in range(2):
        out = slice(h * LANES, h * LANES + 100)

        def lanes(row):
            return slice(h * 64 + row * 8, h * 64 + row * 8 + 8)

        def beside(row):
            return slice(LANES + h * 64 + row * 8, LANES + h * 64 + row * 8 + 8)

        for row in range(NP):
            ahead[lanes(row), out] = np.kron(s[row + 1 : row + 2], inner)
            back[lanes(row), out] = np.kron(s[row + 1 : row + 2], inner)
        ahead[beside(6), out] = np.kron(s[0:1], inner)
        ahead[beside(1), out] = np.kron(s[9:10], inner)
        back[beside(0), out] = np.kron(s[8:9], inner)
        back[beside(1), out] = np.kron(s[9:10], inner)
        back[beside(7), out] = np.kron(s[1:2], inner)
        back[beside(6), out] = np.kron(s[0:1], inner)
    wf = t["fine_weight"]
    wf2 = (wf[:, None] * wf[None, :]).reshape(-1)
    fine_mass = np.zeros((6, 384))
    for j in range(6):
        fine_mass[j, :144] = wf[2 * j] * wf2
        fine_mass[j, 144:288] = wf[2 * j + 1] * wf2
    eigen = np.zeros((2, LANES))
    eigen[0, :100] = t["eigen_around"]
    eigen[1, :100] = t["eigen_radial"]
    nodes = by_tile(t["mass_three"])
    weights = np.concatenate(
        [split_rows(m) for m in (pair, pair.T, fine, fine_slope, fine.T, ahead, back.T)]
    )
    along = np.concatenate([halves(d), halves(d.T), halves(itp), halves(slope), halves(itp.T), halves(d[[0, -1]].T)])
    fine_mass = np.repeat(fine_mass, ES, axis=0)
    tables = np.concatenate(
        [along, nodes]
        + [fine_mass[:, c : c + LANES] for c in range(0, 384, LANES)]
        + [np.pad(eigen, ((0, 6), (0, 0)))]
    )
    return (
        weights,
        np.asarray(tables, np.float32),
        np.asarray(s, np.float32),
        np.asarray(t["eigen_axial"], np.float32),
    )


PAIR = (0, 128, 256)
PAIR_T = (512, 256, 128)
FINE = (1024, 128, 384)
SLOPE = (1792, 128, 768)
FINE_T = (3328, 384, 128)
AHEAD = (4096, 256, 256)
BACK = (5120, 256, 256)
TABLE_NODES, TABLE_FINE, TABLE_EIGEN = 216, 280, 568
COEF_D, COEF_DT, COEF_I, COEF_S, COEF_IT, COEF_FACE = 0, 32, 64, 112, 160, 208


OPERANDS = 7


def stages_of(count):
    stages = []
    stride = 1
    while stride < count:
        size = min(PEERS, count // stride)
        while (count // stride) % size:
            size -= 1
        stages.append((stride, size))
        stride *= size
    return stages


def kernel(
    count,
    *refs,
):
    operands, refs = refs[:OPERANDS], refs[OPERANDS:]
    pressure_ref, residual_ref = refs[:2]
    held, refs = refs[2 : 2 + OPERANDS], refs[2 + OPERANDS :]
    (
        load_sem,
        early_out,
        early_in,
        early_third,
        main_out,
        main_in,
        main_second,
        main_third,
        outbox,
        inbox,
        inbox_far,
        gathered,
        turned,
        basis,
        send_sem,
        recv_sem,
        gather_send_sem,
        gather_recv_sem,
    ) = refs
    split = [(0, None)] * 5 + [(0, AHEAD[0]), (AHEAD[0], None), (0, None)]
    loads = []
    for i, (at, end) in enumerate(split):
        which = min(i, 5) if i < 7 else 6
        rows = slice(None) if i < 5 else pl.ds(at, (end or operands[which].shape[0]) - at)
        loads.append(
            pltpu.make_async_copy(
                operands[which].at[rows], held[which].at[rows], load_sem.at[i]
            )
        )
    for i in (3, 7, 4, 2, 0, 5, 1, 6):
        loads[i].start()
    velocity, past, metric, jacobian, slots, weights, tables = held

    _, _, solve, eigen_axial = constants()
    me = lax.axis_index("dom")
    left = lax.rem(me + count - 1, count)
    right = lax.rem(me + 1, count)
    far_left = lax.rem(me + count - 2, count)
    far_right = lax.rem(me + 2, count)
    third_left = lax.rem(me + count - 3, count)
    third_right = lax.rem(me + 3, count)
    stages = stages_of(count)

    def peer(stage, offset):
        stride, size = stages[stage]
        digit = lax.rem(me // stride, size)
        other = lax.rem(digit + offset, size)
        return me + (other - digit) * stride

    barrier = pltpu.get_barrier_semaphore()
    greeted = [left, right, far_left, far_right, third_left, third_right] + [
        peer(stage, offset)
        for stage in range(len(stages))
        for offset in range(1, stages[stage][1])
    ]
    for other in greeted:
        pl.semaphore_signal(barrier, inc=1, device_id=(other,), device_id_type=MESH)

    lane = lax.broadcasted_iota(jnp.int32, (ES, LANES), 1)
    low = lane < 64
    node_s = lax.rem(lane, 64) // 8

    def tiles(field):
        return [field[i * ES : (i + 1) * ES] for i in range(field.shape[0] // ES)]

    def stack(parts):
        return jnp.concatenate(parts, axis=0)

    def mm(x, w):
        high = x.astype(jnp.bfloat16)
        rest = (x - high.astype(jnp.float32)).astype(jnp.bfloat16)
        at, depth, width = w
        columns = []
        for c in range(width // LANES):
            top = weights[at + 2 * c * depth : at + (2 * c + 1) * depth]
            bottom = weights[at + (2 * c + 1) * depth : at + (2 * c + 2) * depth]
            columns.append(jnp.concatenate([top, top, bottom], axis=0))
        return jnp.dot(
            jnp.concatenate([high, rest, high], axis=1),
            jnp.concatenate(columns, axis=1),
            preferred_element_type=jnp.float32,
        )

    def swap(tile):
        return pltpu.roll(tile, 64, 1)

    def along(field, base, total):
        parts = tiles(field)
        swapped = [swap(part) for part in parts]
        results = []
        for out in range(total):
            acc = None
            for into in range(len(parts)):
                at = base + 2 * (out * len(parts) + into)
                term = tables[at : at + 1] * parts[into] + tables[at + 1 : at + 2] * swapped[into]
                acc = term if acc is None else acc + term
            results.append(acc)
        return stack(results)

    def gradient(field):
        paired = mm(field, PAIR)
        return along(field, COEF_D, 4), paired[:, :LANES], paired[:, LANES:]

    def gradient_t(axial, around, radial):
        paired = mm(jnp.concatenate([around, radial], axis=1), PAIR_T)
        return paired + along(axial, COEF_DT, 4)

    def before(tile):
        return pltpu.roll(tile, 1, 0)

    def after(tile):
        return pltpu.roll(tile, ES - 1, 0)

    def around_sum(field):
        results = []
        for tile in tiles(field):
            first = before(pltpu.roll(tile, 72, 1))
            last = after(pltpu.roll(tile, 56, 1))
            results.append(
                tile + jnp.where(node_s == 0, first, jnp.where(node_s == 7, last, 0.0))
            )
        return stack(results)

    def copies(step):
        if step == 0:
            face = early_out.at[pl.ds(0, ES)]
            plan = [
                (face, early_third.at[1], third_left),
                (face, early_third.at[0], third_right),
                (early_out, early_in.at[3], far_left),
                (early_out, early_in.at[0], far_right),
                (early_out, early_in.at[2], left),
                (early_out, early_in.at[1], right),
            ]
        elif step == 1:
            face = main_out.at[pl.ds(ES, ES)]
            plan = [
                (face, main_third.at[1], third_left),
                (face, main_third.at[0], third_right),
                (main_out.at[pl.ds(0, 4 * ES)], main_second.at[1], far_left),
                (main_out.at[pl.ds(ES, 4 * ES)], main_second.at[0], far_right),
                (main_out, main_in.at[1], left),
                (main_out, main_in.at[0], right),
            ]
        elif step < ROUNDS - 1:
            plan = [
                (outbox.at[step, pl.ds(0, ES)], inbox_far.at[step, 1], far_left),
                (outbox.at[step, pl.ds(3 * ES, ES)], inbox_far.at[step, 0], far_right),
                (outbox.at[step], inbox.at[step, 1], left),
                (outbox.at[step], inbox.at[step, 0], right),
            ]
        else:
            plan = [
                (outbox.at[step, pl.ds(0, ES)], inbox_far.at[step, 1], left),
                (outbox.at[step, pl.ds(3 * ES, ES)], inbox_far.at[step, 0], right),
            ]
        return [
            pltpu.make_async_remote_copy(
                src_ref=source,
                dst_ref=target,
                send_sem=send_sem.at[step, way],
                recv_sem=recv_sem.at[step, way],
                device_id=(other,),
                device_id_type=MESH,
            )
            for way, (source, target, other) in enumerate(plan)
        ]

    def send(step, field):
        outbox[step] = field
        for copy in copies(step):
            copy.start()

    def receive(step):
        for copy in copies(step):
            copy.wait_recv()

    def axial_sum(field, before_it, after_it):
        parts = tiles(field)
        return stack(
            [
                parts[0] + jnp.where(low, swap(before_it), 0.0),
                parts[1],
                parts[2],
                parts[3] + jnp.where(low, 0.0, swap(after_it)),
            ]
        )

    def surrounded(step, field):
        receive(step)
        beside = [inbox[step, 0], inbox[step, 1]]
        ends = [inbox_far[step, 0], inbox_far[step, 1]]
        own = axial_sum(field, beside[0][3 * ES :], beside[1][:ES])
        return own, beside, ends

    def element_field(ref, *index):
        return stack([ref[index + (slice(None), pl.ds(j * LANES, LANES))] for j in range(4)])

    def faces(field):
        return jnp.where(low, field[:ES], field[3 * ES :])

    def across(before_it, after_it):
        return jnp.where(low, swap(before_it), swap(after_it))

    loads[7].wait()
    loads[3].wait()
    weight3 = tables[TABLE_NODES:TABLE_FINE]
    fine_mass = jnp.concatenate(
        [tables[TABLE_FINE + 96 * c : TABLE_FINE + 96 * (c + 1)] for c in range(3)], axis=1
    )
    eigen = tables[TABLE_EIGEN:]
    jac = element_field(jacobian)
    mass = jac * weight3
    coarse = [along(jac, COEF_I, 6)]
    loads[2].wait()
    metrics = [element_field(metric, d) for d in range(3)]
    squares = [mass * m * m for m in metrics]
    loads[0].wait()
    newest = [element_field(velocity, 0, i) for i in range(3)]
    coarse += [along(newest[d] * metrics[d], COEF_I, 6) for d in range(3)]
    coarse += [along(newest[i], COEF_S, 6) for i in range(3)]
    loads[4].wait()
    position = lax.broadcasted_iota(jnp.int32, (ES, ES), 0)
    chosen = jnp.where(slots[...] == position, 1.0, 0.0)
    chosen = jnp.concatenate([chosen, chosen, chosen], axis=1).astype(jnp.bfloat16)

    def into_order(fields):
        wide = jnp.concatenate([tile for field in fields for tile in tiles(field)], axis=1)
        first = wide.astype(jnp.bfloat16)
        rest = wide - first.astype(jnp.float32)
        second = rest.astype(jnp.bfloat16)
        third = (rest - second.astype(jnp.float32)).astype(jnp.bfloat16)
        placed = jnp.dot(
            chosen, stack([first, second, third]), preferred_element_type=jnp.float32
        )
        return [
            stack([placed[:, (4 * f + j) * LANES : (4 * f + j + 1) * LANES] for j in range(4)])
            for f in range(len(fields))
        ]

    placed_mass, *placed_metrics = into_order([mass] + metrics)
    placed_lumps = [placed_mass * m for m in placed_metrics]
    placed_squares = [placed_lumps[d] * placed_metrics[d] for d in range(3)]

    def total(field):
        parts = tiles(field)
        return jnp.sum(parts[0] + parts[1] + parts[2] + parts[3], axis=1, keepdims=True) / 8.0

    flat = (
        total(placed_squares[1]) * eigen[0:1]
        + total(placed_squares[2]) * eigen[1:2]
        + mass_shift * total(placed_mass)
    )
    steep = jnp.broadcast_to(total(placed_squares[0]), (ES, LANES))
    mass_around = around_sum(placed_mass)
    early = [faces(mass_around)] + [faces(lump) for lump in placed_lumps] + [flat, steep]
    early_out[...] = stack(early)
    pl.semaphore_wait(barrier, len(greeted))
    for copy in copies(0):
        copy.start()

    loads[5].wait()
    fine = mm(stack(coarse), FINE)
    fine = [fine[i * 96 : (i + 1) * 96] for i in range(7)]
    crossed = mm(stack([along(newest[i], COEF_I, 6) for i in range(3)]), SLOPE)
    fine_jac = fine[0] * fine_mass
    products = []
    for i in range(3):
        rows = slice(i * 96, (i + 1) * 96)
        products.append(
            fine_jac
            * (
                fine[1] * fine[4 + i]
                + fine[2] * crossed[rows, :384]
                + fine[3] * crossed[rows, 384:]
            )
        )
    advected = mm(stack(products), FINE_T)
    guessed = [
        3.0 * newest[i] - 3.0 * element_field(velocity, 1, i) + element_field(velocity, 2, i)
        for i in range(3)
    ]
    paired = mm(stack(guessed), PAIR)
    slopes = jnp.concatenate(
        [
            stack([squares[1] * paired[i * 64 : (i + 1) * 64, :LANES] for i in range(3)]),
            stack([squares[2] * paired[i * 64 : (i + 1) * 64, LANES:] for i in range(3)]),
        ],
        axis=1,
    )
    paired_t = mm(slopes, PAIR_T)
    forcing = []
    loads[1].wait()
    for i in range(3):
        convect = along(advected[i * 96 : (i + 1) * 96], COEF_IT, 4)
        stiff = paired_t[i * 64 : (i + 1) * 64] + along(
            squares[0] * along(guessed[i], COEF_D, 4), COEF_DT, 4
        )
        history = (
            3.0 * newest[i]
            - 1.5 * element_field(velocity, 1, i)
            + element_field(velocity, 2, i) / 3.0
        )
        extrap = (
            3.0 * convect - 3.0 * element_field(past, 0, i) + element_field(past, 1, i)
        )
        helmholtz = viscosity * stiff + 11.0 / (6.0 * time_step) * mass * guessed[i]
        forcing.append(mass * history / time_step - extrap - helmholtz)

    (f0, f1, f2) = into_order(forcing)
    around = [around_sum(f) for f in (f0, f1, f2)]
    for copy in copies(0):
        copy.wait_recv()
    shown = [tiles(early_in[i]) for i in range(4)]
    shown = [shown[0], shown[1], early, shown[2], shown[3]]
    mass_faces = [early_third[0]] + [one[0] for one in shown] + [early_third[1]]
    total_mass = axial_sum(mass_around, mass_faces[2], mass_faces[4])
    accel = [placed_lumps[d] * (around[d] / total_mass) for d in range(3)]
    partial = gradient_t(accel[0], accel[1], accel[2])
    parts = tiles(partial)
    own_faces = [faces(f) for f in around]
    main_out[...] = stack([parts[0]] + own_faces + [parts[3], parts[1], parts[2]])
    for copy in copies(1):
        copy.start()
    loads[6].wait()
    lump_faces = []
    for b in range(5):
        ratio = mass_faces[b + 1] + across(mass_faces[b], mass_faces[b + 2])
        lump_faces.append([shown[b][1 + d] / ratio for d in range(3)])
    lefts, rights = shown[1], shown[3]
    flats = stack([lefts[4], flat, rights[4]])
    steeps = stack([lefts[5], steep, rights[5]])
    inverse = [1.0 / (steeps * float(eigen_axial[k]) + flats) for k in range(10)]
    for copy in copies(1):
        copy.wait_recv()
    lower, upper = tiles(main_in[0]), tiles(main_in[1])
    beyond = [tiles(main_second[0]), tiles(main_second[1])]
    none = jnp.zeros((ES, LANES), jnp.float32)
    force_faces = [
        [main_third[0], none, none],
        beyond[0][:3],
        lower[1:4],
        own_faces,
        upper[1:4],
        beyond[1][1:],
        [main_third[1], none, none],
    ]
    added = [
        [lump_faces[b][d] * across(force_faces[b][d], force_faces[b + 2][d]) for d in range(3)]
        for b in range(5)
    ]
    sides = tiles(
        mm(
            jnp.concatenate([stack([a[1] for a in added]), stack([a[2] for a in added])], axis=1),
            PAIR_T,
        )
    )
    whole = []
    for b in range(5):
        extra = tiles(along(added[b][0], COEF_FACE, 4))
        extra[0] = extra[0] + jnp.where(low, sides[b], 0.0)
        extra[3] = extra[3] + jnp.where(low, 0.0, sides[b])
        whole.append(extra)
    divergence = partial + stack(whole[2])
    beside = [
        around_sum(stack([near[0], near[5], near[6], near[4]]) + stack(extra))
        for near, extra in ((lower, whole[1]), (upper, whole[3]))
    ]
    ends = [around_sum(beyond[0][3] + whole[0][3]), around_sum(beyond[1][0] + whole[4][0])]
    source = axial_sum(around_sum(divergence), beside[0][3 * ES :], beside[1][:ES])

    def combine(weight, parts):
        acc = parts[0] * float(weight[0])
        for one, part in zip(weight[1:], parts[1:]):
            acc = acc + part * float(one)
        return acc

    def smooth(own, beside, ends):
        lower, upper = tiles(beside[0]), tiles(beside[1])
        lower[0] = lower[0] + jnp.where(low, swap(ends[0]), 0.0)
        upper[3] = upper[3] + jnp.where(low, 0.0, swap(ends[1]))
        parts = [jnp.where(low, ends[0], ends[1])] + lower + upper + tiles(own)
        sides = [
            jnp.where(node_s == 6, before(p), jnp.where(node_s == 1, after(p), 0.0))
            for p in parts
        ]
        modes = tiles(mm(jnp.concatenate([stack(parts), stack(sides)], axis=1), AHEAD))
        firsts = [-7, -5, -3, -1, 7, 9, 11, 13, 0, 2, 4, 6]
        grid = {-8: modes[0][:, :LANES], 15: modes[0][:, LANES:]}
        for row, mode in zip(firsts, modes[1:]):
            grid[row], grid[row + 1] = mode[:, :LANES], mode[:, LANES:]
        order = [stack([grid[a - 7], grid[a], grid[a + 7]]) for a in range(-1, 9)]
        spectra = [combine(solve[:, k], order) * inverse[k] for k in range(10)]
        slabs = [[spectrum[b * ES : (b + 1) * ES] for spectrum in spectra] for b in range(3)]
        rows = [combine(solve[a + 1], slabs[1]) for a in range(NP)]
        rows[0] = rows[0] + combine(solve[8], slabs[0])
        rows[1] = rows[1] + combine(solve[9], slabs[0])
        rows[6] = rows[6] + combine(solve[0], slabs[2])
        rows[7] = rows[7] + combine(solve[1], slabs[2])
        given = mm(jnp.concatenate([stack(rows[0::2]), stack(rows[1::2])], axis=1), BACK)
        return stack(
            [
                o + jnp.where(node_s <= 1, before(n), jnp.where(node_s >= 6, after(n), 0.0))
                for o, n in zip(tiles(given[:, :LANES]), tiles(given[:, LANES:]))
            ]
        )

    def apply(field):
        axial, around, radial = gradient(field)
        local = gradient_t(
            placed_squares[0] * axial, placed_squares[1] * around, placed_squares[2] * radial
        )
        return local + mass_shift * placed_mass * field

    def inner(one, two):
        return jnp.sum(one * two, axis=0, keepdims=True)

    def turn(which, field):
        for j, tile in enumerate(tiles(field)):
            turned[which, pl.ds(2 * j * ES, ES)] = tile
            turned[which, pl.ds((2 * j + 1) * ES, ES)] = swap(tile)
        for p in range(ES):
            block = turned[which, pl.ds(p, NP, stride=ES), :]
            basis[which, :, p * 56 : (p + 1) * 56] = block[:, :56]

    spaces, images, dots = [], [], {}
    current = source
    for it in range(ITERS):
        spaces.append(smooth(current, beside, ends))
        local = apply(spaces[-1])
        image = around_sum(local)
        send(2 + it, image)
        if it == 0:
            head = inner(divergence, spaces[0])
        for j in range(it + 1):
            dots[j, it] = inner(local, spaces[j])
        if it < ITERS - 1:
            turn(2 * it, spaces[it])
            if it == 0:
                turn(6, current)
            else:
                turn(2 * it - 1, current)
            current, beside, ends = surrounded(2 + it, image)
            images.append(current)

    value = jnp.concatenate(
        [head]
        + [dots[i, j] for i in range(3) for j in range(i, 3)]
        + [jnp.zeros((1, LANES), jnp.float32)],
        axis=0,
    )
    started = []
    for stage, (stride, size) in enumerate(stages):
        digit = lax.rem(me // stride, size)
        gathered[stage, digit] = value
        for offset in range(1, size):
            copy = pltpu.make_async_remote_copy(
                src_ref=gathered.at[stage, digit],
                dst_ref=gathered.at[stage, digit],
                send_sem=gather_send_sem.at[stage, offset],
                recv_sem=gather_recv_sem.at[stage, offset],
                device_id=(peer(stage, offset),),
                device_id_type=MESH,
            )
            copy.start()
            started.append(copy)
        if stage == 0:
            turn(4, spaces[2])
            turn(3, images[1])
            receive(ROUNDS - 1)
            ends = [inbox_far[ROUNDS - 1, 0], inbox_far[ROUNDS - 1, 1]]
            turn(5, axial_sum(image, ends[0], ends[1]))
        for copy in started[1 - size :]:
            copy.wait_recv()
        value = gathered[stage, 0]
        for slot in range(1, size):
            value = value + gathered[stage, slot]
    sums = jnp.sum(value, axis=1, keepdims=True)
    sums = [sums[i : i + 1] for i in range(7)]
    gram = {}
    for at, (i, j) in enumerate([(i, j) for i in range(3) for j in range(i, 3)]):
        gram[i, j] = gram[j, i] = sums[1 + at]
    heads = [sums[0], gram[0, 0], gram[0, 1]]
    taken = [None] * 3
    direction = [None] * 3
    result = [None] * 3
    previous = None
    for it in range(ITERS):
        z = [None] * 3
        z[0] = jnp.ones((1, 1), jnp.float32)
        for k in range(1, it + 1):
            z[k] = taken[k - 1]
        rho = heads[0]
        for k in range(1, it + 1):
            rho = rho + z[k] * heads[k]
        for i in range(it):
            row = gram[i, 0]
            for k in range(1, it + 1):
                row = row + z[k] * gram[i, k]
            rho = rho + taken[i] * row
        if it == 0:
            direction = [z[0], None, None]
        else:
            beta = rho / previous
            direction = [
                None if k > it else z[k] if direction[k] is None else z[k] + beta * direction[k]
                for k in range(3)
            ]
        bottom = None
        for i in range(it + 1):
            row = None
            for k in range(it + 1):
                term = direction[k] * gram[i, k]
                row = term if row is None else row + term
            bottom = direction[i] * row if bottom is None else bottom + direction[i] * row
        alpha = rho / bottom
        for k in range(it + 1):
            step = alpha * direction[k]
            result[k] = step if result[k] is None else result[k] + step
            taken[k] = -step if taken[k] is None else taken[k] - step
        previous = rho
    pressure_ref[...] = sum(basis[2 * k] * result[k] for k in range(3))
    residual_ref[...] = basis[6] + sum(basis[2 * k + 1] * taken[k] for k in range(3))

    for step in range(ROUNDS):
        for copy in copies(step):
            copy.wait_send()
    for copy in started:
        copy.wait_send()


def shards(count, velocity, conv_past, metric, jacobian, element_slot):
    weights, tables, _, _ = constants()
    stages = stages_of(count)
    block = jax.ShapeDtypeStruct((A0, A1 * A2), jnp.float32)
    whole = pl.BlockSpec(memory_space=pltpu.VMEM)
    slots = element_slot.reshape(1, ES)
    operands = [velocity, conv_past, metric, jacobian, slots]
    operands += [jnp.asarray(weights), jnp.asarray(tables)]
    return pl.pallas_call(
        functools.partial(kernel, count),
        out_shape=(block, block),
        in_specs=[pl.BlockSpec(memory_space=pltpu.HBM)] * len(operands),
        out_specs=(whole, whole),
        scratch_shapes=[pltpu.VMEM(x.shape, x.dtype) for x in operands]
        + [
            pltpu.SemaphoreType.DMA((len(operands) + 1,)),
            pltpu.VMEM((6 * ES, LANES), jnp.float32),
            pltpu.VMEM((4, 6 * ES, LANES), jnp.float32),
            pltpu.VMEM((2, ES, LANES), jnp.float32),
            pltpu.VMEM((7 * ES, LANES), jnp.float32),
            pltpu.VMEM((2, 7 * ES, LANES), jnp.float32),
            pltpu.VMEM((2, 4 * ES, LANES), jnp.float32),
            pltpu.VMEM((2, ES, LANES), jnp.float32),
            pltpu.VMEM((ROUNDS, 4 * ES, LANES), jnp.float32),
            pltpu.VMEM((ROUNDS, 2, 4 * ES, LANES), jnp.float32),
            pltpu.VMEM((ROUNDS, 2, ES, LANES), jnp.float32),
            pltpu.VMEM((len(stages), PEERS, 8, LANES), jnp.float32),
            pltpu.VMEM((7, NP * ES, LANES), jnp.float32),
            pltpu.VMEM((7, A0, A1 * A2), jnp.float32),
            pltpu.SemaphoreType.DMA((ROUNDS, WAYS)),
            pltpu.SemaphoreType.DMA((ROUNDS, WAYS)),
            pltpu.SemaphoreType.DMA((len(stages), PEERS)),
            pltpu.SemaphoreType.DMA((len(stages), PEERS)),
        ],
        compiler_params=pltpu.CompilerParams(
            collective_id=0, has_side_effects=True, vmem_limit_bytes=55168 * 1024
        ),
    )(*operands)


def solution(mesh):
    return jax.shard_map(
        functools.partial(shards, mesh.shape["dom"]),
        mesh=mesh,
        in_specs=(
            P(None, None, "dom", None),
            P(None, None, "dom", None),
            P(None, "dom", None),
            P("dom", None),
            P("dom"),
        ),
        out_specs=(P("dom", None), P("dom", None)),
        check_vma=False,
    )
```

```python
import functools

import jax
import jax.numpy as jnp
import numpy as np
from jax import lax
from jax.experimental import pallas as pl
from jax.experimental.pallas import tpu as pltpu
from jax.sharding import PartitionSpec as P

NP = 8
NF = 12
ES = 16
ITERS = 3
A0 = 8
A1 = 112
A2 = 8
ROUNDS = 5
WAYS = 4
PEERS = 32
LANES = 128
MESH = pl.DeviceIdType.MESH

time_step = 0.25
viscosity = 0.05
mass_shift = 0.001


def legendre_pair(points, order):
    before = np.ones(points.shape)
    current = points * 1.0
    for level in range(2, order + 1):
        nextone = ((2 * level - 1) * points * current - (level - 1) * before) / level
        before = current
        current = nextone
    return (current, before)


def jacobi_eigen(matrix):
    size = matrix.shape[0]
    work = matrix * 1.0
    vectors = np.eye(size)
    for sweep in range(30):
        for first in range(size - 1):
            for second in range(first + 1, size):
                off = float(work[first, second])
                if abs(off) > 1e-300:
                    tau = (float(work[second, second]) - float(work[first, first])) / (2.0 * off)
                    if tau >= 0.0:
                        tangent = 1.0 / (tau + (1.0 + tau * tau) ** 0.5)
                    else:
                        tangent = -1.0 / (-tau + (1.0 + tau * tau) ** 0.5)
                    cosine = 1.0 / (1.0 + tangent * tangent) ** 0.5
                    sine = tangent * cosine
                    rotation = np.eye(size)
                    rotation[first, first] = cosine
                    rotation[second, second] = cosine
                    rotation[first, second] = sine
                    rotation[second, first] = -sine
                    work = rotation.T @ work @ rotation
                    vectors = vectors @ rotation
    diagonal_index = np.arange(size)
    return (work[diagonal_index, diagonal_index], vectors)


def build_tables(points_edge, points_fine):
    degree = points_edge - 1
    points = -np.cos(np.pi * np.arange(points_edge) / degree)
    for sweep in range(100):
        top, below = legendre_pair(points, degree)
        points = points - (points * top - below) / (points_edge * top)
    top, below = legendre_pair(points, degree)
    weight_gll = 2.0 / (degree * points_edge * top**2)
    spacing = points[:, None] - points[None, :] + np.eye(points_edge)
    barycentric = 1.0 / np.prod(spacing, axis=1)
    derivative = barycentric[None, :] / barycentric[:, None] / spacing
    derivative = derivative * (1.0 - np.eye(points_edge))
    derivative = derivative - np.eye(points_edge) * derivative.sum(axis=1)[:, None]
    fine_points = np.cos(np.pi * (np.arange(points_fine) + 0.75) / (points_fine + 0.5))
    for sweep in range(100):
        top, below = legendre_pair(fine_points, points_fine)
        slope = points_fine * (fine_points * top - below) / (fine_points * fine_points - 1.0)
        fine_points = fine_points - top / slope
    top, below = legendre_pair(fine_points, points_fine)
    slope = points_fine * (fine_points * top - below) / (fine_points * fine_points - 1.0)
    fine_weight = 2.0 / ((1.0 - fine_points * fine_points) * slope * slope)
    fine_points = fine_points[::-1]
    fine_weight = fine_weight[::-1]
    interpolate = np.ones((points_fine, points_edge))
    for column in range(points_edge):
        for other in range(points_edge):
            if other != column:
                interpolate[:, column] = (
                    interpolate[:, column]
                    * (fine_points - points[other])
                    / (points[column] - points[other])
                )
    stiffness = derivative.T @ (weight_gll[:, None] * derivative)
    extent = 3 * degree + 1
    joined_stiff = np.zeros((extent, extent))
    joined_mass = np.zeros(extent)
    for segment in range(3):
        offset = segment * degree
        joined_stiff[offset : offset + points_edge, offset : offset + points_edge] += stiffness
        joined_mass[offset : offset + points_edge] += weight_gll
    low = degree - 1
    high = 2 * degree + 2
    root_mass = np.sqrt(joined_mass[low:high])
    scaled = joined_stiff[low:high, low:high] / root_mass[:, None] / root_mass[None, :]
    scaled = 0.5 * (scaled + scaled.T)
    eigen_values, eigen_vectors = jacobi_eigen(scaled)
    solve_mat = eigen_vectors / root_mass[:, None]
    breadth = high - low
    identity = np.eye(points_edge)
    operator_tables = {
        "derivative": derivative,
        "dpair": np.concatenate(
            [np.kron(derivative, identity).T, np.kron(identity, derivative).T], axis=1
        ),
        "interpolate": interpolate,
        "ipair": np.kron(interpolate, interpolate).T,
        "mass_three": (
            weight_gll[:, None, None] * weight_gll[None, :, None] * weight_gll[None, None, :]
        ).reshape(points_edge, points_edge * points_edge),
        "fine_three": (
            fine_weight[:, None, None] * fine_weight[None, :, None] * fine_weight[None, None, :]
        ).reshape(points_fine, points_fine * points_fine),
        "solve_mat": solve_mat,
        "solve_pair": np.kron(solve_mat, solve_mat),
        "eigen_axial": eigen_values,
        "eigen_around": np.repeat(eigen_values, breadth),
        "eigen_radial": np.tile(eigen_values, breadth),
    }
    operator_tables["weight"] = weight_gll
    operator_tables["fine_weight"] = fine_weight
    return operator_tables


def split_rows(matrix):
    exact = np.asarray(matrix, np.float32)
    high = exact.astype(jnp.bfloat16)
    low = (exact - high.astype(np.float32)).astype(jnp.bfloat16)
    columns = range(0, exact.shape[1], LANES)
    return np.concatenate([part[:, c : c + LANES] for c in columns for part in (high, low)])


def halves(matrix):
    rows, columns = matrix.shape
    table = np.zeros((rows // 2, columns // 2, 2, LANES))
    for out in range(rows // 2):
        for into in range(columns // 2):
            table[out, into, 0, :64] = matrix[2 * out, 2 * into]
            table[out, into, 0, 64:] = matrix[2 * out + 1, 2 * into + 1]
            table[out, into, 1, :64] = matrix[2 * out, 2 * into + 1]
            table[out, into, 1, 64:] = matrix[2 * out + 1, 2 * into]
    return np.asarray(table.reshape(-1, LANES), np.float32)


def twice(block, stride):
    rows, columns = block.shape
    result = np.zeros((2 * rows, 2 * stride))
    result[:rows, :columns] = block
    result[rows:, stride : stride + columns] = block
    return result


def pad_columns(matrix, total):
    return np.pad(matrix, ((0, 0), (0, total - matrix.shape[1])))


def by_tile(table):
    return np.asarray(np.repeat(table.reshape(-1, LANES), ES, axis=0), np.float32)


@functools.cache
def constants():
    t = build_tables(NP, NF)
    d, itp, s = t["derivative"], t["interpolate"], t["solve_mat"]
    eye = np.eye(NP)
    pair = np.concatenate(
        [twice(np.kron(d, eye).T, 64), twice(np.kron(eye, d).T, 64)], axis=1
    )
    fine = pad_columns(twice(np.kron(itp, itp).T, 144), 384)
    slope = itp @ d
    fine_slope = np.concatenate(
        [
            pad_columns(twice(np.kron(slope, itp).T, 144), 384),
            pad_columns(twice(np.kron(itp, slope).T, 144), 384),
        ],
        axis=1,
    )
    inner = s[1:9]
    ahead = np.zeros((2 * LANES, 2 * LANES))
    back = np.zeros((2 * LANES, 2 * LANES))
    for h in range(2):
        out = slice(h * LANES, h * LANES + 100)

        def lanes(row):
            return slice(h * 64 + row * 8, h * 64 + row * 8 + 8)

        def beside(row):
            return slice(LANES + h * 64 + row * 8, LANES + h * 64 + row * 8 + 8)

        for row in range(NP):
            ahead[lanes(row), out] = np.kron(s[row + 1 : row + 2], inner)
            back[lanes(row), out] = np.kron(s[row + 1 : row + 2], inner)
        ahead[beside(6), out] = np.kron(s[0:1], inner)
        ahead[beside(1), out] = np.kron(s[9:10], inner)
        back[beside(0), out] = np.kron(s[8:9], inner)
        back[beside(1), out] = np.kron(s[9:10], inner)
        back[beside(7), out] = np.kron(s[1:2], inner)
        back[beside(6), out] = np.kron(s[0:1], inner)
    wf = t["fine_weight"]
    wf2 = (wf[:, None] * wf[None, :]).reshape(-1)
    fine_mass = np.zeros((6, 384))
    for j in range(6):
        fine_mass[j, :144] = wf[2 * j] * wf2
        fine_mass[j, 144:288] = wf[2 * j + 1] * wf2
    eigen = np.zeros((2, LANES))
    eigen[0, :100] = t["eigen_around"]
    eigen[1, :100] = t["eigen_radial"]
    nodes = by_tile(t["mass_three"])
    weights = np.concatenate(
        [split_rows(m) for m in (pair, pair.T, fine, fine_slope, fine.T, ahead, back.T)]
    )
    along = np.concatenate([halves(d), halves(d.T), halves(itp), halves(slope), halves(itp.T)])
    fine_mass = np.repeat(fine_mass, ES, axis=0)
    tables = np.concatenate(
        [along, nodes]
        + [fine_mass[:, c : c + LANES] for c in range(0, 384, LANES)]
        + [np.pad(eigen, ((0, 6), (0, 0)))]
    )
    return (
        weights,
        np.asarray(tables, np.float32),
        np.asarray(s, np.float32),
        np.asarray(t["eigen_axial"], np.float32),
    )


PAIR = (0, 128, 256)
PAIR_T = (512, 256, 128)
FINE = (1024, 128, 384)
SLOPE = (1792, 128, 768)
FINE_T = (3328, 384, 128)
AHEAD = (4096, 256, 256)
BACK = (5120, 256, 256)
TABLE_NODES, TABLE_FINE, TABLE_EIGEN = 208, 272, 560
COEF_D, COEF_DT, COEF_I, COEF_S, COEF_IT = 0, 32, 64, 112, 160


OPERANDS = 7


def stages_of(count):
    stages = []
    stride = 1
    while stride < count:
        size = min(PEERS, count // stride)
        while (count // stride) % size:
            size -= 1
        stages.append((stride, size))
        stride *= size
    return stages


def kernel(
    count,
    *refs,
):
    operands, refs = refs[:OPERANDS], refs[OPERANDS:]
    pressure_ref, residual_ref = refs[:2]
    held, refs = refs[2 : 2 + OPERANDS], refs[2 + OPERANDS :]
    (
        load_sem,
        first_out,
        first_in,
        outbox,
        inbox,
        inbox_far,
        gathered,
        turned,
        basis,
        send_sem,
        recv_sem,
        gather_send_sem,
        gather_recv_sem,
    ) = refs
    split = [(0, None)] * 5 + [(0, AHEAD[0]), (AHEAD[0], None), (0, None)]
    loads = []
    for i, (at, end) in enumerate(split):
        which = min(i, 5) if i < 7 else 6
        rows = slice(None) if i < 5 else pl.ds(at, (end or operands[which].shape[0]) - at)
        loads.append(
            pltpu.make_async_copy(
                operands[which].at[rows], held[which].at[rows], load_sem.at[i]
            )
        )
    for i in (3, 2, 0, 7, 5, 1, 4, 6):
        loads[i].start()
    velocity, past, metric, jacobian, slots, weights, tables = held

    _, _, solve, eigen_axial = constants()
    me = lax.axis_index("dom")
    left = lax.rem(me + count - 1, count)
    right = lax.rem(me + 1, count)
    far_left = lax.rem(me + count - 2, count)
    far_right = lax.rem(me + 2, count)
    stages = stages_of(count)

    def peer(stage, offset):
        stride, size = stages[stage]
        digit = lax.rem(me // stride, size)
        other = lax.rem(digit + offset, size)
        return me + (other - digit) * stride

    barrier = pltpu.get_barrier_semaphore()
    greeted = [left, right, far_left, far_right] + [
        peer(stage, offset)
        for stage in range(len(stages))
        for offset in range(1, stages[stage][1])
    ]
    for other in greeted:
        pl.semaphore_signal(barrier, inc=1, device_id=(other,), device_id_type=MESH)

    lane = lax.broadcasted_iota(jnp.int32, (ES, LANES), 1)
    low = lane < 64
    node_s = lax.rem(lane, 64) // 8

    def tiles(field):
        return [field[i * ES : (i + 1) * ES] for i in range(field.shape[0] // ES)]

    def stack(parts):
        return jnp.concatenate(parts, axis=0)

    def mm(x, w):
        high = x.astype(jnp.bfloat16)
        rest = (x - high.astype(jnp.float32)).astype(jnp.bfloat16)
        at, depth, width = w
        columns = []
        for c in range(width // LANES):
            top = weights[at + 2 * c * depth : at + (2 * c + 1) * depth]
            bottom = weights[at + (2 * c + 1) * depth : at + (2 * c + 2) * depth]
            columns.append(jnp.concatenate([top, top, bottom], axis=0))
        return jnp.dot(
            jnp.concatenate([high, rest, high], axis=1),
            jnp.concatenate(columns, axis=1),
            preferred_element_type=jnp.float32,
        )

    def swap(tile):
        return pltpu.roll(tile, 64, 1)

    def along(field, base, total):
        parts = tiles(field)
        swapped = [swap(part) for part in parts]
        results = []
        for out in range(total):
            acc = None
            for into in range(len(parts)):
                at = base + 2 * (out * len(parts) + into)
                term = tables[at : at + 1] * parts[into] + tables[at + 1 : at + 2] * swapped[into]
                acc = term if acc is None else acc + term
            results.append(acc)
        return stack(results)

    def gradient(field):
        paired = mm(field, PAIR)
        return along(field, COEF_D, 4), paired[:, :LANES], paired[:, LANES:]

    def gradient_t(axial, around, radial):
        paired = mm(jnp.concatenate([around, radial], axis=1), PAIR_T)
        return paired + along(axial, COEF_DT, 4)

    def before(tile):
        return pltpu.roll(tile, 1, 0)

    def after(tile):
        return pltpu.roll(tile, ES - 1, 0)

    def around_sum(field):
        results = []
        for tile in tiles(field):
            first = before(pltpu.roll(tile, 72, 1))
            last = after(pltpu.roll(tile, 56, 1))
            results.append(
                tile + jnp.where(node_s == 0, first, jnp.where(node_s == 7, last, 0.0))
            )
        return stack(results)

    def copies(step):
        if step == 0:
            plan = [(first_out.at[0], first_in.at[1], left), (first_out.at[1], first_in.at[0], right)]
        elif step < ROUNDS - 1:
            plan = [
                (outbox.at[step, pl.ds(0, ES)], inbox_far.at[step, 1], far_left),
                (outbox.at[step, pl.ds(3 * ES, ES)], inbox_far.at[step, 0], far_right),
                (outbox.at[step], inbox.at[step, 1], left),
                (outbox.at[step], inbox.at[step, 0], right),
            ]
        else:
            plan = [
                (outbox.at[step, pl.ds(0, ES)], inbox_far.at[step, 1], left),
                (outbox.at[step, pl.ds(3 * ES, ES)], inbox_far.at[step, 0], right),
            ]
        return [
            pltpu.make_async_remote_copy(
                src_ref=source,
                dst_ref=target,
                send_sem=send_sem.at[step, way],
                recv_sem=recv_sem.at[step, way],
                device_id=(other,),
                device_id_type=MESH,
            )
            for way, (source, target, other) in enumerate(plan)
        ]

    def send(step, field):
        outbox[step] = field
        for copy in copies(step):
            copy.start()

    def receive(step):
        for copy in copies(step):
            copy.wait_recv()

    def axial_sum(field, before_it, after_it):
        parts = tiles(field)
        return stack(
            [
                parts[0] + jnp.where(low, swap(before_it), 0.0),
                parts[1],
                parts[2],
                parts[3] + jnp.where(low, 0.0, swap(after_it)),
            ]
        )

    def surrounded(step, field):
        receive(step)
        beside = [inbox[step, 0], inbox[step, 1]]
        ends = [inbox_far[step, 0], inbox_far[step, 1]]
        own = axial_sum(field, beside[0][3 * ES :], beside[1][:ES])
        return own, beside, ends

    def element_field(ref, *index):
        return stack([ref[index + (slice(None), pl.ds(j * LANES, LANES))] for j in range(4)])

    loads[7].wait()
    loads[3].wait()
    weight3 = tables[TABLE_NODES:TABLE_FINE]
    fine_mass = jnp.concatenate(
        [tables[TABLE_FINE + 96 * c : TABLE_FINE + 96 * (c + 1)] for c in range(3)], axis=1
    )
    eigen = tables[TABLE_EIGEN:]
    jac = element_field(jacobian)
    mass = jac * weight3
    coarse = [along(jac, COEF_I, 6)]
    loads[2].wait()
    metrics = [element_field(metric, d) for d in range(3)]
    squares = [mass * m * m for m in metrics]
    loads[0].wait()
    newest = [element_field(velocity, 0, i) for i in range(3)]
    coarse += [along(newest[d] * metrics[d], COEF_I, 6) for d in range(3)]
    coarse += [along(newest[i], COEF_S, 6) for i in range(3)]
    loads[5].wait()
    fine = mm(stack(coarse), FINE)
    fine = [fine[i * 96 : (i + 1) * 96] for i in range(7)]
    crossed = mm(stack([along(newest[i], COEF_I, 6) for i in range(3)]), SLOPE)
    fine_jac = fine[0] * fine_mass
    products = []
    for i in range(3):
        rows = slice(i * 96, (i + 1) * 96)
        products.append(
            fine_jac
            * (
                fine[1] * fine[4 + i]
                + fine[2] * crossed[rows, :384]
                + fine[3] * crossed[rows, 384:]
            )
        )
    advected = mm(stack(products), FINE_T)
    guessed = [
        3.0 * newest[i] - 3.0 * element_field(velocity, 1, i) + element_field(velocity, 2, i)
        for i in range(3)
    ]
    paired = mm(stack(guessed), PAIR)
    slopes = jnp.concatenate(
        [
            stack([squares[1] * paired[i * 64 : (i + 1) * 64, :LANES] for i in range(3)]),
            stack([squares[2] * paired[i * 64 : (i + 1) * 64, LANES:] for i in range(3)]),
        ],
        axis=1,
    )
    paired_t = mm(slopes, PAIR_T)
    forcing = []
    loads[1].wait()
    loads[4].wait()
    for i in range(3):
        convect = along(advected[i * 96 : (i + 1) * 96], COEF_IT, 4)
        stiff = paired_t[i * 64 : (i + 1) * 64] + along(
            squares[0] * along(guessed[i], COEF_D, 4), COEF_DT, 4
        )
        history = (
            3.0 * newest[i]
            - 1.5 * element_field(velocity, 1, i)
            + element_field(velocity, 2, i) / 3.0
        )
        extrap = (
            3.0 * convect - 3.0 * element_field(past, 0, i) + element_field(past, 1, i)
        )
        helmholtz = viscosity * stiff + 11.0 / (6.0 * time_step) * mass * guessed[i]
        forcing.append(mass * history / time_step - extrap - helmholtz)

    fields = forcing + [mass] + metrics
    wide = jnp.concatenate([tile for field in fields for tile in tiles(field)], axis=1)
    first = wide.astype(jnp.bfloat16)
    rest = wide - first.astype(jnp.float32)
    second = rest.astype(jnp.bfloat16)
    third = (rest - second.astype(jnp.float32)).astype(jnp.bfloat16)
    position = lax.broadcasted_iota(jnp.int32, (ES, ES), 0)
    chosen = jnp.where(slots[...] == position, 1.0, 0.0)
    chosen = jnp.concatenate([chosen, chosen, chosen], axis=1).astype(jnp.bfloat16)
    placed = jnp.dot(chosen, stack([first, second, third]), preferred_element_type=jnp.float32)
    fields = [
        stack([placed[:, (4 * f + j) * LANES : (4 * f + j + 1) * LANES] for j in range(4)])
        for f in range(7)
    ]
    forcing, mass, metrics = fields[:3], fields[3], fields[4:]
    lumps = [mass * m for m in metrics]
    squares = [lumps[d] * metrics[d] for d in range(3)]

    def total(field):
        parts = tiles(field)
        return jnp.sum(parts[0] + parts[1] + parts[2] + parts[3], axis=1, keepdims=True) / 8.0

    flat = (
        total(squares[1]) * eigen[0:1]
        + total(squares[2]) * eigen[1:2]
        + mass_shift * total(mass)
    )
    steep = jnp.broadcast_to(total(squares[0]), (ES, LANES))

    around = [around_sum(f) for f in forcing + [mass]]
    first_out[0] = stack([f[:ES] for f in around] + [flat, steep])
    first_out[1] = stack([f[3 * ES :] for f in around] + [flat, steep])
    pl.semaphore_wait(barrier, len(greeted))
    for copy in copies(0):
        copy.start()
    receive(0)
    lefts, rights = tiles(first_in[0]), tiles(first_in[1])
    summed = [axial_sum(around[f], lefts[f], rights[f]) for f in range(4)]
    accel = [lumps[d] * (summed[d] / summed[3]) for d in range(3)]
    divergence = gradient_t(accel[0], accel[1], accel[2])
    source = around_sum(divergence)
    send(1, source)
    loads[6].wait()
    flats = stack([lefts[4], flat, rights[4]])
    steeps = stack([lefts[5], steep, rights[5]])
    inverse = [1.0 / (steeps * float(eigen_axial[k]) + flats) for k in range(10)]
    source, beside, ends = surrounded(1, source)

    def combine(weight, parts):
        acc = parts[0] * float(weight[0])
        for one, part in zip(weight[1:], parts[1:]):
            acc = acc + part * float(one)
        return acc

    def smooth(own, beside, ends):
        lower, upper = tiles(beside[0]), tiles(beside[1])
        lower[0] = lower[0] + jnp.where(low, swap(ends[0]), 0.0)
        upper[3] = upper[3] + jnp.where(low, 0.0, swap(ends[1]))
        parts = [jnp.where(low, ends[0], ends[1])] + lower + upper + tiles(own)
        sides = [
            jnp.where(node_s == 6, before(p), jnp.where(node_s == 1, after(p), 0.0))
            for p in parts
        ]
        modes = tiles(mm(jnp.concatenate([stack(parts), stack(sides)], axis=1), AHEAD))
        firsts = [-7, -5, -3, -1, 7, 9, 11, 13, 0, 2, 4, 6]
        grid = {-8: modes[0][:, :LANES], 15: modes[0][:, LANES:]}
        for row, mode in zip(firsts, modes[1:]):
            grid[row], grid[row + 1] = mode[:, :LANES], mode[:, LANES:]
        order = [stack([grid[a - 7], grid[a], grid[a + 7]]) for a in range(-1, 9)]
        spectra = [combine(solve[:, k], order) * inverse[k] for k in range(10)]
        slabs = [[spectrum[b * ES : (b + 1) * ES] for spectrum in spectra] for b in range(3)]
        rows = [combine(solve[a + 1], slabs[1]) for a in range(NP)]
        rows[0] = rows[0] + combine(solve[8], slabs[0])
        rows[1] = rows[1] + combine(solve[9], slabs[0])
        rows[6] = rows[6] + combine(solve[0], slabs[2])
        rows[7] = rows[7] + combine(solve[1], slabs[2])
        given = mm(jnp.concatenate([stack(rows[0::2]), stack(rows[1::2])], axis=1), BACK)
        return stack(
            [
                o + jnp.where(node_s <= 1, before(n), jnp.where(node_s >= 6, after(n), 0.0))
                for o, n in zip(tiles(given[:, :LANES]), tiles(given[:, LANES:]))
            ]
        )

    def apply(field):
        axial, around, radial = gradient(field)
        local = gradient_t(squares[0] * axial, squares[1] * around, squares[2] * radial)
        return local + mass_shift * mass * field

    def inner(one, two):
        return jnp.sum(one * two, axis=0, keepdims=True)

    def turn(which, field):
        for j, tile in enumerate(tiles(field)):
            turned[which, pl.ds(2 * j * ES, ES)] = tile
            turned[which, pl.ds((2 * j + 1) * ES, ES)] = swap(tile)
        for p in range(ES):
            block = turned[which, pl.ds(p, NP, stride=ES), :]
            basis[which, :, p * 56 : (p + 1) * 56] = block[:, :56]

    spaces, images, dots = [], [], {}
    current = source
    for it in range(ITERS):
        spaces.append(smooth(current, beside, ends))
        local = apply(spaces[-1])
        image = around_sum(local)
        send(2 + it, image)
        if it == 0:
            head = inner(divergence, spaces[0])
        for j in range(it + 1):
            dots[j, it] = inner(local, spaces[j])
        if it < ITERS - 1:
            turn(2 * it, spaces[it])
            if it == 0:
                turn(6, current)
            else:
                turn(2 * it - 1, current)
            current, beside, ends = surrounded(2 + it, image)
            images.append(current)

    value = jnp.concatenate(
        [head]
        + [dots[i, j] for i in range(3) for j in range(i, 3)]
        + [jnp.zeros((1, LANES), jnp.float32)],
        axis=0,
    )
    sums = jnp.sum(value, axis=1, keepdims=True)
    row8 = lax.broadcasted_iota(jnp.int32, (8, LANES), 0)
    lane8 = lax.broadcasted_iota(jnp.int32, (8, LANES), 1)
    value = jnp.sum(jnp.where(row8 == lane8, sums, 0.0), axis=0, keepdims=True)
    started = []
    for stage, (stride, size) in enumerate(stages):
        digit = lax.rem(me // stride, size)
        slot = gathered.at[stage, pl.ds(digit, 1)]
        slot[...] = value
        for offset in range(1, size):
            copy = pltpu.make_async_remote_copy(
                src_ref=slot,
                dst_ref=slot,
                send_sem=gather_send_sem.at[stage, offset],
                recv_sem=gather_recv_sem.at[stage, offset],
                device_id=(peer(stage, offset),),
                device_id_type=MESH,
            )
            copy.start()
            started.append(copy)
        if stage == 0:
            turn(4, spaces[2])
            turn(3, images[1])
            receive(ROUNDS - 1)
            ends = [inbox_far[ROUNDS - 1, 0], inbox_far[ROUNDS - 1, 1]]
            turn(5, axial_sum(image, ends[0], ends[1]))
        for copy in started[1 - size :]:
            copy.wait_recv()
        value = jnp.sum(gathered[stage, :size], axis=0, keepdims=True)
    sums = [value[:, i : i + 1] for i in range(7)]
    gram = {}
    for at, (i, j) in enumerate([(i, j) for i in range(3) for j in range(i, 3)]):
        gram[i, j] = gram[j, i] = sums[1 + at]
    heads = [sums[0], gram[0, 0], gram[0, 1]]
    taken = [None] * 3
    direction = [None] * 3
    result = [None] * 3
    previous = None
    for it in range(ITERS):
        z = [None] * 3
        z[0] = jnp.ones((1, 1), jnp.float32)
        for k in range(1, it + 1):
            z[k] = taken[k - 1]
        rho = heads[0]
        for k in range(1, it + 1):
            rho = rho + z[k] * heads[k]
        for i in range(it):
            row = gram[i, 0]
            for k in range(1, it + 1):
                row = row + z[k] * gram[i, k]
            rho = rho + taken[i] * row
        if it == 0:
            direction = [z[0], None, None]
        else:
            beta = rho / previous
            direction = [
                None if k > it else z[k] if direction[k] is None else z[k] + beta * direction[k]
                for k in range(3)
            ]
        bottom = None
        for i in range(it + 1):
            row = None
            for k in range(it + 1):
                term = direction[k] * gram[i, k]
                row = term if row is None else row + term
            bottom = direction[i] * row if bottom is None else bottom + direction[i] * row
        alpha = rho / bottom
        for k in range(it + 1):
            step = alpha * direction[k]
            result[k] = step if result[k] is None else result[k] + step
            taken[k] = -step if taken[k] is None else taken[k] - step
        previous = rho
    pressure_ref[...] = sum(basis[2 * k] * result[k] for k in range(3))
    residual_ref[...] = basis[6] + sum(basis[2 * k + 1] * taken[k] for k in range(3))

    for step in range(ROUNDS):
        for copy in copies(step):
            copy.wait_send()
    for copy in started:
        copy.wait_send()


def shards(count, velocity, conv_past, metric, jacobian, element_slot):
    weights, tables, _, _ = constants()
    stages = stages_of(count)
    block = jax.ShapeDtypeStruct((A0, A1 * A2), jnp.float32)
    whole = pl.BlockSpec(memory_space=pltpu.VMEM)
    slots = element_slot.reshape(1, ES)
    operands = [velocity, conv_past, metric, jacobian, slots]
    operands += [jnp.asarray(weights), jnp.asarray(tables)]
    return pl.pallas_call(
        functools.partial(kernel, count),
        out_shape=(block, block),
        in_specs=[pl.BlockSpec(memory_space=pltpu.HBM)] * len(operands),
        out_specs=(whole, whole),
        scratch_shapes=[pltpu.VMEM(x.shape, x.dtype) for x in operands]
        + [
            pltpu.SemaphoreType.DMA((len(operands) + 1,)),
            pltpu.VMEM((2, 6 * ES, LANES), jnp.float32),
            pltpu.VMEM((2, 6 * ES, LANES), jnp.float32),
            pltpu.VMEM((ROUNDS, 4 * ES, LANES), jnp.float32),
            pltpu.VMEM((ROUNDS, 2, 4 * ES, LANES), jnp.float32),
            pltpu.VMEM((ROUNDS, 2, ES, LANES), jnp.float32),
            pltpu.VMEM((len(stages), PEERS, LANES), jnp.float32),
            pltpu.VMEM((7, NP * ES, LANES), jnp.float32),
            pltpu.VMEM((7, A0, A1 * A2), jnp.float32),
            pltpu.SemaphoreType.DMA((ROUNDS, WAYS)),
            pltpu.SemaphoreType.DMA((ROUNDS, WAYS)),
            pltpu.SemaphoreType.DMA((len(stages), PEERS)),
            pltpu.SemaphoreType.DMA((len(stages), PEERS)),
        ],
        compiler_params=pltpu.CompilerParams(
            collective_id=0, has_side_effects=True, vmem_limit_bytes=55168 * 1024
        ),
    )(*operands)


def solution(mesh):
    return jax.shard_map(
        functools.partial(shards, mesh.shape["dom"]),
        mesh=mesh,
        in_specs=(
            P(None, None, "dom", None),
            P(None, None, "dom", None),
            P(None, "dom", None),
            P("dom", None),
            P("dom"),
        ),
        out_specs=(P("dom", None), P("dom", None)),
        check_vma=False,
    )
```

```python
import functools

import jax
import jax.numpy as jnp
import numpy as np
from jax import lax
from jax.experimental import pallas as pl
from jax.experimental.pallas import tpu as pltpu
from jax.sharding import PartitionSpec as P

NP = 8
NF = 12
ES = 16
ITERS = 3
A0 = 8
A1 = 112
A2 = 8
ROUNDS = 5
WAYS = 6
PEERS = 32
LANES = 128
MESH = pl.DeviceIdType.MESH

time_step = 0.25
viscosity = 0.05
mass_shift = 0.001


def legendre_pair(points, order):
    before = np.ones(points.shape)
    current = points * 1.0
    for level in range(2, order + 1):
        nextone = ((2 * level - 1) * points * current - (level - 1) * before) / level
        before = current
        current = nextone
    return (current, before)


def jacobi_eigen(matrix):
    size = matrix.shape[0]
    work = matrix * 1.0
    vectors = np.eye(size)
    for sweep in range(30):
        for first in range(size - 1):
            for second in range(first + 1, size):
                off = float(work[first, second])
                if abs(off) > 1e-300:
                    tau = (float(work[second, second]) - float(work[first, first])) / (2.0 * off)
                    if tau >= 0.0:
                        tangent = 1.0 / (tau + (1.0 + tau * tau) ** 0.5)
                    else:
                        tangent = -1.0 / (-tau + (1.0 + tau * tau) ** 0.5)
                    cosine = 1.0 / (1.0 + tangent * tangent) ** 0.5
                    sine = tangent * cosine
                    rotation = np.eye(size)
                    rotation[first, first] = cosine
                    rotation[second, second] = cosine
                    rotation[first, second] = sine
                    rotation[second, first] = -sine
                    work = rotation.T @ work @ rotation
                    vectors = vectors @ rotation
    diagonal_index = np.arange(size)
    return (work[diagonal_index, diagonal_index], vectors)


def build_tables(points_edge, points_fine):
    degree = points_edge - 1
    points = -np.cos(np.pi * np.arange(points_edge) / degree)
    for sweep in range(100):
        top, below = legendre_pair(points, degree)
        points = points - (points * top - below) / (points_edge * top)
    top, below = legendre_pair(points, degree)
    weight_gll = 2.0 / (degree * points_edge * top**2)
    spacing = points[:, None] - points[None, :] + np.eye(points_edge)
    barycentric = 1.0 / np.prod(spacing, axis=1)
    derivative = barycentric[None, :] / barycentric[:, None] / spacing
    derivative = derivative * (1.0 - np.eye(points_edge))
    derivative = derivative - np.eye(points_edge) * derivative.sum(axis=1)[:, None]
    fine_points = np.cos(np.pi * (np.arange(points_fine) + 0.75) / (points_fine + 0.5))
    for sweep in range(100):
        top, below = legendre_pair(fine_points, points_fine)
        slope = points_fine * (fine_points * top - below) / (fine_points * fine_points - 1.0)
        fine_points = fine_points - top / slope
    top, below = legendre_pair(fine_points, points_fine)
    slope = points_fine * (fine_points * top - below) / (fine_points * fine_points - 1.0)
    fine_weight = 2.0 / ((1.0 - fine_points * fine_points) * slope * slope)
    fine_points = fine_points[::-1]
    fine_weight = fine_weight[::-1]
    interpolate = np.ones((points_fine, points_edge))
    for column in range(points_edge):
        for other in range(points_edge):
            if other != column:
                interpolate[:, column] = (
                    interpolate[:, column]
                    * (fine_points - points[other])
                    / (points[column] - points[other])
                )
    stiffness = derivative.T @ (weight_gll[:, None] * derivative)
    extent = 3 * degree + 1
    joined_stiff = np.zeros((extent, extent))
    joined_mass = np.zeros(extent)
    for segment in range(3):
        offset = segment * degree
        joined_stiff[offset : offset + points_edge, offset : offset + points_edge] += stiffness
        joined_mass[offset : offset + points_edge] += weight_gll
    low = degree - 1
    high = 2 * degree + 2
    root_mass = np.sqrt(joined_mass[low:high])
    scaled = joined_stiff[low:high, low:high] / root_mass[:, None] / root_mass[None, :]
    scaled = 0.5 * (scaled + scaled.T)
    eigen_values, eigen_vectors = jacobi_eigen(scaled)
    solve_mat = eigen_vectors / root_mass[:, None]
    breadth = high - low
    identity = np.eye(points_edge)
    operator_tables = {
        "derivative": derivative,
        "dpair": np.concatenate(
            [np.kron(derivative, identity).T, np.kron(identity, derivative).T], axis=1
        ),
        "interpolate": interpolate,
        "ipair": np.kron(interpolate, interpolate).T,
        "mass_three": (
            weight_gll[:, None, None] * weight_gll[None, :, None] * weight_gll[None, None, :]
        ).reshape(points_edge, points_edge * points_edge),
        "fine_three": (
            fine_weight[:, None, None] * fine_weight[None, :, None] * fine_weight[None, None, :]
        ).reshape(points_fine, points_fine * points_fine),
        "solve_mat": solve_mat,
        "solve_pair": np.kron(solve_mat, solve_mat),
        "eigen_axial": eigen_values,
        "eigen_around": np.repeat(eigen_values, breadth),
        "eigen_radial": np.tile(eigen_values, breadth),
    }
    operator_tables["weight"] = weight_gll
    operator_tables["fine_weight"] = fine_weight
    return operator_tables


def split_rows(matrix):
    exact = np.asarray(matrix, np.float32)
    high = exact.astype(jnp.bfloat16)
    low = (exact - high.astype(np.float32)).astype(jnp.bfloat16)
    columns = range(0, exact.shape[1], LANES)
    return np.concatenate([part[:, c : c + LANES] for c in columns for part in (high, low)])


def halves(matrix):
    rows, columns = matrix.shape
    table = np.zeros((rows // 2, columns // 2, 2, LANES))
    for out in range(rows // 2):
        for into in range(columns // 2):
            table[out, into, 0, :64] = matrix[2 * out, 2 * into]
            table[out, into, 0, 64:] = matrix[2 * out + 1, 2 * into + 1]
            table[out, into, 1, :64] = matrix[2 * out, 2 * into + 1]
            table[out, into, 1, 64:] = matrix[2 * out + 1, 2 * into]
    return np.asarray(table.reshape(-1, LANES), np.float32)


def twice(block, stride):
    rows, columns = block.shape
    result = np.zeros((2 * rows, 2 * stride))
    result[:rows, :columns] = block
    result[rows:, stride : stride + columns] = block
    return result


def pad_columns(matrix, total):
    return np.pad(matrix, ((0, 0), (0, total - matrix.shape[1])))


def by_tile(table):
    return np.asarray(np.repeat(table.reshape(-1, LANES), ES, axis=0), np.float32)


@functools.cache
def constants():
    t = build_tables(NP, NF)
    d, itp, s = t["derivative"], t["interpolate"], t["solve_mat"]
    eye = np.eye(NP)
    pair = np.concatenate(
        [twice(np.kron(d, eye).T, 64), twice(np.kron(eye, d).T, 64)], axis=1
    )
    fine = pad_columns(twice(np.kron(itp, itp).T, 144), 384)
    slope = itp @ d
    fine_slope = np.concatenate(
        [
            pad_columns(twice(np.kron(slope, itp).T, 144), 384),
            pad_columns(twice(np.kron(itp, slope).T, 144), 384),
        ],
        axis=1,
    )
    inner = s[1:9]
    ahead = np.zeros((2 * LANES, 2 * LANES))
    back = np.zeros((2 * LANES, 2 * LANES))
    for h in range(2):
        out = slice(h * LANES, h * LANES + 100)

        def lanes(row):
            return slice(h * 64 + row * 8, h * 64 + row * 8 + 8)

        def beside(row):
            return slice(LANES + h * 64 + row * 8, LANES + h * 64 + row * 8 + 8)

        for row in range(NP):
            ahead[lanes(row), out] = np.kron(s[row + 1 : row + 2], inner)
            back[lanes(row), out] = np.kron(s[row + 1 : row + 2], inner)
        ahead[beside(6), out] = np.kron(s[0:1], inner)
        ahead[beside(1), out] = np.kron(s[9:10], inner)
        back[beside(0), out] = np.kron(s[8:9], inner)
        back[beside(1), out] = np.kron(s[9:10], inner)
        back[beside(7), out] = np.kron(s[1:2], inner)
        back[beside(6), out] = np.kron(s[0:1], inner)
    wf = t["fine_weight"]
    wf2 = (wf[:, None] * wf[None, :]).reshape(-1)
    fine_mass = np.zeros((6, 384))
    for j in range(6):
        fine_mass[j, :144] = wf[2 * j] * wf2
        fine_mass[j, 144:288] = wf[2 * j + 1] * wf2
    eigen = np.zeros((2, LANES))
    eigen[0, :100] = t["eigen_around"]
    eigen[1, :100] = t["eigen_radial"]
    nodes = by_tile(t["mass_three"])
    weights = np.concatenate(
        [split_rows(m) for m in (pair, pair.T, fine, fine_slope, fine.T, ahead, back.T)]
    )
    along = np.concatenate([halves(d), halves(d.T), halves(itp), halves(slope), halves(itp.T), halves(d[[0, -1]].T)])
    fine_mass = np.repeat(fine_mass, ES, axis=0)
    tables = np.concatenate(
        [along, nodes]
        + [fine_mass[:, c : c + LANES] for c in range(0, 384, LANES)]
        + [np.pad(eigen, ((0, 6), (0, 0)))]
    )
    return (
        weights,
        np.asarray(tables, np.float32),
        np.asarray(s, np.float32),
        np.asarray(t["eigen_axial"], np.float32),
    )


PAIR = (0, 128, 256)
PAIR_T = (512, 256, 128)
FINE = (1024, 128, 384)
SLOPE = (1792, 128, 768)
FINE_T = (3328, 384, 128)
AHEAD = (4096, 256, 256)
BACK = (5120, 256, 256)
TABLE_NODES, TABLE_FINE, TABLE_EIGEN = 216, 280, 568
COEF_D, COEF_DT, COEF_I, COEF_S, COEF_IT, COEF_FACE = 0, 32, 64, 112, 160, 208


OPERANDS = 7


def stages_of(count):
    stages = []
    stride = 1
    while stride < count:
        size = min(PEERS, count // stride)
        while (count // stride) % size:
            size -= 1
        stages.append((stride, size))
        stride *= size
    return stages


def kernel(
    count,
    *refs,
):
    operands, refs = refs[:OPERANDS], refs[OPERANDS:]
    pressure_ref, residual_ref = refs[:2]
    held, refs = refs[2 : 2 + OPERANDS], refs[2 + OPERANDS :]
    (
        load_sem,
        early_out,
        early_in,
        early_third,
        mass_in,
        main_out,
        main_in,
        main_second,
        main_third,
        outbox,
        inbox,
        inbox_far,
        gathered,
        turned,
        basis,
        send_sem,
        recv_sem,
        gather_send_sem,
        gather_recv_sem,
    ) = refs
    split = [(0, None)] * 5 + [(0, AHEAD[0]), (AHEAD[0], None), (0, None)]
    loads = []
    for i, (at, end) in enumerate(split):
        which = min(i, 5) if i < 7 else 6
        rows = slice(None) if i < 5 else pl.ds(at, (end or operands[which].shape[0]) - at)
        loads.append(
            pltpu.make_async_copy(
                operands[which].at[rows], held[which].at[rows], load_sem.at[i]
            )
        )
    for i in (3, 7, 4, 2, 0, 5, 1, 6):
        loads[i].start()
    velocity, past, metric, jacobian, slots, weights, tables = held

    _, _, solve, eigen_axial = constants()
    me = lax.axis_index("dom")
    left = lax.rem(me + count - 1, count)
    right = lax.rem(me + 1, count)
    far_left = lax.rem(me + count - 2, count)
    far_right = lax.rem(me + 2, count)
    third_left = lax.rem(me + count - 3, count)
    third_right = lax.rem(me + 3, count)
    stages = stages_of(count)

    def peer(stage, offset):
        stride, size = stages[stage]
        digit = lax.rem(me // stride, size)
        other = lax.rem(digit + offset, size)
        return me + (other - digit) * stride

    barrier = pltpu.get_barrier_semaphore()
    greeted = [left, right, far_left, far_right, third_left, third_right] + [
        peer(stage, offset)
        for stage in range(len(stages))
        for offset in range(1, stages[stage][1])
    ]
    for other in greeted:
        pl.semaphore_signal(barrier, inc=1, device_id=(other,), device_id_type=MESH)

    lane = lax.broadcasted_iota(jnp.int32, (ES, LANES), 1)
    low = lane < 64
    node_s = lax.rem(lane, 64) // 8

    def tiles(field):
        return [field[i * ES : (i + 1) * ES] for i in range(field.shape[0] // ES)]

    def stack(parts):
        return jnp.concatenate(parts, axis=0)

    def mm(x, w):
        high = x.astype(jnp.bfloat16)
        rest = (x - high.astype(jnp.float32)).astype(jnp.bfloat16)
        at, depth, width = w
        columns = []
        for c in range(width // LANES):
            top = weights[at + 2 * c * depth : at + (2 * c + 1) * depth]
            bottom = weights[at + (2 * c + 1) * depth : at + (2 * c + 2) * depth]
            columns.append(jnp.concatenate([top, top, bottom], axis=0))
        return jnp.dot(
            jnp.concatenate([high, rest, high], axis=1),
            jnp.concatenate(columns, axis=1),
            preferred_element_type=jnp.float32,
        )

    def swap(tile):
        return pltpu.roll(tile, 64, 1)

    def along(field, base, total):
        parts = tiles(field)
        swapped = [swap(part) for part in parts]
        results = []
        for out in range(total):
            acc = None
            for into in range(len(parts)):
                at = base + 2 * (out * len(parts) + into)
                term = tables[at : at + 1] * parts[into] + tables[at + 1 : at + 2] * swapped[into]
                acc = term if acc is None else acc + term
            results.append(acc)
        return stack(results)

    def gradient(field):
        paired = mm(field, PAIR)
        return along(field, COEF_D, 4), paired[:, :LANES], paired[:, LANES:]

    def gradient_t(axial, around, radial):
        paired = mm(jnp.concatenate([around, radial], axis=1), PAIR_T)
        return paired + along(axial, COEF_DT, 4)

    def before(tile):
        return pltpu.roll(tile, 1, 0)

    def after(tile):
        return pltpu.roll(tile, ES - 1, 0)

    def around_sum(field):
        results = []
        for tile in tiles(field):
            first = before(pltpu.roll(tile, 72, 1))
            last = after(pltpu.roll(tile, 56, 1))
            results.append(
                tile + jnp.where(node_s == 0, first, jnp.where(node_s == 7, last, 0.0))
            )
        return stack(results)

    def copies(step):
        if step == 0:
            face = early_out.at[pl.ds(0, ES)]
            plan = [
                (face, early_third.at[1], third_left),
                (face, early_third.at[0], third_right),
                (early_out, early_in.at[3], far_left),
                (early_out, early_in.at[0], far_right),
                (early_out, early_in.at[2], left),
                (early_out, early_in.at[1], right),
            ]
        elif step == ROUNDS:
            face = early_out.at[pl.ds(0, ES)]
            plan = [(face, mass_in.at[1], left), (face, mass_in.at[0], right)]
        elif step == 1:
            face = main_out.at[pl.ds(ES, ES)]
            plan = [
                (face, main_third.at[1], third_left),
                (face, main_third.at[0], third_right),
                (main_out.at[pl.ds(0, 4 * ES)], main_second.at[1], far_left),
                (main_out.at[pl.ds(ES, 4 * ES)], main_second.at[0], far_right),
                (main_out, main_in.at[1], left),
                (main_out, main_in.at[0], right),
            ]
        elif step < ROUNDS - 1:
            plan = [
                (outbox.at[step, pl.ds(0, ES)], inbox_far.at[step, 1], far_left),
                (outbox.at[step, pl.ds(3 * ES, ES)], inbox_far.at[step, 0], far_right),
                (outbox.at[step], inbox.at[step, 1], left),
                (outbox.at[step], inbox.at[step, 0], right),
            ]
        else:
            plan = [
                (outbox.at[step, pl.ds(0, ES)], inbox_far.at[step, 1], left),
                (outbox.at[step, pl.ds(3 * ES, ES)], inbox_far.at[step, 0], right),
            ]
        return [
            pltpu.make_async_remote_copy(
                src_ref=source,
                dst_ref=target,
                send_sem=send_sem.at[step, way],
                recv_sem=recv_sem.at[step, way],
                device_id=(other,),
                device_id_type=MESH,
            )
            for way, (source, target, other) in enumerate(plan)
        ]

    def send(step, field):
        outbox[step] = field
        for copy in copies(step):
            copy.start()

    def receive(step):
        for copy in copies(step):
            copy.wait_recv()

    def axial_sum(field, before_it, after_it):
        parts = tiles(field)
        return stack(
            [
                parts[0] + jnp.where(low, swap(before_it), 0.0),
                parts[1],
                parts[2],
                parts[3] + jnp.where(low, 0.0, swap(after_it)),
            ]
        )

    def surrounded(step, field):
        receive(step)
        beside = [inbox[step, 0], inbox[step, 1]]
        ends = [inbox_far[step, 0], inbox_far[step, 1]]
        own = axial_sum(field, beside[0][3 * ES :], beside[1][:ES])
        return own, beside, ends

    def element_field(ref, *index):
        return stack([ref[index + (slice(None), pl.ds(j * LANES, LANES))] for j in range(4)])

    def faces(field):
        return jnp.where(low, field[:ES], field[3 * ES :])

    def across(before_it, after_it):
        return jnp.where(low, swap(before_it), swap(after_it))

    loads[7].wait()
    loads[3].wait()
    weight3 = tables[TABLE_NODES:TABLE_FINE]
    fine_mass = jnp.concatenate(
        [tables[TABLE_FINE + 96 * c : TABLE_FINE + 96 * (c + 1)] for c in range(3)], axis=1
    )
    eigen = tables[TABLE_EIGEN:]
    jac = element_field(jacobian)
    mass = jac * weight3
    loads[2].wait()
    metrics = [element_field(metric, d) for d in range(3)]
    loads[4].wait()
    position = lax.broadcasted_iota(jnp.int32, (ES, ES), 0)
    chosen = jnp.where(slots[...] == position, 1.0, 0.0)
    chosen = jnp.concatenate([chosen, chosen, chosen], axis=1).astype(jnp.bfloat16)

    def into_order(fields):
        wide = jnp.concatenate([tile for field in fields for tile in tiles(field)], axis=1)
        first = wide.astype(jnp.bfloat16)
        rest = wide - first.astype(jnp.float32)
        second = rest.astype(jnp.bfloat16)
        third = (rest - second.astype(jnp.float32)).astype(jnp.bfloat16)
        placed = jnp.dot(
            chosen, stack([first, second, third]), preferred_element_type=jnp.float32
        )
        return [
            stack([placed[:, (4 * f + j) * LANES : (4 * f + j + 1) * LANES] for j in range(4)])
            for f in range(len(fields))
        ]

    placed_mass, *placed_metrics = into_order([mass] + metrics)
    placed_lumps = [placed_mass * m for m in placed_metrics]
    placed_squares = [placed_lumps[d] * placed_metrics[d] for d in range(3)]

    def total(field):
        parts = tiles(field)
        return jnp.sum(parts[0] + parts[1] + parts[2] + parts[3], axis=1, keepdims=True) / 8.0

    flat = (
        total(placed_squares[1]) * eigen[0:1]
        + total(placed_squares[2]) * eigen[1:2]
        + mass_shift * total(placed_mass)
    )
    steep = jnp.broadcast_to(total(placed_squares[0]), (ES, LANES))
    mass_around = around_sum(placed_mass)
    early = [faces(mass_around)] + [faces(lump) for lump in placed_lumps] + [flat, steep]
    early_out[...] = stack(early)
    pl.semaphore_wait(barrier, len(greeted))
    for copy in copies(ROUNDS) + copies(0):
        copy.start()

    coarse = [along(jac, COEF_I, 6)]
    squares = [mass * m * m for m in metrics]
    loads[0].wait()
    newest = [element_field(velocity, 0, i) for i in range(3)]
    coarse += [along(newest[d] * metrics[d], COEF_I, 6) for d in range(3)]
    coarse += [along(newest[i], COEF_S, 6) for i in range(3)]
    loads[5].wait()
    fine = mm(stack(coarse), FINE)
    fine = [fine[i * 96 : (i + 1) * 96] for i in range(7)]
    crossed = mm(stack([along(newest[i], COEF_I, 6) for i in range(3)]), SLOPE)
    fine_jac = fine[0] * fine_mass
    products = []
    for i in range(3):
        rows = slice(i * 96, (i + 1) * 96)
        products.append(
            fine_jac
            * (
                fine[1] * fine[4 + i]
                + fine[2] * crossed[rows, :384]
                + fine[3] * crossed[rows, 384:]
            )
        )
    advected = mm(stack(products), FINE_T)
    guessed = [
        3.0 * newest[i] - 3.0 * element_field(velocity, 1, i) + element_field(velocity, 2, i)
        for i in range(3)
    ]
    paired = mm(stack(guessed), PAIR)
    slopes = jnp.concatenate(
        [
            stack([squares[1] * paired[i * 64 : (i + 1) * 64, :LANES] for i in range(3)]),
            stack([squares[2] * paired[i * 64 : (i + 1) * 64, LANES:] for i in range(3)]),
        ],
        axis=1,
    )
    paired_t = mm(slopes, PAIR_T)
    forcing = []
    loads[1].wait()
    for i in range(3):
        convect = along(advected[i * 96 : (i + 1) * 96], COEF_IT, 4)
        stiff = paired_t[i * 64 : (i + 1) * 64] + along(
            squares[0] * along(guessed[i], COEF_D, 4), COEF_DT, 4
        )
        history = (
            3.0 * newest[i]
            - 1.5 * element_field(velocity, 1, i)
            + element_field(velocity, 2, i) / 3.0
        )
        extrap = (
            3.0 * convect - 3.0 * element_field(past, 0, i) + element_field(past, 1, i)
        )
        helmholtz = viscosity * stiff + 11.0 / (6.0 * time_step) * mass * guessed[i]
        forcing.append(mass * history / time_step - extrap - helmholtz)

    (f0, f1, f2) = into_order(forcing)
    around = [around_sum(f) for f in (f0, f1, f2)]
    for copy in copies(ROUNDS):
        copy.wait_recv()
    total_mass = axial_sum(mass_around, mass_in[0], mass_in[1])
    accel = [placed_lumps[d] * (around[d] / total_mass) for d in range(3)]
    partial = gradient_t(accel[0], accel[1], accel[2])
    parts = tiles(partial)
    own_faces = [faces(f) for f in around]
    main_out[...] = stack([parts[0]] + own_faces + [parts[3], parts[1], parts[2]])
    for copy in copies(1):
        copy.start()
    for copy in copies(0):
        copy.wait_recv()
    shown = [tiles(early_in[i]) for i in range(4)]
    shown = [shown[0], shown[1], early, shown[2], shown[3]]
    mass_faces = [early_third[0]] + [one[0] for one in shown] + [early_third[1]]
    loads[6].wait()
    lump_faces = []
    for b in range(5):
        ratio = mass_faces[b + 1] + across(mass_faces[b], mass_faces[b + 2])
        lump_faces.append([shown[b][1 + d] / ratio for d in range(3)])
    lefts, rights = shown[1], shown[3]
    flats = stack([lefts[4], flat, rights[4]])
    steeps = stack([lefts[5], steep, rights[5]])
    inverse = [1.0 / (steeps * float(eigen_axial[k]) + flats) for k in range(10)]
    for copy in copies(1):
        copy.wait_recv()
    lower, upper = tiles(main_in[0]), tiles(main_in[1])
    beyond = [tiles(main_second[0]), tiles(main_second[1])]
    none = jnp.zeros((ES, LANES), jnp.float32)
    force_faces = [
        [main_third[0], none, none],
        beyond[0][:3],
        lower[1:4],
        own_faces,
        upper[1:4],
        beyond[1][1:],
        [main_third[1], none, none],
    ]
    added = [
        [lump_faces[b][d] * across(force_faces[b][d], force_faces[b + 2][d]) for d in range(3)]
        for b in range(5)
    ]
    sides = tiles(
        mm(
            jnp.concatenate([stack([a[1] for a in added]), stack([a[2] for a in added])], axis=1),
            PAIR_T,
        )
    )
    whole = []
    for b in range(5):
        extra = tiles(along(added[b][0], COEF_FACE, 4))
        extra[0] = extra[0] + jnp.where(low, sides[b], 0.0)
        extra[3] = extra[3] + jnp.where(low, 0.0, sides[b])
        whole.append(extra)
    divergence = partial + stack(whole[2])
    beside = [
        around_sum(stack([near[0], near[5], near[6], near[4]]) + stack(extra))
        for near, extra in ((lower, whole[1]), (upper, whole[3]))
    ]
    ends = [around_sum(beyond[0][3] + whole[0][3]), around_sum(beyond[1][0] + whole[4][0])]
    source = axial_sum(around_sum(divergence), beside[0][3 * ES :], beside[1][:ES])

    def combine(weight, parts):
        acc = parts[0] * float(weight[0])
        for one, part in zip(weight[1:], parts[1:]):
            acc = acc + part * float(one)
        return acc

    def smooth(own, beside, ends):
        lower, upper = tiles(beside[0]), tiles(beside[1])
        lower[0] = lower[0] + jnp.where(low, swap(ends[0]), 0.0)
        upper[3] = upper[3] + jnp.where(low, 0.0, swap(ends[1]))
        parts = [jnp.where(low, ends[0], ends[1])] + lower + upper + tiles(own)
        sides = [
            jnp.where(node_s == 6, before(p), jnp.where(node_s == 1, after(p), 0.0))
            for p in parts
        ]
        modes = tiles(mm(jnp.concatenate([stack(parts), stack(sides)], axis=1), AHEAD))
        firsts = [-7, -5, -3, -1, 7, 9, 11, 13, 0, 2, 4, 6]
        grid = {-8: modes[0][:, :LANES], 15: modes[0][:, LANES:]}
        for row, mode in zip(firsts, modes[1:]):
            grid[row], grid[row + 1] = mode[:, :LANES], mode[:, LANES:]
        order = [stack([grid[a - 7], grid[a], grid[a + 7]]) for a in range(-1, 9)]
        spectra = [combine(solve[:, k], order) * inverse[k] for k in range(10)]
        slabs = [[spectrum[b * ES : (b + 1) * ES] for spectrum in spectra] for b in range(3)]
        rows = [combine(solve[a + 1], slabs[1]) for a in range(NP)]
        rows[0] = rows[0] + combine(solve[8], slabs[0])
        rows[1] = rows[1] + combine(solve[9], slabs[0])
        rows[6] = rows[6] + combine(solve[0], slabs[2])
        rows[7] = rows[7] + combine(solve[1], slabs[2])
        given = mm(jnp.concatenate([stack(rows[0::2]), stack(rows[1::2])], axis=1), BACK)
        return stack(
            [
                o + jnp.where(node_s <= 1, before(n), jnp.where(node_s >= 6, after(n), 0.0))
                for o, n in zip(tiles(given[:, :LANES]), tiles(given[:, LANES:]))
            ]
        )

    def apply(field):
        axial, around, radial = gradient(field)
        local = gradient_t(
            placed_squares[0] * axial, placed_squares[1] * around, placed_squares[2] * radial
        )
        return local + mass_shift * placed_mass * field

    def inner(one, two):
        return jnp.sum(one * two, axis=0, keepdims=True)

    def turn(which, field):
        for j, tile in enumerate(tiles(field)):
            turned[which, pl.ds(2 * j * ES, ES)] = tile
            turned[which, pl.ds((2 * j + 1) * ES, ES)] = swap(tile)
        for p in range(ES):
            block = turned[which, pl.ds(p, NP, stride=ES), :]
            basis[which, :, p * 56 : (p + 1) * 56] = block[:, :56]

    spaces, images, dots = [], [], {}
    current = source
    for it in range(ITERS):
        spaces.append(smooth(current, beside, ends))
        local = apply(spaces[-1])
        image = around_sum(local)
        send(2 + it, image)
        if it == 0:
            head = inner(divergence, spaces[0])
        for j in range(it + 1):
            dots[j, it] = inner(local, spaces[j])
        if it < ITERS - 1:
            turn(2 * it, spaces[it])
            if it == 0:
                turn(6, current)
            else:
                turn(2 * it - 1, current)
            current, beside, ends = surrounded(2 + it, image)
            images.append(current)

    value = jnp.concatenate(
        [head]
        + [dots[i, j] for i in range(3) for j in range(i, 3)]
        + [jnp.zeros((1, LANES), jnp.float32)],
        axis=0,
    )
    sums = jnp.sum(value, axis=1, keepdims=True)
    row8 = lax.broadcasted_iota(jnp.int32, (8, LANES), 0)
    lane8 = lax.broadcasted_iota(jnp.int32, (8, LANES), 1)
    value = jnp.sum(jnp.where(row8 == lane8, sums, 0.0), axis=0, keepdims=True)
    started = []
    for stage, (stride, size) in enumerate(stages):
        digit = lax.rem(me // stride, size)
        slot = gathered.at[stage, pl.ds(digit, 1)]
        slot[...] = value
        for offset in range(1, size):
            copy = pltpu.make_async_remote_copy(
                src_ref=slot,
                dst_ref=slot,
                send_sem=gather_send_sem.at[stage, offset],
                recv_sem=gather_recv_sem.at[stage, offset],
                device_id=(peer(stage, offset),),
                device_id_type=MESH,
            )
            copy.start()
            started.append(copy)
        if stage == 0:
            turn(4, spaces[2])
            turn(3, images[1])
            receive(ROUNDS - 1)
            ends = [inbox_far[ROUNDS - 1, 0], inbox_far[ROUNDS - 1, 1]]
            turn(5, axial_sum(image, ends[0], ends[1]))
        for copy in started[1 - size :]:
            copy.wait_recv()
        value = jnp.sum(gathered[stage, :size], axis=0, keepdims=True)
    sums = [value[:, i : i + 1] for i in range(7)]
    gram = {}
    for at, (i, j) in enumerate([(i, j) for i in range(3) for j in range(i, 3)]):
        gram[i, j] = gram[j, i] = sums[1 + at]
    heads = [sums[0], gram[0, 0], gram[0, 1]]
    taken = [None] * 3
    direction = [None] * 3
    result = [None] * 3
    previous = None
    for it in range(ITERS):
        z = [None] * 3
        z[0] = jnp.ones((1, 1), jnp.float32)
        for k in range(1, it + 1):
            z[k] = taken[k - 1]
        rho = heads[0]
        for k in range(1, it + 1):
            rho = rho + z[k] * heads[k]
        for i in range(it):
            row = gram[i, 0]
            for k in range(1, it + 1):
                row = row + z[k] * gram[i, k]
            rho = rho + taken[i] * row
        if it == 0:
            direction = [z[0], None, None]
        else:
            beta = rho / previous
            direction = [
                None if k > it else z[k] if direction[k] is None else z[k] + beta * direction[k]
                for k in range(3)
            ]
        bottom = None
        for i in range(it + 1):
            row = None
            for k in range(it + 1):
                term = direction[k] * gram[i, k]
                row = term if row is None else row + term
            bottom = direction[i] * row if bottom is None else bottom + direction[i] * row
        alpha = rho / bottom
        for k in range(it + 1):
            step = alpha * direction[k]
            result[k] = step if result[k] is None else result[k] + step
            taken[k] = -step if taken[k] is None else taken[k] - step
        previous = rho
    pressure_ref[...] = sum(basis[2 * k] * result[k] for k in range(3))
    residual_ref[...] = basis[6] + sum(basis[2 * k + 1] * taken[k] for k in range(3))

    for step in range(ROUNDS + 1):
        for copy in copies(step):
            copy.wait_send()
    for copy in started:
        copy.wait_send()


def shards(count, velocity, conv_past, metric, jacobian, element_slot):
    weights, tables, _, _ = constants()
    stages = stages_of(count)
    block = jax.ShapeDtypeStruct((A0, A1 * A2), jnp.float32)
    whole = pl.BlockSpec(memory_space=pltpu.VMEM)
    slots = element_slot.reshape(1, ES)
    operands = [velocity, conv_past, metric, jacobian, slots]
    operands += [jnp.asarray(weights), jnp.asarray(tables)]
    return pl.pallas_call(
        functools.partial(kernel, count),
        out_shape=(block, block),
        in_specs=[pl.BlockSpec(memory_space=pltpu.HBM)] * len(operands),
        out_specs=(whole, whole),
        scratch_shapes=[pltpu.VMEM(x.shape, x.dtype) for x in operands]
        + [
            pltpu.SemaphoreType.DMA((len(operands) + 1,)),
            pltpu.VMEM((6 * ES, LANES), jnp.float32),
            pltpu.VMEM((4, 6 * ES, LANES), jnp.float32),
            pltpu.VMEM((2, ES, LANES), jnp.float32),
            pltpu.VMEM((2, ES, LANES), jnp.float32),
            pltpu.VMEM((7 * ES, LANES), jnp.float32),
            pltpu.VMEM((2, 7 * ES, LANES), jnp.float32),
            pltpu.VMEM((2, 4 * ES, LANES), jnp.float32),
            pltpu.VMEM((2, ES, LANES), jnp.float32),
            pltpu.VMEM((ROUNDS, 4 * ES, LANES), jnp.float32),
            pltpu.VMEM((ROUNDS, 2, 4 * ES, LANES), jnp.float32),
            pltpu.VMEM((ROUNDS, 2, ES, LANES), jnp.float32),
            pltpu.VMEM((len(stages), PEERS, LANES), jnp.float32),
            pltpu.VMEM((7, NP * ES, LANES), jnp.float32),
            pltpu.VMEM((7, A0, A1 * A2), jnp.float32),
            pltpu.SemaphoreType.DMA((ROUNDS + 1, WAYS)),
            pltpu.SemaphoreType.DMA((ROUNDS + 1, WAYS)),
            pltpu.SemaphoreType.DMA((len(stages), PEERS)),
            pltpu.SemaphoreType.DMA((len(stages), PEERS)),
        ],
        compiler_params=pltpu.CompilerParams(
            collective_id=0, has_side_effects=True, vmem_limit_bytes=55168 * 1024
        ),
    )(*operands)


def solution(mesh):
    return jax.shard_map(
        functools.partial(shards, mesh.shape["dom"]),
        mesh=mesh,
        in_specs=(
            P(None, None, "dom", None),
            P(None, None, "dom", None),
            P(None, "dom", None),
            P("dom", None),
            P("dom"),
        ),
        out_specs=(P("dom", None), P("dom", None)),
        check_vma=False,
    )
```

```python
import functools

import jax
import jax.numpy as jnp
import numpy as np
from jax import lax
from jax.experimental import pallas as pl
from jax.experimental.pallas import tpu as pltpu
from jax.sharding import PartitionSpec as P

NP = 8
NF = 12
ES = 16
ITERS = 3
A0 = 8
A1 = 112
A2 = 8
ROUNDS = 5
WAYS = 6
PEERS = 32
LANES = 128
MESH = pl.DeviceIdType.MESH

time_step = 0.25
viscosity = 0.05
mass_shift = 0.001


def legendre_pair(points, order):
    before = np.ones(points.shape)
    current = points * 1.0
    for level in range(2, order + 1):
        nextone = ((2 * level - 1) * points * current - (level - 1) * before) / level
        before = current
        current = nextone
    return (current, before)


def jacobi_eigen(matrix):
    size = matrix.shape[0]
    work = matrix * 1.0
    vectors = np.eye(size)
    for sweep in range(30):
        for first in range(size - 1):
            for second in range(first + 1, size):
                off = float(work[first, second])
                if abs(off) > 1e-300:
                    tau = (float(work[second, second]) - float(work[first, first])) / (2.0 * off)
                    if tau >= 0.0:
                        tangent = 1.0 / (tau + (1.0 + tau * tau) ** 0.5)
                    else:
                        tangent = -1.0 / (-tau + (1.0 + tau * tau) ** 0.5)
                    cosine = 1.0 / (1.0 + tangent * tangent) ** 0.5
                    sine = tangent * cosine
                    rotation = np.eye(size)
                    rotation[first, first] = cosine
                    rotation[second, second] = cosine
                    rotation[first, second] = sine
                    rotation[second, first] = -sine
                    work = rotation.T @ work @ rotation
                    vectors = vectors @ rotation
    diagonal_index = np.arange(size)
    return (work[diagonal_index, diagonal_index], vectors)


def build_tables(points_edge, points_fine):
    degree = points_edge - 1
    points = -np.cos(np.pi * np.arange(points_edge) / degree)
    for sweep in range(100):
        top, below = legendre_pair(points, degree)
        points = points - (points * top - below) / (points_edge * top)
    top, below = legendre_pair(points, degree)
    weight_gll = 2.0 / (degree * points_edge * top**2)
    spacing = points[:, None] - points[None, :] + np.eye(points_edge)
    barycentric = 1.0 / np.prod(spacing, axis=1)
    derivative = barycentric[None, :] / barycentric[:, None] / spacing
    derivative = derivative * (1.0 - np.eye(points_edge))
    derivative = derivative - np.eye(points_edge) * derivative.sum(axis=1)[:, None]
    fine_points = np.cos(np.pi * (np.arange(points_fine) + 0.75) / (points_fine + 0.5))
    for sweep in range(100):
        top, below = legendre_pair(fine_points, points_fine)
        slope = points_fine * (fine_points * top - below) / (fine_points * fine_points - 1.0)
        fine_points = fine_points - top / slope
    top, below = legendre_pair(fine_points, points_fine)
    slope = points_fine * (fine_points * top - below) / (fine_points * fine_points - 1.0)
    fine_weight = 2.0 / ((1.0 - fine_points * fine_points) * slope * slope)
    fine_points = fine_points[::-1]
    fine_weight = fine_weight[::-1]
    interpolate = np.ones((points_fine, points_edge))
    for column in range(points_edge):
        for other in range(points_edge):
            if other != column:
                interpolate[:, column] = (
                    interpolate[:, column]
                    * (fine_points - points[other])
                    / (points[column] - points[other])
                )
    stiffness = derivative.T @ (weight_gll[:, None] * derivative)
    extent = 3 * degree + 1
    joined_stiff = np.zeros((extent, extent))
    joined_mass = np.zeros(extent)
    for segment in range(3):
        offset = segment * degree
        joined_stiff[offset : offset + points_edge, offset : offset + points_edge] += stiffness
        joined_mass[offset : offset + points_edge] += weight_gll
    low = degree - 1
    high = 2 * degree + 2
    root_mass = np.sqrt(joined_mass[low:high])
    scaled = joined_stiff[low:high, low:high] / root_mass[:, None] / root_mass[None, :]
    scaled = 0.5 * (scaled + scaled.T)
    eigen_values, eigen_vectors = jacobi_eigen(scaled)
    solve_mat = eigen_vectors / root_mass[:, None]
    breadth = high - low
    identity = np.eye(points_edge)
    operator_tables = {
        "derivative": derivative,
        "dpair": np.concatenate(
            [np.kron(derivative, identity).T, np.kron(identity, derivative).T], axis=1
        ),
        "interpolate": interpolate,
        "ipair": np.kron(interpolate, interpolate).T,
        "mass_three": (
            weight_gll[:, None, None] * weight_gll[None, :, None] * weight_gll[None, None, :]
        ).reshape(points_edge, points_edge * points_edge),
        "fine_three": (
            fine_weight[:, None, None] * fine_weight[None, :, None] * fine_weight[None, None, :]
        ).reshape(points_fine, points_fine * points_fine),
        "solve_mat": solve_mat,
        "solve_pair": np.kron(solve_mat, solve_mat),
        "eigen_axial": eigen_values,
        "eigen_around": np.repeat(eigen_values, breadth),
        "eigen_radial": np.tile(eigen_values, breadth),
    }
    operator_tables["weight"] = weight_gll
    operator_tables["fine_weight"] = fine_weight
    return operator_tables


def split_rows(matrix):
    exact = np.asarray(matrix, np.float32)
    high = exact.astype(jnp.bfloat16)
    low = (exact - high.astype(np.float32)).astype(jnp.bfloat16)
    columns = range(0, exact.shape[1], LANES)
    return np.concatenate([part[:, c : c + LANES] for c in columns for part in (high, low)])


def halves(matrix):
    rows, columns = matrix.shape
    table = np.zeros((rows // 2, columns // 2, 2, LANES))
    for out in range(rows // 2):
        for into in range(columns // 2):
            table[out, into, 0, :64] = matrix[2 * out, 2 * into]
            table[out, into, 0, 64:] = matrix[2 * out + 1, 2 * into + 1]
            table[out, into, 1, :64] = matrix[2 * out, 2 * into + 1]
            table[out, into, 1, 64:] = matrix[2 * out + 1, 2 * into]
    return np.asarray(table.reshape(-1, LANES), np.float32)


def twice(block, stride):
    rows, columns = block.shape
    result = np.zeros((2 * rows, 2 * stride))
    result[:rows, :columns] = block
    result[rows:, stride : stride + columns] = block
    return result


def pad_columns(matrix, total):
    return np.pad(matrix, ((0, 0), (0, total - matrix.shape[1])))


def by_tile(table):
    return np.asarray(np.repeat(table.reshape(-1, LANES), ES, axis=0), np.float32)


@functools.cache
def constants():
    t = build_tables(NP, NF)
    d, itp, s = t["derivative"], t["interpolate"], t["solve_mat"]
    eye = np.eye(NP)
    pair = np.concatenate(
        [twice(np.kron(d, eye).T, 64), twice(np.kron(eye, d).T, 64)], axis=1
    )
    fine = pad_columns(twice(np.kron(itp, itp).T, 144), 384)
    slope = itp @ d
    fine_slope = np.concatenate(
        [
            pad_columns(twice(np.kron(slope, itp).T, 144), 384),
            pad_columns(twice(np.kron(itp, slope).T, 144), 384),
        ],
        axis=1,
    )
    inner = s[1:9]
    ahead = np.zeros((2 * LANES, 2 * LANES))
    back = np.zeros((2 * LANES, 2 * LANES))
    for h in range(2):
        out = slice(h * LANES, h * LANES + 100)

        def lanes(row):
            return slice(h * 64 + row * 8, h * 64 + row * 8 + 8)

        def beside(row):
            return slice(LANES + h * 64 + row * 8, LANES + h * 64 + row * 8 + 8)

        for row in range(NP):
            ahead[lanes(row), out] = np.kron(s[row + 1 : row + 2], inner)
            back[lanes(row), out] = np.kron(s[row + 1 : row + 2], inner)
        ahead[beside(6), out] = np.kron(s[0:1], inner)
        ahead[beside(1), out] = np.kron(s[9:10], inner)
        back[beside(0), out] = np.kron(s[8:9], inner)
        back[beside(1), out] = np.kron(s[9:10], inner)
        back[beside(7), out] = np.kron(s[1:2], inner)
        back[beside(6), out] = np.kron(s[0:1], inner)
    wf = t["fine_weight"]
    wf2 = (wf[:, None] * wf[None, :]).reshape(-1)
    fine_mass = np.zeros((6, 384))
    for j in range(6):
        fine_mass[j, :144] = wf[2 * j] * wf2
        fine_mass[j, 144:288] = wf[2 * j + 1] * wf2
    eigen = np.zeros((2, LANES))
    eigen[0, :100] = t["eigen_around"]
    eigen[1, :100] = t["eigen_radial"]
    nodes = by_tile(t["mass_three"])
    weights = np.concatenate(
        [split_rows(m) for m in (pair, pair.T, fine, fine_slope, fine.T, ahead, back.T)]
    )
    along = np.concatenate([halves(d), halves(d.T), halves(itp), halves(slope), halves(itp.T), halves(d[[0, -1]].T)])
    fine_mass = np.repeat(fine_mass, ES, axis=0)
    tables = np.concatenate(
        [along, nodes]
        + [fine_mass[:, c : c + LANES] for c in range(0, 384, LANES)]
        + [np.pad(eigen, ((0, 6), (0, 0)))]
    )
    return (
        weights,
        np.asarray(tables, np.float32),
        np.asarray(s, np.float32),
        np.asarray(t["eigen_axial"], np.float32),
    )


PAIR = (0, 128, 256)
PAIR_T = (512, 256, 128)
FINE = (1024, 128, 384)
SLOPE = (1792, 128, 768)
FINE_T = (3328, 384, 128)
AHEAD = (4096, 256, 256)
BACK = (5120, 256, 256)
TABLE_NODES, TABLE_FINE, TABLE_EIGEN = 216, 280, 568
COEF_D, COEF_DT, COEF_I, COEF_S, COEF_IT, COEF_FACE = 0, 32, 64, 112, 160, 208


OPERANDS = 7


def stages_of(count):
    stages = []
    stride = 1
    while stride < count:
        size = min(PEERS, count // stride)
        while (count // stride) % size:
            size -= 1
        stages.append((stride, size))
        stride *= size
    return stages


def kernel(
    count,
    *refs,
):
    operands, refs = refs[:OPERANDS], refs[OPERANDS:]
    pressure_ref, residual_ref = refs[:2]
    held, refs = refs[2 : 2 + OPERANDS], refs[2 + OPERANDS :]
    (
        load_sem,
        early_out,
        early_in,
        early_third,
        mass_in,
        main_out,
        main_in,
        main_second,
        main_third,
        outbox,
        inbox,
        inbox_far,
        gathered,
        turned,
        basis,
        send_sem,
        recv_sem,
        gather_send_sem,
        gather_recv_sem,
    ) = refs
    split = [(0, None)] * 5 + [(0, AHEAD[0]), (AHEAD[0], None), (0, None)]
    loads = []
    for i, (at, end) in enumerate(split):
        which = min(i, 5) if i < 7 else 6
        rows = slice(None) if i < 5 else pl.ds(at, (end or operands[which].shape[0]) - at)
        loads.append(
            pltpu.make_async_copy(
                operands[which].at[rows], held[which].at[rows], load_sem.at[i]
            )
        )
    for i in (3, 7, 4, 2, 0, 5, 1, 6):
        loads[i].start()
    velocity, past, metric, jacobian, slots, weights, tables = held

    _, _, solve, eigen_axial = constants()
    me = lax.axis_index("dom")
    left = lax.rem(me + count - 1, count)
    right = lax.rem(me + 1, count)
    far_left = lax.rem(me + count - 2, count)
    far_right = lax.rem(me + 2, count)
    third_left = lax.rem(me + count - 3, count)
    third_right = lax.rem(me + 3, count)
    stages = stages_of(count)

    def peer(stage, offset):
        stride, size = stages[stage]
        digit = lax.rem(me // stride, size)
        other = lax.rem(digit + offset, size)
        return me + (other - digit) * stride

    barrier = pltpu.get_barrier_semaphore()
    greeted = ([] if len(stages) == 1 else [left, right, far_left, far_right, third_left, third_right]) + [
        peer(stage, offset)
        for stage in range(len(stages))
        for offset in range(1, stages[stage][1])
    ]
    for other in greeted:
        pl.semaphore_signal(barrier, inc=1, device_id=(other,), device_id_type=MESH)

    lane = lax.broadcasted_iota(jnp.int32, (ES, LANES), 1)
    low = lane < 64
    node_s = lax.rem(lane, 64) // 8

    def tiles(field):
        return [field[i * ES : (i + 1) * ES] for i in range(field.shape[0] // ES)]

    def stack(parts):
        return jnp.concatenate(parts, axis=0)

    def mm(x, w):
        high = x.astype(jnp.bfloat16)
        rest = (x - high.astype(jnp.float32)).astype(jnp.bfloat16)
        at, depth, width = w
        columns = []
        for c in range(width // LANES):
            top = weights[at + 2 * c * depth : at + (2 * c + 1) * depth]
            bottom = weights[at + (2 * c + 1) * depth : at + (2 * c + 2) * depth]
            columns.append(jnp.concatenate([top, top, bottom], axis=0))
        return jnp.dot(
            jnp.concatenate([high, rest, high], axis=1),
            jnp.concatenate(columns, axis=1),
            preferred_element_type=jnp.float32,
        )

    def swap(tile):
        return pltpu.roll(tile, 64, 1)

    def along(field, base, total):
        parts = tiles(field)
        swapped = [swap(part) for part in parts]
        results = []
        for out in range(total):
            acc = None
            for into in range(len(parts)):
                at = base + 2 * (out * len(parts) + into)
                term = tables[at : at + 1] * parts[into] + tables[at + 1 : at + 2] * swapped[into]
                acc = term if acc is None else acc + term
            results.append(acc)
        return stack(results)

    def gradient(field):
        paired = mm(field, PAIR)
        return along(field, COEF_D, 4), paired[:, :LANES], paired[:, LANES:]

    def gradient_t(axial, around, radial):
        paired = mm(jnp.concatenate([around, radial], axis=1), PAIR_T)
        return paired + along(axial, COEF_DT, 4)

    def before(tile):
        return pltpu.roll(tile, 1, 0)

    def after(tile):
        return pltpu.roll(tile, ES - 1, 0)

    def around_sum(field):
        results = []
        for tile in tiles(field):
            first = before(pltpu.roll(tile, 72, 1))
            last = after(pltpu.roll(tile, 56, 1))
            results.append(
                tile + jnp.where(node_s == 0, first, jnp.where(node_s == 7, last, 0.0))
            )
        return stack(results)

    def copies(step):
        if step == 0:
            face = early_out.at[pl.ds(0, ES)]
            plan = [
                (face, early_third.at[1], third_left),
                (face, early_third.at[0], third_right),
                (early_out, early_in.at[3], far_left),
                (early_out, early_in.at[0], far_right),
                (early_out, early_in.at[2], left),
                (early_out, early_in.at[1], right),
            ]
        elif step == ROUNDS:
            face = early_out.at[pl.ds(0, ES)]
            plan = [(face, mass_in.at[1], left), (face, mass_in.at[0], right)]
        elif step == 1:
            face = main_out.at[pl.ds(ES, ES)]
            plan = [
                (face, main_third.at[1], third_left),
                (face, main_third.at[0], third_right),
                (main_out.at[pl.ds(0, 4 * ES)], main_second.at[1], far_left),
                (main_out.at[pl.ds(ES, 4 * ES)], main_second.at[0], far_right),
                (main_out, main_in.at[1], left),
                (main_out, main_in.at[0], right),
            ]
        elif step < ROUNDS - 1:
            plan = [
                (outbox.at[step, pl.ds(0, ES)], inbox_far.at[step, 1], far_left),
                (outbox.at[step, pl.ds(3 * ES, ES)], inbox_far.at[step, 0], far_right),
                (outbox.at[step], inbox.at[step, 1], left),
                (outbox.at[step], inbox.at[step, 0], right),
            ]
        else:
            plan = [
                (outbox.at[step, pl.ds(0, ES)], inbox_far.at[step, 1], left),
                (outbox.at[step, pl.ds(3 * ES, ES)], inbox_far.at[step, 0], right),
            ]
        return [
            pltpu.make_async_remote_copy(
                src_ref=source,
                dst_ref=target,
                send_sem=send_sem.at[step, way],
                recv_sem=recv_sem.at[step, way],
                device_id=(other,),
                device_id_type=MESH,
            )
            for way, (source, target, other) in enumerate(plan)
        ]

    def send(step, field):
        outbox[step] = field
        for copy in copies(step):
            copy.start()

    def receive(step):
        for copy in copies(step):
            copy.wait_recv()

    def axial_sum(field, before_it, after_it):
        parts = tiles(field)
        return stack(
            [
                parts[0] + jnp.where(low, swap(before_it), 0.0),
                parts[1],
                parts[2],
                parts[3] + jnp.where(low, 0.0, swap(after_it)),
            ]
        )

    def surrounded(step, field):
        receive(step)
        beside = [inbox[step, 0], inbox[step, 1]]
        ends = [inbox_far[step, 0], inbox_far[step, 1]]
        own = axial_sum(field, beside[0][3 * ES :], beside[1][:ES])
        return own, beside, ends

    def element_field(ref, *index):
        return stack([ref[index + (slice(None), pl.ds(j * LANES, LANES))] for j in range(4)])

    def faces(field):
        return jnp.where(low, field[:ES], field[3 * ES :])

    def across(before_it, after_it):
        return jnp.where(low, swap(before_it), swap(after_it))

    loads[7].wait()
    loads[3].wait()
    weight3 = tables[TABLE_NODES:TABLE_FINE]
    fine_mass = jnp.concatenate(
        [tables[TABLE_FINE + 96 * c : TABLE_FINE + 96 * (c + 1)] for c in range(3)], axis=1
    )
    eigen = tables[TABLE_EIGEN:]
    jac = element_field(jacobian)
    mass = jac * weight3
    loads[2].wait()
    metrics = [element_field(metric, d) for d in range(3)]
    loads[4].wait()
    position = lax.broadcasted_iota(jnp.int32, (ES, ES), 0)
    chosen = jnp.where(slots[...] == position, 1.0, 0.0)
    chosen = jnp.concatenate([chosen, chosen, chosen], axis=1).astype(jnp.bfloat16)

    def into_order(fields):
        wide = jnp.concatenate([tile for field in fields for tile in tiles(field)], axis=1)
        first = wide.astype(jnp.bfloat16)
        rest = wide - first.astype(jnp.float32)
        second = rest.astype(jnp.bfloat16)
        third = (rest - second.astype(jnp.float32)).astype(jnp.bfloat16)
        placed = jnp.dot(
            chosen, stack([first, second, third]), preferred_element_type=jnp.float32
        )
        return [
            stack([placed[:, (4 * f + j) * LANES : (4 * f + j + 1) * LANES] for j in range(4)])
            for f in range(len(fields))
        ]

    placed_mass, *placed_metrics = into_order([mass] + metrics)
    placed_lumps = [placed_mass * m for m in placed_metrics]
    placed_squares = [placed_lumps[d] * placed_metrics[d] for d in range(3)]

    def total(field):
        parts = tiles(field)
        return jnp.sum(parts[0] + parts[1] + parts[2] + parts[3], axis=1, keepdims=True) / 8.0

    flat = (
        total(placed_squares[1]) * eigen[0:1]
        + total(placed_squares[2]) * eigen[1:2]
        + mass_shift * total(placed_mass)
    )
    steep = jnp.broadcast_to(total(placed_squares[0]), (ES, LANES))
    mass_around = around_sum(placed_mass)
    early = [faces(mass_around)] + [faces(lump) for lump in placed_lumps] + [flat, steep]
    early_out[...] = stack(early)
    pl.semaphore_wait(barrier, len(greeted))
    for copy in copies(ROUNDS) + copies(0):
        copy.start()

    coarse = [along(jac, COEF_I, 6)]
    squares = [mass * m * m for m in metrics]
    loads[0].wait()
    newest = [element_field(velocity, 0, i) for i in range(3)]
    coarse += [along(newest[d] * metrics[d], COEF_I, 6) for d in range(3)]
    coarse += [along(newest[i], COEF_S, 6) for i in range(3)]
    loads[5].wait()
    fine = mm(stack(coarse), FINE)
    fine = [fine[i * 96 : (i + 1) * 96] for i in range(7)]
    crossed = mm(stack([along(newest[i], COEF_I, 6) for i in range(3)]), SLOPE)
    fine_jac = fine[0] * fine_mass
    products = []
    for i in range(3):
        rows = slice(i * 96, (i + 1) * 96)
        products.append(
            fine_jac
            * (
                fine[1] * fine[4 + i]
                + fine[2] * crossed[rows, :384]
                + fine[3] * crossed[rows, 384:]
            )
        )
    advected = mm(stack(products), FINE_T)
    guessed = [
        3.0 * newest[i] - 3.0 * element_field(velocity, 1, i) + element_field(velocity, 2, i)
        for i in range(3)
    ]
    paired = mm(stack(guessed), PAIR)
    slopes = jnp.concatenate(
        [
            stack([squares[1] * paired[i * 64 : (i + 1) * 64, :LANES] for i in range(3)]),
            stack([squares[2] * paired[i * 64 : (i + 1) * 64, LANES:] for i in range(3)]),
        ],
        axis=1,
    )
    paired_t = mm(slopes, PAIR_T)
    forcing = []
    loads[1].wait()
    for i in range(3):
        convect = along(advected[i * 96 : (i + 1) * 96], COEF_IT, 4)
        stiff = paired_t[i * 64 : (i + 1) * 64] + along(
            squares[0] * along(guessed[i], COEF_D, 4), COEF_DT, 4
        )
        history = (
            3.0 * newest[i]
            - 1.5 * element_field(velocity, 1, i)
            + element_field(velocity, 2, i) / 3.0
        )
        extrap = (
            3.0 * convect - 3.0 * element_field(past, 0, i) + element_field(past, 1, i)
        )
        helmholtz = viscosity * stiff + 11.0 / (6.0 * time_step) * mass * guessed[i]
        forcing.append(mass * history / time_step - extrap - helmholtz)

    (f0, f1, f2) = into_order(forcing)
    around = [around_sum(f) for f in (f0, f1, f2)]
    for copy in copies(ROUNDS):
        copy.wait_recv()
    total_mass = axial_sum(mass_around, mass_in[0], mass_in[1])
    accel = [placed_lumps[d] * (around[d] / total_mass) for d in range(3)]
    partial = gradient_t(accel[0], accel[1], accel[2])
    parts = tiles(partial)
    own_faces = [faces(f) for f in around]
    main_out[...] = stack([parts[0]] + own_faces + [parts[3], parts[1], parts[2]])
    for copy in copies(1):
        copy.start()
    for copy in copies(0):
        copy.wait_recv()
    shown = [tiles(early_in[i]) for i in range(4)]
    shown = [shown[0], shown[1], early, shown[2], shown[3]]
    mass_faces = [early_third[0]] + [one[0] for one in shown] + [early_third[1]]
    loads[6].wait()
    lump_faces = []
    for b in range(5):
        ratio = mass_faces[b + 1] + across(mass_faces[b], mass_faces[b + 2])
        lump_faces.append([shown[b][1 + d] / ratio for d in range(3)])
    lefts, rights = shown[1], shown[3]
    flats = stack([lefts[4], flat, rights[4]])
    steeps = stack([lefts[5], steep, rights[5]])
    inverse = [1.0 / (steeps * float(eigen_axial[k]) + flats) for k in range(10)]
    for copy in copies(1):
        copy.wait_recv()
    lower, upper = tiles(main_in[0]), tiles(main_in[1])
    beyond = [tiles(main_second[0]), tiles(main_second[1])]
    none = jnp.zeros((ES, LANES), jnp.float32)
    force_faces = [
        [main_third[0], none, none],
        beyond[0][:3],
        lower[1:4],
        own_faces,
        upper[1:4],
        beyond[1][1:],
        [main_third[1], none, none],
    ]
    added = [
        [lump_faces[b][d] * across(force_faces[b][d], force_faces[b + 2][d]) for d in range(3)]
        for b in range(5)
    ]
    sides = tiles(
        mm(
            jnp.concatenate([stack([a[1] for a in added]), stack([a[2] for a in added])], axis=1),
            PAIR_T,
        )
    )
    whole = []
    for b in range(5):
        extra = tiles(along(added[b][0], COEF_FACE, 4))
        extra[0] = extra[0] + jnp.where(low, sides[b], 0.0)
        extra[3] = extra[3] + jnp.where(low, 0.0, sides[b])
        whole.append(extra)
    divergence = partial + stack(whole[2])
    beside = [
        around_sum(stack([near[0], near[5], near[6], near[4]]) + stack(extra))
        for near, extra in ((lower, whole[1]), (upper, whole[3]))
    ]
    ends = [around_sum(beyond[0][3] + whole[0][3]), around_sum(beyond[1][0] + whole[4][0])]
    source = axial_sum(around_sum(divergence), beside[0][3 * ES :], beside[1][:ES])

    def combine(weight, parts):
        acc = parts[0] * float(weight[0])
        for one, part in zip(weight[1:], parts[1:]):
            acc = acc + part * float(one)
        return acc

    def smooth(own, beside, ends):
        lower, upper = tiles(beside[0]), tiles(beside[1])
        lower[0] = lower[0] + jnp.where(low, swap(ends[0]), 0.0)
        upper[3] = upper[3] + jnp.where(low, 0.0, swap(ends[1]))
        parts = [jnp.where(low, ends[0], ends[1])] + lower + upper + tiles(own)
        sides = [
            jnp.where(node_s == 6, before(p), jnp.where(node_s == 1, after(p), 0.0))
            for p in parts
        ]
        modes = tiles(mm(jnp.concatenate([stack(parts), stack(sides)], axis=1), AHEAD))
        firsts = [-7, -5, -3, -1, 7, 9, 11, 13, 0, 2, 4, 6]
        grid = {-8: modes[0][:, :LANES], 15: modes[0][:, LANES:]}
        for row, mode in zip(firsts, modes[1:]):
            grid[row], grid[row + 1] = mode[:, :LANES], mode[:, LANES:]
        order = [stack([grid[a - 7], grid[a], grid[a + 7]]) for a in range(-1, 9)]
        spectra = [combine(solve[:, k], order) * inverse[k] for k in range(10)]
        slabs = [[spectrum[b * ES : (b + 1) * ES] for spectrum in spectra] for b in range(3)]
        rows = [combine(solve[a + 1], slabs[1]) for a in range(NP)]
        rows[0] = rows[0] + combine(solve[8], slabs[0])
        rows[1] = rows[1] + combine(solve[9], slabs[0])
        rows[6] = rows[6] + combine(solve[0], slabs[2])
        rows[7] = rows[7] + combine(solve[1], slabs[2])
        given = mm(jnp.concatenate([stack(rows[0::2]), stack(rows[1::2])], axis=1), BACK)
        return stack(
            [
                o + jnp.where(node_s <= 1, before(n), jnp.where(node_s >= 6, after(n), 0.0))
                for o, n in zip(tiles(given[:, :LANES]), tiles(given[:, LANES:]))
            ]
        )

    def apply(field):
        axial, around, radial = gradient(field)
        local = gradient_t(
            placed_squares[0] * axial, placed_squares[1] * around, placed_squares[2] * radial
        )
        return local + mass_shift * placed_mass * field

    def inner(one, two):
        return jnp.sum(one * two, axis=0, keepdims=True)

    def turn(which, field):
        for j, tile in enumerate(tiles(field)):
            turned[which, pl.ds(2 * j * ES, ES)] = tile
            turned[which, pl.ds((2 * j + 1) * ES, ES)] = swap(tile)
        for p in range(ES):
            block = turned[which, pl.ds(p, NP, stride=ES), :]
            basis[which, :, p * 56 : (p + 1) * 56] = block[:, :56]

    spaces, images, dots = [], [], {}
    current = source
    for it in range(ITERS):
        spaces.append(smooth(current, beside, ends))
        local = apply(spaces[-1])
        image = around_sum(local)
        send(2 + it, image)
        if it == 0:
            head = inner(divergence, spaces[0])
        for j in range(it + 1):
            dots[j, it] = inner(local, spaces[j])
        if it < ITERS - 1:
            turn(2 * it, spaces[it])
            if it == 0:
                turn(6, current)
            else:
                turn(2 * it - 1, current)
            current, beside, ends = surrounded(2 + it, image)
            images.append(current)

    value = jnp.concatenate(
        [head]
        + [dots[i, j] for i in range(3) for j in range(i, 3)]
        + [jnp.zeros((1, LANES), jnp.float32)],
        axis=0,
    )
    sums = jnp.sum(value, axis=1, keepdims=True)
    row8 = lax.broadcasted_iota(jnp.int32, (8, LANES), 0)
    lane8 = lax.broadcasted_iota(jnp.int32, (8, LANES), 1)
    value = jnp.sum(jnp.where(row8 == lane8, sums, 0.0), axis=0, keepdims=True)
    started = []
    for stage, (stride, size) in enumerate(stages):
        digit = lax.rem(me // stride, size)
        slot = gathered.at[stage, pl.ds(digit, 1)]
        slot[...] = value
        for offset in range(1, size):
            copy = pltpu.make_async_remote_copy(
                src_ref=slot,
                dst_ref=slot,
                send_sem=gather_send_sem.at[stage, offset],
                recv_sem=gather_recv_sem.at[stage, offset],
                device_id=(peer(stage, offset),),
                device_id_type=MESH,
            )
            copy.start()
            started.append(copy)
        if stage == 0:
            turn(4, spaces[2])
            turn(3, images[1])
            receive(ROUNDS - 1)
            ends = [inbox_far[ROUNDS - 1, 0], inbox_far[ROUNDS - 1, 1]]
            turn(5, axial_sum(image, ends[0], ends[1]))
        for copy in started[1 - size :]:
            copy.wait_recv()
        value = jnp.sum(gathered[stage, :size], axis=0, keepdims=True)
    sums = [value[:, i : i + 1] for i in range(7)]
    gram = {}
    for at, (i, j) in enumerate([(i, j) for i in range(3) for j in range(i, 3)]):
        gram[i, j] = gram[j, i] = sums[1 + at]
    heads = [sums[0], gram[0, 0], gram[0, 1]]
    taken = [None] * 3
    direction = [None] * 3
    result = [None] * 3
    previous = None
    for it in range(ITERS):
        z = [None] * 3
        z[0] = jnp.ones((1, 1), jnp.float32)
        for k in range(1, it + 1):
            z[k] = taken[k - 1]
        rho = heads[0]
        for k in range(1, it + 1):
            rho = rho + z[k] * heads[k]
        for i in range(it):
            row = gram[i, 0]
            for k in range(1, it + 1):
                row = row + z[k] * gram[i, k]
            rho = rho + taken[i] * row
        if it == 0:
            direction = [z[0], None, None]
        else:
            beta = rho / previous
            direction = [
                None if k > it else z[k] if direction[k] is None else z[k] + beta * direction[k]
                for k in range(3)
            ]
        bottom = None
        for i in range(it + 1):
            row = None
            for k in range(it + 1):
                term = direction[k] * gram[i, k]
                row = term if row is None else row + term
            bottom = direction[i] * row if bottom is None else bottom + direction[i] * row
        alpha = rho / bottom
        for k in range(it + 1):
            step = alpha * direction[k]
            result[k] = step if result[k] is None else result[k] + step
            taken[k] = -step if taken[k] is None else taken[k] - step
        previous = rho
    pressure_ref[...] = sum(basis[2 * k] * result[k] for k in range(3))
    residual_ref[...] = basis[6] + sum(basis[2 * k + 1] * taken[k] for k in range(3))

    for step in range(ROUNDS + 1):
        for copy in copies(step):
            copy.wait_send()
    for copy in started:
        copy.wait_send()


def shards(count, velocity, conv_past, metric, jacobian, element_slot):
    weights, tables, _, _ = constants()
    stages = stages_of(count)
    block = jax.ShapeDtypeStruct((A0, A1 * A2), jnp.float32)
    whole = pl.BlockSpec(memory_space=pltpu.VMEM)
    slots = element_slot.reshape(1, ES)
    operands = [velocity, conv_past, metric, jacobian, slots]
    operands += [jnp.asarray(weights), jnp.asarray(tables)]
    return pl.pallas_call(
        functools.partial(kernel, count),
        out_shape=(block, block),
        in_specs=[pl.BlockSpec(memory_space=pltpu.HBM)] * len(operands),
        out_specs=(whole, whole),
        scratch_shapes=[pltpu.VMEM(x.shape, x.dtype) for x in operands]
        + [
            pltpu.SemaphoreType.DMA((len(operands) + 1,)),
            pltpu.VMEM((6 * ES, LANES), jnp.float32),
            pltpu.VMEM((4, 6 * ES, LANES), jnp.float32),
            pltpu.VMEM((2, ES, LANES), jnp.float32),
            pltpu.VMEM((2, ES, LANES), jnp.float32),
            pltpu.VMEM((7 * ES, LANES), jnp.float32),
            pltpu.VMEM((2, 7 * ES, LANES), jnp.float32),
            pltpu.VMEM((2, 4 * ES, LANES), jnp.float32),
            pltpu.VMEM((2, ES, LANES), jnp.float32),
            pltpu.VMEM((ROUNDS, 4 * ES, LANES), jnp.float32),
            pltpu.VMEM((ROUNDS, 2, 4 * ES, LANES), jnp.float32),
            pltpu.VMEM((ROUNDS, 2, ES, LANES), jnp.float32),
            pltpu.VMEM((len(stages), PEERS, LANES), jnp.float32),
            pltpu.VMEM((7, NP * ES, LANES), jnp.float32),
            pltpu.VMEM((7, A0, A1 * A2), jnp.float32),
            pltpu.SemaphoreType.DMA((ROUNDS + 1, WAYS)),
            pltpu.SemaphoreType.DMA((ROUNDS + 1, WAYS)),
            pltpu.SemaphoreType.DMA((len(stages), PEERS)),
            pltpu.SemaphoreType.DMA((len(stages), PEERS)),
        ],
        compiler_params=pltpu.CompilerParams(
            collective_id=0, has_side_effects=True, vmem_limit_bytes=55168 * 1024
        ),
    )(*operands)


def solution(mesh):
    return jax.shard_map(
        functools.partial(shards, mesh.shape["dom"]),
        mesh=mesh,
        in_specs=(
            P(None, None, "dom", None),
            P(None, None, "dom", None),
            P(None, "dom", None),
            P("dom", None),
            P("dom"),
        ),
        out_specs=(P("dom", None), P("dom", None)),
        check_vma=False,
    )
```
